1024 devices in a mesh: dp: 128 (over y, z), tensor: 8 (over x, core).
Axes of the slice: x: 4, y: 4, z: 32, core: 2. Of those that a mesh axis runs over, the one named last changes fastest.
Arguments:
- hidden_states: bfloat16 [32768, 4096], P('dp'), may hold values from -120 to 120
- key_cotangent: bfloat16 [32768, 1024], P('dp', 'tensor'), may hold values from -0.04 to 0.04
- norm_gain: float32 [4096], replicated, may hold values from 0.1 to 1.9
- key_weight: bfloat16 [4096, 1024], P(None, 'tensor'), may hold values from -0.09375 to 0.09375
Outputs:
- merged_key_grad: bfloat16 [4096, 1024], P('dp', 'tensor')
- merged_gain_grad: bfloat16 [4096], P('dp')
The draws below stay inside these ranges and needn't reach their ends.
All inputs are finite; a program needn't handle non-finite values.
Results may differ from the reference program's by a relative error of at most 0.0065.
Values may be sent and summed in bfloat16 or wider, within the bound.
No kernel may reach another device: no remote copies, remote signals or barrier semaphores. Data moves between devices by JAX's collectives and lax.ppermute only.
A program may use at most 32 MiB of HBM per device.

```python
import math
import jax
import jax.numpy as jnp
from jax import lax

D = 4096
KVW = 1024
TOK_DEV = 256
TOKENS = 32768
N_DP = 128


def draw_hidden_states(key, part):
    key = jax.random.fold_in(key, 11)
    keys = jax.random.split(key, 4)
    noise = jnp.clip(jax.random.normal(keys[0], (TOKENS, D), jnp.float32), -6.0, 6.0)
    offset = jnp.clip(jax.random.normal(keys[3], (1, D), jnp.float32), -3.0, 3.0) * 0.3
    row_scale = jnp.exp(jax.random.uniform(keys[1], (TOKENS, 1), jnp.float32, math.log(0.3), math.log(3.0)))
    col_scale = jnp.exp(jax.random.uniform(keys[2], (1, D), jnp.float32, math.log(0.5), math.log(4.0)))
    return ((noise + offset) * row_scale * col_scale).astype(jnp.bfloat16)


def draw_key_cotangent(key, part):
    key = jax.random.fold_in(key, 23)
    keys = jax.random.split(key, 5)
    replicas = TOKENS // TOK_DEV
    noise = jnp.clip(jax.random.normal(keys[0], (replicas, TOK_DEV, KVW), jnp.float32), -6.0, 6.0)
    share = 2.4 / math.sqrt(TOK_DEV)
    common = jnp.clip(jax.random.normal(keys[1], (1, 1, KVW), jnp.float32), -3.0, 3.0) * share
    own_amp = jnp.exp(jax.random.uniform(keys[2], (replicas, 1, 1), jnp.float32, math.log(0.4), math.log(1.6)))
    own = jnp.clip(jax.random.normal(keys[3], (replicas, 1, KVW), jnp.float32), -3.0, 3.0) * share * own_amp
    scale = jnp.exp(jax.random.uniform(keys[4], (replicas, 1, 1), jnp.float32, math.log(0.5), math.log(2.0)))
    values = jnp.clip(0.004 * scale * (noise + common + own), -0.0398, 0.0398)
    return values.reshape(TOKENS, KVW).astype(jnp.bfloat16)


def block_scale(key, dims, cuts, least, high):
    factor_of = 1.0
    for axis_at, blocks in cuts:
        steps = jax.random.uniform(jax.random.fold_in(jax.random.fold_in(key, 6), axis_at), (blocks,), jnp.float32, least / len(cuts), high / len(cuts))
        factor_of = factor_of * jnp.repeat(jnp.exp(steps), dims[axis_at] // blocks).reshape((-1,) + (1,) * (len(dims) - 1 - axis_at))
    return factor_of


def bell_draw(stream_key, dims, spread, most, shards=(), held_as=jnp.bfloat16):
    loudness = block_scale(stream_key, dims, shards, -0.22, 0.18) if shards else 1.0
    values = jax.random.normal(stream_key, dims, jnp.float32) * spread * loudness
    return jnp.minimum(jnp.maximum(values, -most), most).astype(held_as)


def setup_inputs(seed: int = 0) -> dict:
    arg_keys = jax.random.split(jax.random.key(seed), 5)
    hidden_states = draw_hidden_states(jax.random.fold_in(arg_keys[4], 71), 0)
    key_cotangent = draw_key_cotangent(jax.random.fold_in(arg_keys[4], 71), 0)
    norm_gain = jnp.clip(1.0 + 0.18 * jax.random.normal(arg_keys[2], (D,), jnp.float32), 0.1, 1.9)
    key_weight = bell_draw(arg_keys[3], (D, KVW), D ** -0.5, 0.09375, ((1, 8),))
    return {"hidden_states": hidden_states, "key_cotangent": key_cotangent, "norm_gain": norm_gain, "key_weight": key_weight}


eps_norm = 1e-05
eps_merge = 1e-06

def local_grads(rows_now, cotangent, norm_gain, key_weight):
    wide_rows = rows_now.astype(jnp.float32)
    inv_rms = lax.rsqrt(lax.optimization_barrier(jnp.mean(wide_rows * wide_rows, axis=1, keepdims=True)) + eps_norm)
    normed = wide_rows * inv_rms
    inputs = (normed * norm_gain).astype(jnp.bfloat16)
    key_grad = lax.dot_general(inputs, cotangent, (((0,), (0,)), ((), ())), preferred_element_type=jnp.float32).astype(jnp.bfloat16)
    input_grad = lax.dot_general(cotangent, key_weight, (((1,), (1,)), ((), ())), preferred_element_type=jnp.float32)
    gain_grad = lax.optimization_barrier(jnp.sum(input_grad * normed, axis=0)).astype(jnp.bfloat16)
    return (key_grad, gain_grad)

def merge_pair(low_key, high_key, low_gain, high_gain):
    low_wide = low_key.astype(jnp.float32)
    high_wide = high_key.astype(jnp.float32)
    low_gw = low_gain.astype(jnp.float32)
    high_gw = high_gain.astype(jnp.float32)
    cross_key = jnp.sum(low_wide * high_wide)
    low_sq = jnp.sum(low_wide * low_wide)
    high_sq = jnp.sum(high_wide * high_wide)
    cross_gain = jnp.sum(low_gw * high_gw)
    low_gsq = jnp.sum(low_gw * low_gw)
    high_gsq = jnp.sum(high_gw * high_gw)
    new_key = (1.0 - cross_key / (2.0 * (low_sq + eps_merge))) * low_wide + (1.0 - cross_key / (2.0 * (high_sq + eps_merge))) * high_wide
    new_gain = (1.0 - cross_gain / (2.0 * (low_gsq + eps_merge))) * low_gw + (1.0 - cross_gain / (2.0 * (high_gsq + eps_merge))) * high_gw
    return (new_key.astype(jnp.bfloat16), new_gain.astype(jnp.bfloat16))

def reference(hidden_states, key_cotangent, norm_gain, key_weight):
    section_count = N_DP.bit_length() - 1
    depth = max(section_count, 1)
    stack_key = jnp.zeros((depth, D, KVW), jnp.bfloat16)
    stack_gain = jnp.zeros((depth, D), jnp.bfloat16)
    start_key = jnp.zeros((D, KVW), jnp.bfloat16)
    start_gain = jnp.zeros((D,), jnp.bfloat16)

    def absorb(state_now, replica):
        stack_k, stack_g, value_k, value_g = state_now
        rows_now = lax.dynamic_slice_in_dim(hidden_states, replica * TOK_DEV, TOK_DEV, 0)
        cotangent = lax.dynamic_slice_in_dim(key_cotangent, replica * TOK_DEV, TOK_DEV, 0)
        value_k, value_g = local_grads(rows_now, cotangent, norm_gain, key_weight)
        active = jnp.array(True)
        for section_bit in range(section_count):
            bit_set = replica >> section_bit & 1 == 1
            merged_k, merged_g = merge_pair(stack_k[section_bit], value_k, stack_g[section_bit], value_g)
            store_now = jnp.logical_and(active, jnp.logical_not(bit_set))
            take_now = jnp.logical_and(active, bit_set)
            stack_k = stack_k.at[section_bit].set(jnp.where(store_now, value_k, stack_k[section_bit]))
            stack_g = stack_g.at[section_bit].set(jnp.where(store_now, value_g, stack_g[section_bit]))
            value_k = jnp.where(take_now, merged_k, value_k)
            value_g = jnp.where(take_now, merged_g, value_g)
            active = take_now
        return ((stack_k, stack_g, value_k, value_g), None)
    final_state, unused = lax.scan(absorb, (stack_key, stack_gain, start_key, start_gain), jnp.arange(N_DP, dtype=jnp.int32))
    return (final_state[2], final_state[3])
```

```python
import jax
import jax.numpy as jnp
from jax import lax
from jax.experimental import pallas as pl
from jax.experimental.pallas import tpu as pltpu
from jax.sharding import Mesh
from jax.sharding import PartitionSpec as P

eps_norm = 1e-05
eps_merge = 1e-06

f32 = jnp.float32
bf16 = jnp.bfloat16

NEAR = 4
FAR = 32
FAR_Z = 8
WIDTH = 8
PIECE = 32
LANES = 128
VMEM_SPEC = pl.BlockSpec(memory_space=pltpu.VMEM)
SMEM_SPEC = pl.BlockSpec(memory_space=pltpu.SMEM)


def factor(cross, own_sq):
    return 1.0 - cross / (2.0 * (jnp.maximum(own_sq, 0.0) + eps_merge))


def grads_kernel(place, hidden, cot, gain, weight, p0, p1, p2, p3, gain_out, inv_wide, pieces):
    tokens, width = hidden.shape
    blocks = width // LANES
    half = tokens // 2
    for part in range(2):
        rows = pl.ds(part * half, half)
        total = jnp.zeros((half, LANES), f32)
        for block in range(blocks):
            x = hidden[rows, pl.ds(block * LANES, LANES)].astype(f32)
            total = total + x * x
        mean = jnp.sum(total, axis=1, keepdims=True) * (1.0 / width)
        inv_wide[rows, :] = jnp.broadcast_to(lax.rsqrt(mean + eps_norm), (half, LANES))
    step = 4 * LANES
    for chunk in range(width // step):
        inv = inv_wide[...]
        normed = []
        inputs = []
        for sub in range(4):
            block = 4 * chunk + sub
            x = hidden[:, pl.ds(block * LANES, LANES)].astype(f32) * inv
            normed.append(x)
            inputs.append((x * gain[pl.ds(block, 1), :]).astype(bf16))
        grad = lax.dot_general(
            jnp.concatenate(inputs, axis=1),
            cot[...],
            (((0,), (0,)), ((), ())),
            preferred_element_type=f32,
        ).astype(bf16)
        back = lax.dot_general(
            cot[...],
            weight[pl.ds(chunk * step, step), :],
            (((1,), (1,)), ((), ())),
            preferred_element_type=f32,
        )
        for sub in range(4):
            block = 4 * chunk + sub
            for near in range(NEAR):
                at = sub * LANES + near * PIECE
                pieces[near, pl.ds(block * PIECE, PIECE), :] = grad[at : at + PIECE]
            row = jnp.sum(
                back[:, sub * LANES : (sub + 1) * LANES] * normed[sub], axis=0, keepdims=True
            )
            for other in range(WIDTH):
                gain_out[other, pl.ds(block, 1), :] = row
    here = place[0]
    for apart, out in enumerate((p0, p1, p2, p3)):
        out[...] = pieces[here ^ apart]


def local_grads(place, hidden, cot, gain, weight):
    piece = jax.ShapeDtypeStruct((FAR * PIECE, LANES), bf16)
    return pl.pallas_call(
        grads_kernel,
        out_shape=[piece] * NEAR + [jax.ShapeDtypeStruct((WIDTH, FAR, LANES), f32)],
        in_specs=[SMEM_SPEC] + [VMEM_SPEC] * 4,
        out_specs=[VMEM_SPEC] * (NEAR + 1),
        scratch_shapes=[
            pltpu.VMEM((hidden.shape[0], LANES), f32),
            pltpu.VMEM((NEAR, FAR * PIECE, LANES), bf16),
        ],
        compiler_params=pltpu.CompilerParams(vmem_limit_bytes=32 << 20),
        name="local_grads",
    )(place, hidden, cot, gain, weight)


def all_sum(x):
    return jnp.sum(jnp.sum(x, axis=0, keepdims=True), axis=1, keepdims=True)


def near_dots_kernel(place, p0, p1, p2, p3, out):
    refs = (p0, p1, p2, p3)
    pairs = [(a, b) for a in range(NEAR) for b in range(a, NEAR)]
    rows = 64

    def add(step, totals):
        values = [ref[pl.ds(step * rows, rows), :].astype(f32) for ref in refs]
        return tuple(
            total + jnp.sum((values[a] * values[b]).reshape(rows // 8, 8, LANES), axis=0)
            for total, (a, b) in zip(totals, pairs)
        )

    totals = lax.fori_loop(
        0, p0.shape[0] // rows, add, tuple(jnp.zeros((8, LANES), f32) for _ in pairs)
    )
    here = place[0]
    lane = lax.broadcasted_iota(jnp.int32, (1, LANES), 1)
    row = jnp.zeros((1, LANES), f32)
    for total, (a, b) in zip(totals, pairs):
        dot = all_sum(total)
        row = jnp.where(lane == ((NEAR * a + b) ^ (5 * here)), dot, row)
        row = jnp.where(lane == ((NEAR * b + a) ^ (5 * here)), dot, row)
    out[...] = jnp.broadcast_to(row.reshape(1, 1, LANES), out.shape)


def near_dots(place, pieces):
    return pl.pallas_call(
        near_dots_kernel,
        out_shape=jax.ShapeDtypeStruct((NEAR * WIDTH, 1, LANES), f32),
        in_specs=[SMEM_SPEC] + [VMEM_SPEC] * NEAR,
        out_specs=VMEM_SPEC,
        name="near_dots",
    )(place, *pieces)


def near_shares(dots):
    low = (factor(dots[0][1], dots[0][0]), factor(dots[0][1], dots[1][1]))
    high = (factor(dots[2][3], dots[2][2]), factor(dots[2][3], dots[3][3]))
    low_sq = (
        low[0] * low[0] * dots[0][0]
        + 2.0 * (low[0] * low[1] * dots[0][1])
        + low[1] * low[1] * dots[1][1]
    )
    high_sq = (
        high[0] * high[0] * dots[2][2]
        + 2.0 * (high[0] * high[1] * dots[2][3])
        + high[1] * high[1] * dots[3][3]
    )
    cross = low[0] * (high[0] * dots[0][2] + high[1] * dots[0][3]) + low[1] * (
        high[0] * dots[1][2] + high[1] * dots[1][3]
    )
    of_low = factor(cross, low_sq)
    of_high = factor(cross, high_sq)
    return (of_low * low[0], of_low * low[1], of_high * high[0], of_high * high[1])


def near_merge_kernel(place, dots, gains, p0, p1, p2, p3, out):
    here = place[0]
    row = jnp.sum(dots[...], axis=0)
    lane = lax.broadcasted_iota(jnp.int32, (1, LANES), 1)

    def entry(a, b):
        return jnp.sum(jnp.where(lane == NEAR * a + b, row, 0.0), axis=1, keepdims=True)

    shares = near_shares([[entry(a, b) if a <= b else None for b in range(NEAR)] for a in range(NEAR)])
    by_apart = []
    for apart in range(NEAR):
        share = shares[apart]
        for other in range(1, NEAR):
            share = jnp.where(here == other, shares[other ^ apart], share)
        by_apart.append(share)
    for far in range(FAR):
        rows = pl.ds(far * PIECE, PIECE)
        total = by_apart[0] * p0[rows, :].astype(f32)
        for share, ref in zip(by_apart[1:], (p1, p2, p3)):
            total = total + share * ref[rows, :].astype(f32)
        out[far, pl.ds(0, PIECE), :] = total.astype(bf16)

    gain = [gains[near] for near in range(NEAR)]
    gain_shares = near_shares(
        [[all_sum(gain[a] * gain[b]) if a <= b else None for b in range(NEAR)] for a in range(NEAR)]
    )
    merged = gain_shares[0] * gain[0]
    for near in range(1, NEAR):
        merged = merged + gain_shares[near] * gain[near]
    for far in range(FAR):
        out[far, pl.ds(PIECE, 8), :] = jnp.broadcast_to(merged[far : far + 1], (8, LANES)).astype(bf16)


def near_merge(place, dots, gains, pieces):
    return pl.pallas_call(
        near_merge_kernel,
        out_shape=jax.ShapeDtypeStruct((FAR, PIECE + 8, LANES), bf16),
        in_specs=[SMEM_SPEC] + [VMEM_SPEC] * (2 + NEAR),
        out_specs=VMEM_SPEC,
        name="near_merge",
    )(place, dots, gains, *pieces)


def packed(dots):
    total = dots[0:8]
    for block in range(1, 4):
        total = total + pltpu.roll(dots[8 * block : 8 * block + 8], 32 * block, 1)
    return total


def unpacked(rows):
    lane = lax.broadcasted_iota(jnp.int32, (8, LANES), 1)
    blocks = []
    for block in range(4):
        moved = rows if block == 0 else pltpu.roll(rows, LANES - 32 * block, 1)
        blocks.append(jnp.where(lane < FAR, moved, 0.0))
    return jnp.concatenate(blocks, axis=0)


def far_dots_kernel(values, key_out, gain_out, by_row, wide):
    for far in range(FAR):
        wide[pl.ds(far * (PIECE + 8), PIECE + 8), :] = values[far].astype(f32)
    columns = []
    for row in range(PIECE + 1):
        block = wide[pl.ds(row, FAR, stride=PIECE + 8), :]
        by_row[pl.ds(row * FAR, FAR), :] = block
        columns.append(block.astype(bf16))

    def dots(matrix):
        padded = jnp.concatenate(
            [matrix, jnp.zeros((LANES - FAR, matrix.shape[1]), bf16)], axis=0
        )
        return lax.dot_general(
            matrix, padded, (((1,), (1,)), ((), ())), preferred_element_type=f32
        )

    key_rows = packed(dots(jnp.concatenate(columns[:PIECE], axis=1)))
    key_out[...] = jnp.broadcast_to(key_rows[None], key_out.shape)
    gain_out[...] = packed(dots(columns[PIECE]))


def far_dots(values):
    return pl.pallas_call(
        far_dots_kernel,
        out_shape=[
            jax.ShapeDtypeStruct((NEAR * WIDTH, 8, LANES), f32),
            jax.ShapeDtypeStruct((8, LANES), f32),
            jax.ShapeDtypeStruct(((PIECE + 1) * FAR, LANES), f32),
        ],
        in_specs=[VMEM_SPEC],
        out_specs=[VMEM_SPEC] * 3,
        scratch_shapes=[pltpu.VMEM((FAR * (PIECE + 8), LANES), f32)],
        name="far_dots",
    )(values)


def far_shares(dots):
    shape = dots.shape
    row = lax.broadcasted_iota(jnp.int32, shape, 0)
    lane = lax.broadcasted_iota(jnp.int32, shape, 1)
    share = jnp.ones((shape[0], 1), f32)
    for level in range(5):
        same = (row >> level) == (lane >> level)
        across = ((row >> level) ^ 1) == (lane >> level)
        own_part = jnp.sum(jnp.where(same, dots, 0.0), axis=0, keepdims=True)
        cross_part = jnp.sum(jnp.where(across, dots, 0.0), axis=0, keepdims=True)
        own_sq = jnp.sum(jnp.where(same, own_part, 0.0), axis=1, keepdims=True)
        cross = jnp.sum(jnp.where(same, cross_part, 0.0), axis=1, keepdims=True)
        scale = factor(cross, own_sq)
        share = share * scale
        if level < 4:
            scale_row = jnp.sum(jnp.where(row == lane, scale, 0.0), axis=0, keepdims=True)
            dots = dots * scale * scale_row
    return share


def far_merge_kernel(place, dots, by_row, key_out, gain_out):
    key_share = far_shares(unpacked(dots[pl.ds(0, 8), :]))
    gain_share = far_shares(unpacked(dots[pl.ds(8, 8), :]))
    key_wide = jnp.broadcast_to(key_share, (FAR, LANES))
    rows = []
    for row in range(PIECE):
        rows.append(
            jnp.sum(key_wide * by_row[pl.ds(row * FAR, FAR), :], axis=0, keepdims=True)
        )
    key_out[...] = jnp.concatenate(rows, axis=0).astype(bf16)
    gain = jnp.sum(gain_share * by_row[pl.ds(PIECE * FAR, FAR), :], axis=0, keepdims=True)
    wide = jnp.broadcast_to(gain, (8, LANES))
    moved = wide
    for near in range(1, NEAR):
        moved = jnp.where(place[0] == near, pltpu.roll(wide, LANES - PIECE * near, 1), moved)
    gain_out[...] = moved[0:1].astype(bf16)


def far_merge(place, dots, by_row):
    return pl.pallas_call(
        far_merge_kernel,
        out_shape=[
            jax.ShapeDtypeStruct((PIECE, LANES), bf16),
            jax.ShapeDtypeStruct((1, LANES), bf16),
        ],
        in_specs=[SMEM_SPEC] + [VMEM_SPEC] * 2,
        out_specs=[VMEM_SPEC] * 2,
        name="far_merge",
    )(place, dots, by_row)


def paired(x, axis, apart):
    return lax.ppermute(x, axis, [(i, i ^ apart) for i in range(lax.axis_size(axis))])


def exchanged(x, axes):
    return lax.all_to_all(x, axes, 0, 0)


def body(hidden_states, key_cotangent, norm_gain, key_weight):
    place = lax.axis_index("zl").astype(jnp.int32).reshape(1)
    *pieces, gain_parts = local_grads(
        place, hidden_states, key_cotangent, norm_gain.reshape(FAR, LANES), key_weight
    )
    with jax.named_scope("near_exchange"):
        arrived = {apart: paired(pieces[apart], "zl", apart) for apart in (2, 3, 1)}
    with jax.named_scope("gain_sum"):
        gain = jnp.sum(exchanged(gain_parts, ("x", "core")), axis=0)
        gain = lax.reduce_precision(gain, 8, 7)
        gains = exchanged(jnp.broadcast_to(gain[None], (NEAR, FAR, LANES)), "zl")
    pieces = [pieces[0]] + [arrived[apart] for apart in range(1, NEAR)]
    with jax.named_scope("near_dots_sum"):
        dots = exchanged(near_dots(place, pieces), ("zl", "x", "core"))
    values = near_merge(place, dots, gains, pieces)
    with jax.named_scope("far_exchange"):
        values = exchanged(values, ("y", "zh"))
    key_dots, gain_dots, by_row = far_dots(values)
    with jax.named_scope("far_dots_sum"):
        key_dots = jnp.sum(exchanged(key_dots, ("zl", "x", "core")), axis=0)
        dots = jnp.concatenate([key_dots, gain_dots], axis=0)
        dots = jnp.sum(exchanged(jnp.broadcast_to(dots[None], (4, 16, LANES)), "y"), axis=0)
        for apart in (1, 2, 4):
            dots = dots + paired(dots, "zh", apart)
    merged_key, merged_gain = far_merge(place, dots, by_row)
    return (merged_key, merged_gain[0, :PIECE])


def solution(mesh):
    split = Mesh(mesh.devices.reshape(4, FAR_Z, NEAR, 4, 2), ("y", "zh", "zl", "x", "core"))
    rows = ("y", "zh", "zl")
    columns = ("x", "core")
    return jax.shard_map(
        body,
        mesh=split,
        in_specs=(P(rows, None), P(rows, columns), P(), P(None, columns)),
        out_specs=(P(rows, columns), P(rows)),
        check_vma=False,
    )
```

```python
import jax
import jax.numpy as jnp
from jax import lax
from jax.experimental import pallas as pl
from jax.experimental.pallas import tpu as pltpu
from jax.sharding import Mesh
from jax.sharding import PartitionSpec as P

eps_norm = 1e-05
eps_merge = 1e-06

f32 = jnp.float32
bf16 = jnp.bfloat16

NEAR = 4
FAR = 32
FAR_Z = 8
WIDTH = 8
GAIN_AT = 16
PIECE = 32
LANES = 128
VMEM_SPEC = pl.BlockSpec(memory_space=pltpu.VMEM)
SMEM_SPEC = pl.BlockSpec(memory_space=pltpu.SMEM)
PARAMS = pltpu.CompilerParams(vmem_limit_bytes=16 << 20)


def factor(cross, own_sq):
    return 1.0 - cross / (2.0 * (jnp.maximum(own_sq, 0.0) + eps_merge))


def grads_kernel(
    place, hidden_hbm, cot_hbm, gain_hbm, weight_hbm, p0, p1, p2, p3, gain_out,
    hidden, cot, gain, weight, inv_wide, pieces, gain_rows, sems,
):
    tokens, width = hidden.shape
    parts = 8
    height = tokens // parts
    copies = [
        pltpu.make_async_copy(
            hidden_hbm.at[pl.ds(part * height, height)],
            hidden.at[pl.ds(part * height, height)],
            sems.at[part],
        )
        for part in range(parts)
    ]
    for at, (there, here) in enumerate(((cot_hbm, cot), (gain_hbm, gain), (weight_hbm, weight))):
        copies.append(pltpu.make_async_copy(there, here, sems.at[parts + at]))
    for copy in copies:
        copy.start()
    blocks = width // LANES
    for part in range(parts):
        rows = pl.ds(part * height, height)
        copies[part].wait()
        totals = [jnp.zeros((height, LANES), f32) for _ in range(2)]
        for block in range(blocks):
            x = hidden[rows, pl.ds(block * LANES, LANES)].astype(f32)
            totals[block % 2] = totals[block % 2] + x * x
        mean = jnp.sum(totals[0] + totals[1], axis=1, keepdims=True) * (1.0 / width)
        inv_wide[rows, :] = jnp.broadcast_to(lax.rsqrt(mean + eps_norm), (height, LANES))
    for copy in copies[parts:]:
        copy.wait()
    step = 4 * LANES
    for chunk in range(width // step):
        inv = inv_wide[...]
        normed = []
        inputs = []
        for sub in range(4):
            block = 4 * chunk + sub
            x = hidden[:, pl.ds(block * LANES, LANES)].astype(f32) * inv
            normed.append(x)
            inputs.append((x * gain[pl.ds(block, 1), :]).astype(bf16))
        grad = lax.dot_general(
            jnp.concatenate(inputs, axis=1),
            cot[...],
            (((0,), (0,)), ((), ())),
            preferred_element_type=f32,
        ).astype(bf16)
        back = lax.dot_general(
            cot[...],
            weight[pl.ds(chunk * step, step), :],
            (((1,), (1,)), ((), ())),
            preferred_element_type=f32,
        )
        for sub in range(4):
            block = 4 * chunk + sub
            for near in range(NEAR):
                at = sub * LANES + near * PIECE
                pieces[near, pl.ds(block * PIECE, PIECE), :] = grad[at : at + PIECE]
            gain_rows[pl.ds(block, 1), :] = jnp.sum(
                back[:, sub * LANES : (sub + 1) * LANES] * normed[sub], axis=0, keepdims=True
            )
    here = place[0]
    for apart, out in enumerate((p0, p1, p2, p3)):
        out[...] = pieces[here ^ apart]
    lane = lax.broadcasted_iota(jnp.int32, (8, LANES), 1)
    for near in range(NEAR):
        total = jnp.zeros((8, LANES), f32)
        for block in range(4):
            part = jnp.where(lane // PIECE == near, gain_rows[pl.ds(8 * block, 8), :], 0.0)
            turn = PIECE * (block - near) % LANES
            total = total + (pltpu.roll(part, turn, 1) if turn else part)
        for other in range(WIDTH):
            gain_out[near * WIDTH + other] = total


def local_grads(place, hidden, cot, gain, weight):
    piece = jax.ShapeDtypeStruct((FAR * PIECE, LANES), bf16)
    return pl.pallas_call(
        grads_kernel,
        out_shape=[piece] * NEAR + [jax.ShapeDtypeStruct((NEAR * WIDTH, 8, LANES), f32)],
        in_specs=[SMEM_SPEC] + [pl.BlockSpec(memory_space=pltpu.HBM)] * 4,
        out_specs=[VMEM_SPEC] * (NEAR + 1),
        scratch_shapes=[
            pltpu.VMEM(hidden.shape, bf16),
            pltpu.VMEM(cot.shape, bf16),
            pltpu.VMEM(gain.shape, f32),
            pltpu.VMEM(weight.shape, bf16),
            pltpu.VMEM((hidden.shape[0], LANES), f32),
            pltpu.VMEM((NEAR, FAR * PIECE, LANES), bf16),
            pltpu.VMEM((FAR, LANES), f32),
            pltpu.SemaphoreType.DMA((11,)),
        ],
        compiler_params=PARAMS,
        name="local_grads",
    )(place, hidden, cot, gain, weight)


def all_sum(x):
    return jnp.sum(jnp.sum(x, axis=0, keepdims=True), axis=1, keepdims=True)


def near_dots_kernel(place, gain_parts, p0, p1, p2, p3, out, gain_out):
    refs = (p0, p1, p2, p3)
    pairs = [(a, b) for a in range(NEAR) for b in range(a, NEAR)]
    rows = 64

    def add(step, totals):
        values = [ref[pl.ds(step * rows, rows), :].astype(f32) for ref in refs]
        return tuple(
            total + jnp.sum((values[a] * values[b]).reshape(rows // 8, 8, LANES), axis=0)
            for total, (a, b) in zip(totals, pairs)
        )

    totals = lax.fori_loop(
        0, p0.shape[0] // rows, add, tuple(jnp.zeros((8, LANES), f32) for _ in pairs)
    )
    here = place[0]
    lane = lax.broadcasted_iota(jnp.int32, (1, LANES), 1)
    row = jnp.zeros((1, LANES), f32)
    for total, (a, b) in zip(totals, pairs):
        dot = all_sum(total)
        row = jnp.where(lane == ((NEAR * a + b) ^ (5 * here)), dot, row)
        row = jnp.where(lane == ((NEAR * b + a) ^ (5 * here)), dot, row)
    gain = []
    for near in range(NEAR):
        total = gain_parts[near * WIDTH]
        for other in range(1, WIDTH):
            total = total + gain_parts[near * WIDTH + other]
        gain.append(total.astype(bf16).astype(f32))
        gain_out[pl.ds(8 * near, 8), :] = gain[near]
    for a, b in pairs:
        row = jnp.where(lane == GAIN_AT + NEAR * a + b, all_sum(gain[a] * gain[b]), row)
    out[...] = jnp.broadcast_to(row.reshape(1, 1, LANES), out.shape)


def near_dots(place, gain_parts, pieces):
    return pl.pallas_call(
        near_dots_kernel,
        out_shape=[
            jax.ShapeDtypeStruct((NEAR * WIDTH, 1, LANES), f32),
            jax.ShapeDtypeStruct((NEAR * 8, LANES), f32),
        ],
        in_specs=[SMEM_SPEC] + [VMEM_SPEC] * (1 + NEAR),
        out_specs=[VMEM_SPEC] * 2,
        compiler_params=PARAMS,
        name="near_dots",
    )(place, gain_parts, *pieces)


def near_shares(dots):
    low = (factor(dots[0][1], dots[0][0]), factor(dots[0][1], dots[1][1]))
    high = (factor(dots[2][3], dots[2][2]), factor(dots[2][3], dots[3][3]))
    low_sq = (
        low[0] * low[0] * dots[0][0]
        + 2.0 * (low[0] * low[1] * dots[0][1])
        + low[1] * low[1] * dots[1][1]
    )
    high_sq = (
        high[0] * high[0] * dots[2][2]
        + 2.0 * (high[0] * high[1] * dots[2][3])
        + high[1] * high[1] * dots[3][3]
    )
    cross = low[0] * (high[0] * dots[0][2] + high[1] * dots[0][3]) + low[1] * (
        high[0] * dots[1][2] + high[1] * dots[1][3]
    )
    of_low = factor(cross, low_sq)
    of_high = factor(cross, high_sq)
    return (of_low * low[0], of_low * low[1], of_high * high[0], of_high * high[1])


def packed(dots):
    total = dots[0:8]
    for block in range(1, 4):
        total = total + pltpu.roll(dots[8 * block : 8 * block + 8], 32 * block, 1)
    return total


def unpacked(rows):
    lane = lax.broadcasted_iota(jnp.int32, (8, LANES), 1)
    blocks = []
    for block in range(4):
        moved = rows if block == 0 else pltpu.roll(rows, LANES - 32 * block, 1)
        blocks.append(jnp.where(lane < FAR, moved, 0.0))
    return jnp.concatenate(blocks, axis=0)


def near_merge_kernel(place, dots, gains, p0, p1, p2, p3, out):
    here = place[0]
    row = jnp.sum(dots[...], axis=0)
    lane = lax.broadcasted_iota(jnp.int32, (1, LANES), 1)
    row = jnp.where(lane < GAIN_AT, row, row * (1.0 / WIDTH))

    def shares_at(first):
        def entry(a, b):
            at = first + NEAR * a + b
            return jnp.sum(jnp.where(lane == at, row, 0.0), axis=1, keepdims=True)

        return near_shares(
            [[entry(a, b) if a <= b else None for b in range(NEAR)] for a in range(NEAR)]
        )

    shares = shares_at(0)
    by_apart = []
    for apart in range(NEAR):
        share = shares[apart]
        for other in range(1, NEAR):
            share = jnp.where(here == other, shares[other ^ apart], share)
        by_apart.append(share)
    for far in range(FAR):
        rows = pl.ds(far * PIECE, PIECE)
        total = by_apart[0] * p0[rows, :].astype(f32)
        for share, ref in zip(by_apart[1:], (p1, p2, p3)):
            total = total + share * ref[rows, :].astype(f32)
        out[far, pl.ds(0, PIECE), :] = total.astype(bf16)

    gain_shares = shares_at(GAIN_AT)
    merged = gain_shares[0] * gains[pl.ds(0, 8), :]
    for near in range(1, NEAR):
        merged = merged + gain_shares[near] * gains[pl.ds(8 * near, 8), :]
    merged = unpacked(merged)
    for far in range(FAR):
        out[far, pl.ds(PIECE, 8), :] = jnp.broadcast_to(merged[far : far + 1], (8, LANES)).astype(bf16)


def near_merge(place, dots, gains, pieces):
    return pl.pallas_call(
        near_merge_kernel,
        out_shape=jax.ShapeDtypeStruct((FAR, PIECE + 8, LANES), bf16),
        in_specs=[SMEM_SPEC] + [VMEM_SPEC] * (2 + NEAR),
        out_specs=VMEM_SPEC,
        compiler_params=PARAMS,
        name="near_merge",
    )(place, dots, gains, *pieces)


def far_dots_kernel(values, out, by_row, wide):
    for far in range(FAR):
        wide[pl.ds(far * (PIECE + 8), PIECE + 8), :] = values[far].astype(f32)
    columns = []
    for row in range(PIECE + 1):
        block = wide[pl.ds(row, FAR, stride=PIECE + 8), :]
        by_row[pl.ds(row * FAR, FAR), :] = block
        columns.append(block.astype(bf16))

    def dots(matrix):
        padded = jnp.concatenate(
            [matrix, jnp.zeros((LANES - FAR, matrix.shape[1]), bf16)], axis=0
        )
        return lax.dot_general(
            matrix, padded, (((1,), (1,)), ((), ())), preferred_element_type=f32
        )

    key_rows = packed(dots(jnp.concatenate(columns[:PIECE], axis=1)))
    gain_rows = packed(dots(columns[PIECE])) * (1.0 / WIDTH)
    out[...] = jnp.broadcast_to(jnp.concatenate([key_rows, gain_rows], axis=0)[None], out.shape)


def far_dots(values):
    return pl.pallas_call(
        far_dots_kernel,
        out_shape=[
            jax.ShapeDtypeStruct((4 * WIDTH, 16, LANES), f32),
            jax.ShapeDtypeStruct(((PIECE + 1) * FAR, LANES), f32),
        ],
        in_specs=[VMEM_SPEC],
        out_specs=[VMEM_SPEC] * 2,
        scratch_shapes=[pltpu.VMEM((FAR * (PIECE + 8), LANES), f32)],
        compiler_params=PARAMS,
        name="far_dots",
    )(values)


def far_shares(dots):
    shape = dots.shape
    row = lax.broadcasted_iota(jnp.int32, shape, 0)
    lane = lax.broadcasted_iota(jnp.int32, shape, 1)
    share = jnp.ones((shape[0], 1), f32)
    for level in range(5):
        same = (row >> level) == (lane >> level)
        across = ((row >> level) ^ 1) == (lane >> level)
        own_part = jnp.sum(jnp.where(same, dots, 0.0), axis=0, keepdims=True)
        cross_part = jnp.sum(jnp.where(across, dots, 0.0), axis=0, keepdims=True)
        own_sq = jnp.sum(jnp.where(same, own_part, 0.0), axis=1, keepdims=True)
        cross = jnp.sum(jnp.where(same, cross_part, 0.0), axis=1, keepdims=True)
        scale = factor(cross, own_sq)
        share = share * scale
        if level < 4:
            scale_row = jnp.sum(jnp.where(row == lane, scale, 0.0), axis=0, keepdims=True)
            dots = dots * scale * scale_row
    return share


def far_merge_kernel(dots, by_row, key_out, gain_out):
    key_share = far_shares(unpacked(dots[pl.ds(0, 8), :]))
    gain_share = far_shares(unpacked(dots[pl.ds(8, 8), :]))
    key_wide = jnp.broadcast_to(key_share, (FAR, LANES))
    rows = []
    for row in range(PIECE):
        rows.append(
            jnp.sum(key_wide * by_row[pl.ds(row * FAR, FAR), :], axis=0, keepdims=True)
        )
    key_out[...] = jnp.concatenate(rows, axis=0).astype(bf16)
    gain = jnp.sum(gain_share * by_row[pl.ds(PIECE * FAR, FAR), :], axis=0, keepdims=True)
    gain_out[...] = gain[:, :PIECE].astype(bf16)


def far_merge(dots, by_row):
    return pl.pallas_call(
        far_merge_kernel,
        out_shape=[
            jax.ShapeDtypeStruct((PIECE, LANES), bf16),
            jax.ShapeDtypeStruct((1, PIECE), bf16),
        ],
        in_specs=[VMEM_SPEC] * 2,
        out_specs=[VMEM_SPEC] * 2,
        compiler_params=PARAMS,
        name="far_merge",
    )(dots, by_row)


def paired(x, axis, apart):
    return lax.ppermute(x, axis, [(i, i ^ apart) for i in range(lax.axis_size(axis))])


def exchanged(x, axes):
    return lax.all_to_all(x, axes, 0, 0)


def body(hidden_states, key_cotangent, norm_gain, key_weight):
    place = lax.axis_index("zl").astype(jnp.int32).reshape(1)
    *pieces, gain_parts = local_grads(
        place, hidden_states, key_cotangent, norm_gain.reshape(FAR, LANES), key_weight
    )
    with jax.named_scope("near_exchange"):
        arrived = {apart: paired(pieces[apart], "zl", apart) for apart in (2, 3, 1)}
    with jax.named_scope("gain_exchange"):
        gain_parts = exchanged(gain_parts, ("zl", "x", "core"))
    pieces = [pieces[0]] + [arrived[apart] for apart in range(1, NEAR)]
    dots, gains = near_dots(place, gain_parts, pieces)
    with jax.named_scope("near_dots_sum"):
        dots = exchanged(dots, ("zl", "x", "core"))
    values = near_merge(place, dots, gains, pieces)
    with jax.named_scope("far_exchange"):
        values = exchanged(values, ("y", "zh"))
    dots, by_row = far_dots(values)
    with jax.named_scope("far_dots_sum"):
        dots = jnp.sum(exchanged(dots, ("y", "x", "core")), axis=0)
        dots = lax.psum(lax.psum(dots, "zl"), "zh")
    merged_key, merged_gain = far_merge(dots, by_row)
    return (merged_key, merged_gain.reshape(PIECE))


def solution(mesh):
    split = Mesh(mesh.devices.reshape(4, FAR_Z, NEAR, 4, 2), ("y", "zh", "zl", "x", "core"))
    rows = ("y", "zh", "zl")
    columns = ("x", "core")
    return jax.shard_map(
        body,
        mesh=split,
        in_specs=(P(rows, None), P(rows, columns), P(), P(None, columns)),
        out_specs=(P(rows, columns), P(rows)),
        check_vma=False,
    )
```

```python
import jax
import jax.numpy as jnp
from jax import lax
from jax.experimental import pallas as pl
from jax.experimental.pallas import tpu as pltpu
from jax.sharding import Mesh
from jax.sharding import PartitionSpec as P

eps_norm = 1e-05
eps_merge = 1e-06

f32 = jnp.float32
bf16 = jnp.bfloat16

NEAR = 4
FAR = 32
FAR_Z = 8
WIDTH = 8
GAIN_AT = 16
PIECE = 32
LANES = 128
VMEM_SPEC = pl.BlockSpec(memory_space=pltpu.VMEM)
SMEM_SPEC = pl.BlockSpec(memory_space=pltpu.SMEM)
HBM_SPEC = pl.BlockSpec(memory_space=pltpu.HBM)
PARAMS = pltpu.CompilerParams(vmem_limit_bytes=16 << 20)


def in_hbm(x):
    return pltpu.with_memory_space_constraint(x, pltpu.HBM)


def factor(cross, own_sq):
    return 1.0 - cross / (2.0 * (jnp.maximum(own_sq, 0.0) + eps_merge))


def grads_kernel(
    place, hidden_hbm, cot_hbm, gain_hbm, p0, p1, p2, p3, inv_wide, hidden, cot, gain, pieces, sems
):
    tokens, width = hidden.shape
    parts = 8
    height = tokens // parts
    copies = [
        pltpu.make_async_copy(
            hidden_hbm.at[pl.ds(part * height, height)],
            hidden.at[pl.ds(part * height, height)],
            sems.at[part],
        )
        for part in range(parts)
    ]
    for at, (there, here) in enumerate(((cot_hbm, cot), (gain_hbm, gain))):
        copies.append(pltpu.make_async_copy(there, here, sems.at[parts + at]))
    for copy in copies:
        copy.start()
    blocks = width // LANES
    for part in range(parts):
        rows = pl.ds(part * height, height)
        copies[part].wait()
        totals = [jnp.zeros((height, LANES), f32) for _ in range(2)]
        for block in range(blocks):
            x = hidden[rows, pl.ds(block * LANES, LANES)].astype(f32)
            totals[block % 2] = totals[block % 2] + x * x
        mean = jnp.sum(totals[0] + totals[1], axis=1, keepdims=True) * (1.0 / width)
        inv_wide[rows, :] = jnp.broadcast_to(lax.rsqrt(mean + eps_norm), (height, LANES))
    for copy in copies[parts:]:
        copy.wait()
    for chunk in range(blocks // 4):
        inv = inv_wide[...]
        inputs = []
        for block in range(4 * chunk, 4 * chunk + 4):
            x = hidden[:, pl.ds(block * LANES, LANES)].astype(f32) * inv
            inputs.append((x * gain[pl.ds(block, 1), :]).astype(bf16))
        grad = lax.dot_general(
            jnp.concatenate(inputs, axis=1),
            cot[...],
            (((0,), (0,)), ((), ())),
            preferred_element_type=f32,
        ).astype(bf16)
        for sub in range(4):
            for near in range(NEAR):
                at = sub * LANES + near * PIECE
                pieces[near, pl.ds((4 * chunk + sub) * PIECE, PIECE), :] = grad[at : at + PIECE]
    here = place[0]
    for apart, out in enumerate((p0, p1, p2, p3)):
        out[...] = pieces[here ^ apart]


def local_grads(place, hidden, cot, gain):
    piece = jax.ShapeDtypeStruct((FAR * PIECE, LANES), bf16)
    return pl.pallas_call(
        grads_kernel,
        out_shape=[piece] * NEAR + [jax.ShapeDtypeStruct((hidden.shape[0], LANES), f32)],
        in_specs=[SMEM_SPEC] + [HBM_SPEC] * 3,
        out_specs=[VMEM_SPEC] * (NEAR + 1),
        scratch_shapes=[
            pltpu.VMEM(hidden.shape, bf16),
            pltpu.VMEM(cot.shape, bf16),
            pltpu.VMEM(gain.shape, f32),
            pltpu.VMEM((NEAR, FAR * PIECE, LANES), bf16),
            pltpu.SemaphoreType.DMA((10,)),
        ],
        compiler_params=PARAMS,
        name="local_grads",
    )(place, in_hbm(hidden), in_hbm(cot), in_hbm(gain))


def gains_kernel(
    hidden_hbm, cot_hbm, weight_hbm, inv_wide, p1, p1_out, out, hidden, cot, weight, rows, sems
):
    blocks = hidden.shape[1] // LANES
    step = 4 * LANES
    copies = [pltpu.make_async_copy(cot_hbm, cot, sems.at[0])]
    for part in range(2):
        half = pl.ds(part * (blocks // 2) * LANES, (blocks // 2) * LANES)
        copies.append(
            pltpu.make_async_copy(weight_hbm.at[half], weight.at[half], sems.at[1 + part])
        )
        copies.append(
            pltpu.make_async_copy(
                hidden_hbm.at[:, half], hidden.at[:, half], sems.at[3 + part]
            )
        )
    for copy in copies:
        copy.start()
    p1_out[...] = p1[...]
    for copy in copies[:3]:
        copy.wait()
    for chunk in range(blocks // 4):
        if chunk == blocks // 8:
            for copy in copies[3:]:
                copy.wait()
        back = lax.dot_general(
            cot[...],
            weight[pl.ds(chunk * step, step), :],
            (((1,), (1,)), ((), ())),
            preferred_element_type=f32,
        )
        inv = inv_wide[...]
        for sub in range(4):
            block = 4 * chunk + sub
            normed = hidden[:, pl.ds(block * LANES, LANES)].astype(f32) * inv
            rows[pl.ds(block, 1), :] = jnp.sum(
                back[:, sub * LANES : (sub + 1) * LANES] * normed, axis=0, keepdims=True
            )
    lane = lax.broadcasted_iota(jnp.int32, (8, LANES), 1)
    for near in range(NEAR):
        total = jnp.zeros((8, LANES), f32)
        for block in range(4):
            part = jnp.where(lane // PIECE == near, rows[pl.ds(8 * block, 8), :], 0.0)
            turn = PIECE * (block - near) % LANES
            total = total + (pltpu.roll(part, turn, 1) if turn else part)
        for other in range(WIDTH):
            out[near * WIDTH + other] = total


def local_gains(hidden, cot, weight, inv_wide, p1):
    return pl.pallas_call(
        gains_kernel,
        out_shape=[
            jax.ShapeDtypeStruct(p1.shape, bf16),
            jax.ShapeDtypeStruct((NEAR * WIDTH, 8, LANES), f32),
        ],
        in_specs=[HBM_SPEC] * 3 + [VMEM_SPEC] * 2,
        out_specs=[VMEM_SPEC] * 2,
        scratch_shapes=[
            pltpu.VMEM(hidden.shape, bf16),
            pltpu.VMEM(cot.shape, bf16),
            pltpu.VMEM(weight.shape, bf16),
            pltpu.VMEM((FAR, LANES), f32),
            pltpu.SemaphoreType.DMA((5,)),
        ],
        compiler_params=PARAMS,
        cost_estimate=pl.CostEstimate(
            flops=2 * hidden.shape[0] * weight.size,
            bytes_accessed=2 * (hidden.size + weight.size),
            transcendentals=0,
        ),
        name="local_gains",
    )(in_hbm(hidden), in_hbm(cot), in_hbm(weight), inv_wide, p1)


def all_sum(x):
    return jnp.sum(jnp.sum(x, axis=0, keepdims=True), axis=1, keepdims=True)


def near_dots_kernel(place, p3, p2, p1, p0, gain_parts, out, gain_out):
    refs = (p0, p1, p2, p3)
    pairs = [(a, b) for a in range(NEAR) for b in range(a, NEAR)]
    rows = 64

    def add(step, totals):
        values = [ref[pl.ds(step * rows, rows), :].astype(f32) for ref in refs]
        return tuple(
            total + jnp.sum((values[a] * values[b]).reshape(rows // 8, 8, LANES), axis=0)
            for total, (a, b) in zip(totals, pairs)
        )

    totals = lax.fori_loop(
        0, p0.shape[0] // rows, add, tuple(jnp.zeros((8, LANES), f32) for _ in pairs)
    )
    here = place[0]
    lane = lax.broadcasted_iota(jnp.int32, (1, LANES), 1)
    row = jnp.zeros((1, LANES), f32)
    for total, (a, b) in zip(totals, pairs):
        dot = all_sum(total)
        row = jnp.where(lane == ((NEAR * a + b) ^ (5 * here)), dot, row)
        row = jnp.where(lane == ((NEAR * b + a) ^ (5 * here)), dot, row)
    gain = []
    for near in range(NEAR):
        total = gain_parts[near * WIDTH]
        for other in range(1, WIDTH):
            total = total + gain_parts[near * WIDTH + other]
        gain.append(total.astype(bf16).astype(f32))
        gain_out[pl.ds(8 * near, 8), :] = gain[near]
    for a, b in pairs:
        row = jnp.where(lane == GAIN_AT + NEAR * a + b, all_sum(gain[a] * gain[b]), row)
    out[...] = jnp.broadcast_to(row.reshape(1, 1, LANES), out.shape)


def near_dots(place, gain_parts, pieces):
    return pl.pallas_call(
        near_dots_kernel,
        out_shape=[
            jax.ShapeDtypeStruct((NEAR * WIDTH, 1, LANES), f32),
            jax.ShapeDtypeStruct((NEAR * 8, LANES), f32),
        ],
        in_specs=[SMEM_SPEC] + [VMEM_SPEC] * (1 + NEAR),
        out_specs=[VMEM_SPEC] * 2,
        compiler_params=PARAMS,
        name="near_dots",
    )(place, *pieces[::-1], gain_parts)


def near_shares(dots):
    low = (factor(dots[0][1], dots[0][0]), factor(dots[0][1], dots[1][1]))
    high = (factor(dots[2][3], dots[2][2]), factor(dots[2][3], dots[3][3]))
    low_sq = (
        low[0] * low[0] * dots[0][0]
        + 2.0 * (low[0] * low[1] * dots[0][1])
        + low[1] * low[1] * dots[1][1]
    )
    high_sq = (
        high[0] * high[0] * dots[2][2]
        + 2.0 * (high[0] * high[1] * dots[2][3])
        + high[1] * high[1] * dots[3][3]
    )
    cross = low[0] * (high[0] * dots[0][2] + high[1] * dots[0][3]) + low[1] * (
        high[0] * dots[1][2] + high[1] * dots[1][3]
    )
    of_low = factor(cross, low_sq)
    of_high = factor(cross, high_sq)
    return (of_low * low[0], of_low * low[1], of_high * high[0], of_high * high[1])


def sent_at(far):
    return far % FAR_Z * (FAR // FAR_Z) + far // FAR_Z


def packed(dots):
    total = dots[0:8]
    for block in range(1, 4):
        total = total + pltpu.roll(dots[8 * block : 8 * block + 8], 32 * block, 1)
    return total


def unpacked(rows):
    lane = lax.broadcasted_iota(jnp.int32, (8, LANES), 1)
    blocks = []
    for block in range(4):
        moved = rows if block == 0 else pltpu.roll(rows, LANES - 32 * block, 1)
        blocks.append(jnp.where(lane < FAR, moved, 0.0))
    return jnp.concatenate(blocks, axis=0)


def near_merge_kernel(place, p3, p2, p1, p0, dots, gains, out):
    here = place[0]
    row = jnp.sum(dots[...], axis=0)
    lane = lax.broadcasted_iota(jnp.int32, (1, LANES), 1)
    row = jnp.where(lane < GAIN_AT, row, row * (1.0 / WIDTH))

    def shares_at(first):
        def entry(a, b):
            at = first + NEAR * a + b
            return jnp.sum(jnp.where(lane == at, row, 0.0), axis=1, keepdims=True)

        return near_shares(
            [[entry(a, b) if a <= b else None for b in range(NEAR)] for a in range(NEAR)]
        )

    shares = shares_at(0)
    by_apart = []
    for apart in range(NEAR):
        share = shares[apart]
        for other in range(1, NEAR):
            share = jnp.where(here == other, shares[other ^ apart], share)
        by_apart.append(share)
    for far in range(FAR):
        rows = pl.ds(far * PIECE, PIECE)
        total = by_apart[0] * p0[rows, :].astype(f32)
        for share, ref in zip(by_apart[1:], (p1, p2, p3)):
            total = total + share * ref[rows, :].astype(f32)
        out[sent_at(far), pl.ds(0, PIECE), :] = total.astype(bf16)

    gain_shares = shares_at(GAIN_AT)
    merged = gain_shares[0] * gains[pl.ds(0, 8), :]
    for near in range(1, NEAR):
        merged = merged + gain_shares[near] * gains[pl.ds(8 * near, 8), :]
    merged = unpacked(merged)
    for far in range(FAR):
        out[sent_at(far), pl.ds(PIECE, 8), :] = jnp.broadcast_to(merged[far : far + 1], (8, LANES)).astype(bf16)


def near_merge(place, dots, gains, pieces):
    return pl.pallas_call(
        near_merge_kernel,
        out_shape=jax.ShapeDtypeStruct((FAR, PIECE + 8, LANES), bf16),
        in_specs=[SMEM_SPEC] + [VMEM_SPEC] * (2 + NEAR),
        out_specs=VMEM_SPEC,
        compiler_params=PARAMS,
        name="near_merge",
    )(place, *pieces[::-1], dots, gains)


def far_dots_kernel(values, out, by_row, wide):
    for far in range(FAR):
        wide[pl.ds(far * (PIECE + 8), PIECE + 8), :] = values[sent_at(far)].astype(f32)
    columns = []
    for row in range(PIECE + 1):
        block = wide[pl.ds(row, FAR, stride=PIECE + 8), :]
        by_row[pl.ds(row * FAR, FAR), :] = block
        columns.append(block.astype(bf16))

    def dots(matrix):
        padded = jnp.concatenate(
            [matrix, jnp.zeros((LANES - FAR, matrix.shape[1]), bf16)], axis=0
        )
        return lax.dot_general(
            matrix, padded, (((1,), (1,)), ((), ())), preferred_element_type=f32
        )

    key_rows = packed(dots(jnp.concatenate(columns[:PIECE], axis=1)))
    gain_rows = packed(dots(columns[PIECE])) * (1.0 / WIDTH)
    out[...] = jnp.broadcast_to(jnp.concatenate([key_rows, gain_rows], axis=0)[None], out.shape)


def far_dots(values):
    return pl.pallas_call(
        far_dots_kernel,
        out_shape=[
            jax.ShapeDtypeStruct((4 * WIDTH, 16, LANES), f32),
            jax.ShapeDtypeStruct(((PIECE + 1) * FAR, LANES), f32),
        ],
        in_specs=[VMEM_SPEC],
        out_specs=[VMEM_SPEC] * 2,
        scratch_shapes=[pltpu.VMEM((FAR * (PIECE + 8), LANES), f32)],
        compiler_params=PARAMS,
        name="far_dots",
    )(values)


def far_shares(dots):
    shape = dots.shape
    row = lax.broadcasted_iota(jnp.int32, shape, 0)
    lane = lax.broadcasted_iota(jnp.int32, shape, 1)
    share = jnp.ones((shape[0], 1), f32)
    for level in range(5):
        same = (row >> level) == (lane >> level)
        across = ((row >> level) ^ 1) == (lane >> level)
        own_part = jnp.sum(jnp.where(same, dots, 0.0), axis=0, keepdims=True)
        cross_part = jnp.sum(jnp.where(across, dots, 0.0), axis=0, keepdims=True)
        own_sq = jnp.sum(jnp.where(same, own_part, 0.0), axis=1, keepdims=True)
        cross = jnp.sum(jnp.where(same, cross_part, 0.0), axis=1, keepdims=True)
        scale = factor(cross, own_sq)
        share = share * scale
        if level < 4:
            scale_row = jnp.sum(jnp.where(row == lane, scale, 0.0), axis=0, keepdims=True)
            dots = dots * scale * scale_row
    return share


def far_merge_kernel(dots, by_row, key_out, gain_out):
    key_share = far_shares(unpacked(dots[pl.ds(0, 8), :]))
    gain_share = far_shares(unpacked(dots[pl.ds(8, 8), :]))
    key_wide = jnp.broadcast_to(key_share, (FAR, LANES))
    rows = []
    for row in range(PIECE):
        rows.append(
            jnp.sum(key_wide * by_row[pl.ds(row * FAR, FAR), :], axis=0, keepdims=True)
        )
    key_out[...] = jnp.concatenate(rows, axis=0).astype(bf16)
    gain = jnp.sum(gain_share * by_row[pl.ds(PIECE * FAR, FAR), :], axis=0, keepdims=True)
    gain_out[...] = gain[:, :PIECE].astype(bf16)


def far_merge(dots, by_row):
    return pl.pallas_call(
        far_merge_kernel,
        out_shape=[
            jax.ShapeDtypeStruct((PIECE, LANES), bf16),
            jax.ShapeDtypeStruct((1, PIECE), bf16),
        ],
        in_specs=[VMEM_SPEC] * 2,
        out_specs=[VMEM_SPEC] * 2,
        compiler_params=PARAMS,
        name="far_merge",
    )(dots, by_row)


def paired(x, axis, apart):
    return lax.ppermute(x, axis, [(i, i ^ apart) for i in range(lax.axis_size(axis))])


def exchanged(x, axes):
    return lax.all_to_all(x, axes, 0, 0)


def body(hidden_states, key_cotangent, norm_gain, key_weight):
    place = lax.axis_index("zl").astype(jnp.int32).reshape(1)
    *pieces, inv_wide = local_grads(
        place, hidden_states, key_cotangent, norm_gain.reshape(FAR, LANES)
    )
    with jax.named_scope("near_exchange"):
        arrived = {apart: paired(pieces[apart], "zl", apart) for apart in (3, 2)}
        piece, gain_parts = local_gains(
            hidden_states, key_cotangent, key_weight, inv_wide, pieces[1]
        )
        arrived[1] = paired(piece, "zl", 1)
    with jax.named_scope("gain_exchange"):
        gain_parts = exchanged(gain_parts, ("zl", "x", "core"))
    pieces = [pieces[0]] + [arrived[apart] for apart in range(1, NEAR)]
    dots, gains = near_dots(place, gain_parts, pieces)
    with jax.named_scope("near_dots_sum"):
        dots = exchanged(dots, ("zl", "x", "core"))
    values = near_merge(place, dots, gains, pieces)
    with jax.named_scope("far_exchange"):
        values = exchanged(values, ("zh", "y"))
    dots, by_row = far_dots(values)
    with jax.named_scope("far_dots_sum"):
        dots = jnp.sum(exchanged(dots, ("y", "x", "core")), axis=0)
        dots = lax.psum(lax.psum(dots, "zl"), "zh")
    merged_key, merged_gain = far_merge(dots, by_row)
    return (merged_key, merged_gain.reshape(PIECE))


def solution(mesh):
    split = Mesh(mesh.devices.reshape(4, FAR_Z, NEAR, 4, 2), ("y", "zh", "zl", "x", "core"))
    rows = ("y", "zh", "zl")
    columns = ("x", "core")
    return jax.shard_map(
        body,
        mesh=split,
        in_specs=(P(rows, None), P(rows, columns), P(), P(None, columns)),
        out_specs=(P(rows, columns), P(rows)),
        check_vma=False,
    )
```

```python
import jax
import jax.numpy as jnp
from jax import lax
from jax.experimental import pallas as pl
from jax.experimental.pallas import tpu as pltpu
from jax.sharding import Mesh
from jax.sharding import PartitionSpec as P

eps_norm = 1e-05
eps_merge = 1e-06

f32 = jnp.float32
bf16 = jnp.bfloat16

NEAR = 4
FAR = 32
FAR_Z = 8
WIDTH = 8
NEAR_PAIRS = [(a, b) for a in range(NEAR) for b in range(a, NEAR)]
PIECE = 32
LANES = 128
VMEM_SPEC = pl.BlockSpec(memory_space=pltpu.VMEM)
SMEM_SPEC = pl.BlockSpec(memory_space=pltpu.SMEM)
HBM_SPEC = pl.BlockSpec(memory_space=pltpu.HBM)
PARAMS = pltpu.CompilerParams(vmem_limit_bytes=16 << 20)


def in_hbm(x):
    return pltpu.with_memory_space_constraint(x, pltpu.HBM)


def factor(cross, own_sq):
    return 1.0 - cross / (2.0 * (jnp.maximum(own_sq, 0.0) + eps_merge))


def grads_kernel(
    place, hidden_hbm, cot_hbm, gain_hbm, p0, p1, p2, p3, inv_wide, hidden, cot, gain, pieces, sems
):
    tokens, width = hidden.shape
    parts = 8
    height = tokens // parts
    copies = [
        pltpu.make_async_copy(
            hidden_hbm.at[pl.ds(part * height, height)],
            hidden.at[pl.ds(part * height, height)],
            sems.at[part],
        )
        for part in range(parts)
    ]
    for at, (there, here) in enumerate(((cot_hbm, cot), (gain_hbm, gain))):
        copies.append(pltpu.make_async_copy(there, here, sems.at[parts + at]))
    for copy in copies:
        copy.start()
    blocks = width // LANES
    for part in range(parts):
        rows = pl.ds(part * height, height)
        copies[part].wait()
        totals = [jnp.zeros((height, LANES), f32) for _ in range(2)]
        for block in range(blocks):
            x = hidden[rows, pl.ds(block * LANES, LANES)].astype(f32)
            totals[block % 2] = totals[block % 2] + x * x
        mean = jnp.sum(totals[0] + totals[1], axis=1, keepdims=True) * (1.0 / width)
        inv_wide[rows, :] = jnp.broadcast_to(lax.rsqrt(mean + eps_norm), (height, LANES))
    for copy in copies[parts:]:
        copy.wait()
    for chunk in range(blocks // 4):
        inv = inv_wide[...]
        inputs = []
        for block in range(4 * chunk, 4 * chunk + 4):
            x = hidden[:, pl.ds(block * LANES, LANES)].astype(f32) * inv
            inputs.append((x * gain[pl.ds(block, 1), :]).astype(bf16))
        grad = lax.dot_general(
            jnp.concatenate(inputs, axis=1),
            cot[...],
            (((0,), (0,)), ((), ())),
            preferred_element_type=f32,
        ).astype(bf16)
        for sub in range(4):
            for near in range(NEAR):
                at = sub * LANES + near * PIECE
                pieces[near, pl.ds((4 * chunk + sub) * PIECE, PIECE), :] = grad[at : at + PIECE]
    here = place[0]
    for apart, out in enumerate((p0, p1, p2, p3)):
        out[...] = pieces[here ^ apart]


def local_grads(place, hidden, cot, gain):
    piece = jax.ShapeDtypeStruct((FAR * PIECE, LANES), bf16)
    return pl.pallas_call(
        grads_kernel,
        out_shape=[piece] * NEAR + [jax.ShapeDtypeStruct((hidden.shape[0], LANES), f32)],
        in_specs=[SMEM_SPEC] + [HBM_SPEC] * 3,
        out_specs=[VMEM_SPEC] * (NEAR + 1),
        scratch_shapes=[
            pltpu.VMEM(hidden.shape, bf16),
            pltpu.VMEM(cot.shape, bf16),
            pltpu.VMEM(gain.shape, f32),
            pltpu.VMEM((NEAR, FAR * PIECE, LANES), bf16),
            pltpu.SemaphoreType.DMA((10,)),
        ],
        compiler_params=PARAMS,
        name="local_grads",
    )(place, in_hbm(hidden), in_hbm(cot), in_hbm(gain))


def gains_kernel(
    hidden_hbm, cot_hbm, weight_hbm, inv_wide, rows, hidden, cot, weight, sems
):
    blocks = hidden.shape[1] // LANES
    step = 4 * LANES
    copies = [pltpu.make_async_copy(cot_hbm, cot, sems.at[0])]
    for part in range(2):
        half = pl.ds(part * (blocks // 2) * LANES, (blocks // 2) * LANES)
        copies.append(
            pltpu.make_async_copy(weight_hbm.at[half], weight.at[half], sems.at[1 + part])
        )
        copies.append(
            pltpu.make_async_copy(
                hidden_hbm.at[:, half], hidden.at[:, half], sems.at[3 + part]
            )
        )
    for copy in copies:
        copy.start()
    for copy in copies[:3]:
        copy.wait()
    for chunk in range(blocks // 4):
        if chunk == blocks // 8:
            for copy in copies[3:]:
                copy.wait()
        back = lax.dot_general(
            cot[...],
            weight[pl.ds(chunk * step, step), :],
            (((1,), (1,)), ((), ())),
            preferred_element_type=f32,
        )
        inv = inv_wide[...]
        for sub in range(4):
            block = 4 * chunk + sub
            normed = hidden[:, pl.ds(block * LANES, LANES)].astype(f32) * inv
            rows[pl.ds(block, 1), :] = jnp.sum(
                back[:, sub * LANES : (sub + 1) * LANES] * normed, axis=0, keepdims=True
            )


def local_gains(hidden, cot, weight, inv_wide):
    return pl.pallas_call(
        gains_kernel,
        out_shape=jax.ShapeDtypeStruct((FAR, LANES), f32),
        in_specs=[HBM_SPEC] * 3 + [VMEM_SPEC],
        out_specs=VMEM_SPEC,
        scratch_shapes=[
            pltpu.VMEM(hidden.shape, bf16),
            pltpu.VMEM(cot.shape, bf16),
            pltpu.VMEM(weight.shape, bf16),
            pltpu.SemaphoreType.DMA((5,)),
        ],
        compiler_params=PARAMS,
        cost_estimate=pl.CostEstimate(
            flops=2 * hidden.shape[0] * weight.size,
            bytes_accessed=2 * (hidden.size + weight.size),
            transcendentals=0,
        ),
        name="local_gains",
    )(in_hbm(hidden), in_hbm(cot), in_hbm(weight), inv_wide)


def all_sum(x):
    return jnp.sum(jnp.sum(x, axis=0, keepdims=True), axis=1, keepdims=True)


def near_dots_kernel(place, p3, p2, p1, p0, gains, out, gain_out):
    refs = (p0, p1, p2, p3)
    pairs = NEAR_PAIRS
    rows = 64

    def add(step, totals):
        values = [ref[pl.ds(step * rows, rows), :].astype(f32) for ref in refs]
        return tuple(
            total + jnp.sum((values[a] * values[b]).reshape(rows // 8, 8, LANES), axis=0)
            for total, (a, b) in zip(totals, pairs)
        )

    totals = lax.fori_loop(
        0, p0.shape[0] // rows, add, tuple(jnp.zeros((8, LANES), f32) for _ in pairs)
    )
    here = place[0]
    lane = lax.broadcasted_iota(jnp.int32, (1, LANES), 1)
    row = jnp.zeros((1, LANES), f32)
    for total, (a, b) in zip(totals, pairs):
        dot = all_sum(total)
        row = jnp.where(lane == ((NEAR * a + b) ^ (5 * here)), dot, row)
        row = jnp.where(lane == ((NEAR * b + a) ^ (5 * here)), dot, row)
    out[...] = jnp.broadcast_to(row.reshape(1, 1, LANES), out.shape)
    gain = [gains[near] for near in range(NEAR)]
    gain_shares = near_shares(
        [[all_sum(gain[a] * gain[b]) if a <= b else None for b in range(NEAR)] for a in range(NEAR)]
    )
    merged = gain_shares[0] * gain[0]
    for near in range(1, NEAR):
        merged = merged + gain_shares[near] * gain[near]
    gain_out[...] = merged


def near_dots(place, pieces, gains):
    return pl.pallas_call(
        near_dots_kernel,
        out_shape=[
            jax.ShapeDtypeStruct((NEAR * WIDTH, 1, LANES), f32),
            jax.ShapeDtypeStruct((FAR, LANES), f32),
        ],
        in_specs=[SMEM_SPEC] + [VMEM_SPEC] * (NEAR + 1),
        out_specs=[VMEM_SPEC] * 2,
        compiler_params=PARAMS,
        cost_estimate=pl.CostEstimate(
            flops=20 * pieces[0].size, bytes_accessed=8 * pieces[0].size, transcendentals=0
        ),
        name="near_dots",
    )(place, *pieces[::-1], gains)


def near_shares(dots):
    low = (factor(dots[0][1], dots[0][0]), factor(dots[0][1], dots[1][1]))
    high = (factor(dots[2][3], dots[2][2]), factor(dots[2][3], dots[3][3]))
    low_sq = (
        low[0] * low[0] * dots[0][0]
        + 2.0 * (low[0] * low[1] * dots[0][1])
        + low[1] * low[1] * dots[1][1]
    )
    high_sq = (
        high[0] * high[0] * dots[2][2]
        + 2.0 * (high[0] * high[1] * dots[2][3])
        + high[1] * high[1] * dots[3][3]
    )
    cross = low[0] * (high[0] * dots[0][2] + high[1] * dots[0][3]) + low[1] * (
        high[0] * dots[1][2] + high[1] * dots[1][3]
    )
    of_low = factor(cross, low_sq)
    of_high = factor(cross, high_sq)
    return (of_low * low[0], of_low * low[1], of_high * high[0], of_high * high[1])


def sent_at(far):
    return far % FAR_Z * (FAR // FAR_Z) + far // FAR_Z


def packed(dots):
    total = dots[0:8]
    for block in range(1, 4):
        total = total + pltpu.roll(dots[8 * block : 8 * block + 8], 32 * block, 1)
    return total


def unpacked(rows):
    lane = lax.broadcasted_iota(jnp.int32, (8, LANES), 1)
    blocks = []
    for block in range(4):
        moved = rows if block == 0 else pltpu.roll(rows, LANES - 32 * block, 1)
        blocks.append(jnp.where(lane < FAR, moved, 0.0))
    return jnp.concatenate(blocks, axis=0)


def near_merge_kernel(place, p3, p2, p1, p0, dots, gains, out):
    here = place[0]
    row = jnp.sum(dots[...], axis=0)
    lane = lax.broadcasted_iota(jnp.int32, (1, LANES), 1)

    def entry(a, b):
        return jnp.sum(jnp.where(lane == NEAR * a + b, row, 0.0), axis=1, keepdims=True)

    shares = near_shares([[entry(a, b) if a <= b else None for b in range(NEAR)] for a in range(NEAR)])
    by_apart = []
    for apart in range(NEAR):
        share = shares[apart]
        for other in range(1, NEAR):
            share = jnp.where(here == other, shares[other ^ apart], share)
        by_apart.append(share)
    for far in range(FAR):
        rows = pl.ds(far * PIECE, PIECE)
        total = by_apart[0] * p0[rows, :].astype(f32)
        for share, ref in zip(by_apart[1:], (p1, p2, p3)):
            total = total + share * ref[rows, :].astype(f32)
        out[sent_at(far), pl.ds(0, PIECE), :] = total.astype(bf16)

    merged = gains[...]
    for far in range(FAR):
        out[sent_at(far), pl.ds(PIECE, 8), :] = jnp.broadcast_to(merged[far : far + 1], (8, LANES)).astype(bf16)


def near_merge(place, dots, gains, pieces):
    return pl.pallas_call(
        near_merge_kernel,
        out_shape=jax.ShapeDtypeStruct((FAR, PIECE + 8, LANES), bf16),
        in_specs=[SMEM_SPEC] + [VMEM_SPEC] * (2 + NEAR),
        out_specs=VMEM_SPEC,
        compiler_params=PARAMS,
        name="near_merge",
    )(place, *pieces[::-1], dots, gains)


def far_dots_kernel(values, out, by_row, wide):
    for far in range(FAR):
        wide[pl.ds(far * (PIECE + 8), PIECE + 8), :] = values[sent_at(far)].astype(f32)
    columns = []
    for row in range(PIECE + 1):
        block = wide[pl.ds(row, FAR, stride=PIECE + 8), :]
        by_row[pl.ds(row * FAR, FAR), :] = block
        columns.append(block.astype(bf16))

    def dots(matrix):
        padded = jnp.concatenate(
            [matrix, jnp.zeros((LANES - FAR, matrix.shape[1]), bf16)], axis=0
        )
        return lax.dot_general(
            matrix, padded, (((1,), (1,)), ((), ())), preferred_element_type=f32
        )

    key_rows = packed(dots(jnp.concatenate(columns[:PIECE], axis=1)))
    gain_rows = packed(dots(columns[PIECE])) * (1.0 / (NEAR * WIDTH))
    out[...] = jnp.broadcast_to(jnp.concatenate([key_rows, gain_rows], axis=0)[None], out.shape)


def far_dots(values):
    return pl.pallas_call(
        far_dots_kernel,
        out_shape=[
            jax.ShapeDtypeStruct((4 * WIDTH, 16, LANES), f32),
            jax.ShapeDtypeStruct(((PIECE + 1) * FAR, LANES), f32),
        ],
        in_specs=[VMEM_SPEC],
        out_specs=[VMEM_SPEC] * 2,
        scratch_shapes=[pltpu.VMEM((FAR * (PIECE + 8), LANES), f32)],
        compiler_params=PARAMS,
        name="far_dots",
    )(values)


def far_shares(dots):
    shape = dots.shape
    row = lax.broadcasted_iota(jnp.int32, shape, 0)
    lane = lax.broadcasted_iota(jnp.int32, shape, 1)
    share = jnp.ones((shape[0], 1), f32)
    for level in range(5):
        same = (row >> level) == (lane >> level)
        across = ((row >> level) ^ 1) == (lane >> level)
        own_part = jnp.sum(jnp.where(same, dots, 0.0), axis=0, keepdims=True)
        cross_part = jnp.sum(jnp.where(across, dots, 0.0), axis=0, keepdims=True)
        own_sq = jnp.sum(jnp.where(same, own_part, 0.0), axis=1, keepdims=True)
        cross = jnp.sum(jnp.where(same, cross_part, 0.0), axis=1, keepdims=True)
        scale = factor(cross, own_sq)
        share = share * scale
        if level < 4:
            scale_row = jnp.sum(jnp.where(row == lane, scale, 0.0), axis=0, keepdims=True)
            dots = dots * scale * scale_row
    return share


def far_merge_kernel(place, dots, by_row, key_out, gain_out):
    key_share = far_shares(unpacked(dots[pl.ds(0, 8), :]))
    gain_share = far_shares(unpacked(dots[pl.ds(8, 8), :]))
    key_wide = jnp.broadcast_to(key_share, (FAR, LANES))
    rows = []
    for row in range(PIECE):
        rows.append(
            jnp.sum(key_wide * by_row[pl.ds(row * FAR, FAR), :], axis=0, keepdims=True)
        )
    key_out[...] = jnp.concatenate(rows, axis=0).astype(bf16)
    gain = jnp.sum(gain_share * by_row[pl.ds(PIECE * FAR, FAR), :], axis=0, keepdims=True)
    wide = jnp.broadcast_to(gain, (8, LANES))
    moved = wide
    for near in range(1, NEAR):
        moved = jnp.where(place[0] == near, pltpu.roll(wide, LANES - PIECE * near, 1), moved)
    gain_out[...] = moved[0:1, :PIECE].astype(bf16)


def far_merge(place, dots, by_row):
    return pl.pallas_call(
        far_merge_kernel,
        out_shape=[
            jax.ShapeDtypeStruct((PIECE, LANES), bf16),
            jax.ShapeDtypeStruct((1, PIECE), bf16),
        ],
        in_specs=[SMEM_SPEC] + [VMEM_SPEC] * 2,
        out_specs=[VMEM_SPEC] * 2,
        compiler_params=PARAMS,
        name="far_merge",
    )(place, dots, by_row)


def paired(x, axis, apart):
    return lax.ppermute(x, axis, [(i, i ^ apart) for i in range(lax.axis_size(axis))])


def exchanged(x, axes):
    return lax.all_to_all(x, axes, 0, 0)


def body(hidden_states, key_cotangent, norm_gain, key_weight):
    place = lax.axis_index("zl").astype(jnp.int32).reshape(1)
    *pieces, inv_wide = local_grads(
        place, hidden_states, key_cotangent, norm_gain.reshape(FAR, LANES)
    )
    with jax.named_scope("near_exchange"):
        arrived = {apart: paired(pieces[apart], "zl", apart) for apart in (3, 2, 1)}
    with jax.named_scope("gain_sum"):
        gain = local_gains(hidden_states, key_cotangent, key_weight, inv_wide)
        gain = jnp.sum(lax.all_gather(gain, ("x", "core")), axis=0)
        gains = lax.all_gather(lax.reduce_precision(gain, 8, 7), "zl")
    pieces = [pieces[0]] + [arrived[apart] for apart in range(1, NEAR)]
    dots, gain = near_dots(place, pieces, gains)
    with jax.named_scope("near_dots_sum"):
        dots = exchanged(dots, ("zl", "x", "core"))
    values = near_merge(place, dots, gain, pieces)
    with jax.named_scope("far_exchange"):
        values = exchanged(values, ("zh", "y"))
    dots, by_row = far_dots(values)
    with jax.named_scope("far_dots_sum"):
        dots = jnp.sum(exchanged(dots, ("y", "x", "core")), axis=0)
        dots = lax.psum(lax.psum(dots, "zl"), "zh")
    merged_key, merged_gain = far_merge(place, dots, by_row)
    return (merged_key, merged_gain.reshape(PIECE))


def solution(mesh):
    split = Mesh(mesh.devices.reshape(4, FAR_Z, NEAR, 4, 2), ("y", "zh", "zl", "x", "core"))
    rows = ("y", "zh", "zl")
    columns = ("x", "core")
    return jax.shard_map(
        body,
        mesh=split,
        in_specs=(P(rows, None), P(rows, columns), P(), P(None, columns)),
        out_specs=(P(rows, columns), P(rows)),
        check_vma=False,
    )
```

```python
import jax
import jax.numpy as jnp
from jax import lax
from jax.experimental import pallas as pl
from jax.experimental.pallas import tpu as pltpu
from jax.sharding import Mesh
from jax.sharding import PartitionSpec as P

eps_norm = 1e-05
eps_merge = 1e-06

f32 = jnp.float32
bf16 = jnp.bfloat16

NEAR = 4
FAR = 32
FAR_Z = 8
WIDTH = 8
NEAR_PAIRS = [(a, b) for a in range(NEAR) for b in range(a, NEAR)]
PIECE = 32
LANES = 128
VMEM_SPEC = pl.BlockSpec(memory_space=pltpu.VMEM)
SMEM_SPEC = pl.BlockSpec(memory_space=pltpu.SMEM)
HBM_SPEC = pl.BlockSpec(memory_space=pltpu.HBM)
PARAMS = pltpu.CompilerParams(vmem_limit_bytes=16 << 20)


def in_hbm(x):
    return pltpu.with_memory_space_constraint(x, pltpu.HBM)


def factor(cross, own_sq):
    return 1.0 - cross / (2.0 * (jnp.maximum(own_sq, 0.0) + eps_merge))


def grads_kernel(
    place, hidden_hbm, cot_hbm, gain_hbm, p0, p1, p2, p3, inv_wide, hidden, cot, gain, pieces, sems
):
    tokens, width = hidden.shape
    parts = 8
    height = tokens // parts
    copies = [
        pltpu.make_async_copy(
            hidden_hbm.at[pl.ds(part * height, height)],
            hidden.at[pl.ds(part * height, height)],
            sems.at[part],
        )
        for part in range(parts)
    ]
    for at, (there, here) in enumerate(((cot_hbm, cot), (gain_hbm, gain))):
        copies.append(pltpu.make_async_copy(there, here, sems.at[parts + at]))
    for copy in copies:
        copy.start()
    blocks = width // LANES
    for part in range(parts):
        rows = pl.ds(part * height, height)
        copies[part].wait()
        totals = [jnp.zeros((height, LANES), f32) for _ in range(2)]
        for block in range(blocks):
            x = hidden[rows, pl.ds(block * LANES, LANES)].astype(f32)
            totals[block % 2] = totals[block % 2] + x * x
        mean = jnp.sum(totals[0] + totals[1], axis=1, keepdims=True) * (1.0 / width)
        inv_wide[rows, :] = jnp.broadcast_to(lax.rsqrt(mean + eps_norm), (height, LANES))
    for copy in copies[parts:]:
        copy.wait()
    for chunk in range(blocks // 4):
        inv = inv_wide[...]
        inputs = []
        for block in range(4 * chunk, 4 * chunk + 4):
            x = hidden[:, pl.ds(block * LANES, LANES)].astype(f32) * inv
            inputs.append((x * gain[pl.ds(block, 1), :]).astype(bf16))
        grad = lax.dot_general(
            jnp.concatenate(inputs, axis=1),
            cot[...],
            (((0,), (0,)), ((), ())),
            preferred_element_type=f32,
        ).astype(bf16)
        for sub in range(4):
            for near in range(NEAR):
                at = sub * LANES + near * PIECE
                pieces[near, pl.ds((4 * chunk + sub) * PIECE, PIECE), :] = grad[at : at + PIECE]
    here = place[0]
    for apart, out in enumerate((p0, p1, p2, p3)):
        out[...] = pieces[here ^ apart]


def local_grads(place, hidden, cot, gain):
    piece = jax.ShapeDtypeStruct((FAR * PIECE, LANES), bf16)
    return pl.pallas_call(
        grads_kernel,
        out_shape=[piece] * NEAR + [jax.ShapeDtypeStruct((hidden.shape[0], LANES), f32)],
        in_specs=[SMEM_SPEC] + [HBM_SPEC] * 3,
        out_specs=[VMEM_SPEC] * (NEAR + 1),
        scratch_shapes=[
            pltpu.VMEM(hidden.shape, bf16),
            pltpu.VMEM(cot.shape, bf16),
            pltpu.VMEM(gain.shape, f32),
            pltpu.VMEM((NEAR, FAR * PIECE, LANES), bf16),
            pltpu.SemaphoreType.DMA((10,)),
        ],
        compiler_params=PARAMS,
        name="local_grads",
    )(place, in_hbm(hidden), in_hbm(cot), in_hbm(gain))


def gains_kernel(
    hidden_hbm, cot_hbm, weight_hbm, inv_wide, rows, hidden, cot, weight, sems
):
    blocks = hidden.shape[1] // LANES
    step = 4 * LANES
    copies = [pltpu.make_async_copy(cot_hbm, cot, sems.at[0])]
    for part in range(2):
        half = pl.ds(part * (blocks // 2) * LANES, (blocks // 2) * LANES)
        copies.append(
            pltpu.make_async_copy(weight_hbm.at[half], weight.at[half], sems.at[1 + part])
        )
        copies.append(
            pltpu.make_async_copy(
                hidden_hbm.at[:, half], hidden.at[:, half], sems.at[3 + part]
            )
        )
    for copy in copies:
        copy.start()
    for copy in copies[:3]:
        copy.wait()
    for chunk in range(blocks // 4):
        if chunk == blocks // 8:
            for copy in copies[3:]:
                copy.wait()
        back = lax.dot_general(
            cot[...],
            weight[pl.ds(chunk * step, step), :],
            (((1,), (1,)), ((), ())),
            preferred_element_type=f32,
        )
        inv = inv_wide[...]
        for sub in range(4):
            block = 4 * chunk + sub
            normed = hidden[:, pl.ds(block * LANES, LANES)].astype(f32) * inv
            rows[pl.ds(block, 1), :] = jnp.sum(
                back[:, sub * LANES : (sub + 1) * LANES] * normed, axis=0, keepdims=True
            )


def local_gains(hidden, cot, weight, inv_wide):
    return pl.pallas_call(
        gains_kernel,
        out_shape=jax.ShapeDtypeStruct((FAR, LANES), f32),
        in_specs=[HBM_SPEC] * 3 + [VMEM_SPEC],
        out_specs=VMEM_SPEC,
        scratch_shapes=[
            pltpu.VMEM(hidden.shape, bf16),
            pltpu.VMEM(cot.shape, bf16),
            pltpu.VMEM(weight.shape, bf16),
            pltpu.SemaphoreType.DMA((5,)),
        ],
        compiler_params=PARAMS,
        cost_estimate=pl.CostEstimate(
            flops=2 * hidden.shape[0] * weight.size,
            bytes_accessed=2 * (hidden.size + weight.size),
            transcendentals=0,
        ),
        name="local_gains",
    )(in_hbm(hidden), in_hbm(cot), in_hbm(weight), inv_wide)


def all_sum(x):
    return jnp.sum(jnp.sum(x, axis=0, keepdims=True), axis=1, keepdims=True)


def near_dots_kernel(place, p3, p2, p1, p0, gain_parts, out, gain_out):
    refs = (p0, p1, p2, p3)
    pairs = NEAR_PAIRS
    rows = 64

    def add(step, totals):
        values = [ref[pl.ds(step * rows, rows), :].astype(f32) for ref in refs]
        return tuple(
            total + jnp.sum((values[a] * values[b]).reshape(rows // 8, 8, LANES), axis=0)
            for total, (a, b) in zip(totals, pairs)
        )

    totals = lax.fori_loop(
        0, p0.shape[0] // rows, add, tuple(jnp.zeros((8, LANES), f32) for _ in pairs)
    )
    here = place[0]
    lane = lax.broadcasted_iota(jnp.int32, (1, LANES), 1)
    row = jnp.zeros((1, LANES), f32)
    for total, (a, b) in zip(totals, pairs):
        dot = all_sum(total)
        row = jnp.where(lane == ((NEAR * a + b) ^ (5 * here)), dot, row)
        row = jnp.where(lane == ((NEAR * b + a) ^ (5 * here)), dot, row)
    out[...] = jnp.broadcast_to(row.reshape(1, 1, LANES), out.shape)
    total = gain_parts[0]
    for part in range(1, WIDTH):
        total = total + gain_parts[part]
    gain_out[...] = total.astype(bf16)


def near_dots(place, pieces, gain_parts):
    return pl.pallas_call(
        near_dots_kernel,
        out_shape=[
            jax.ShapeDtypeStruct((NEAR * WIDTH, 1, LANES), f32),
            jax.ShapeDtypeStruct((FAR, LANES), bf16),
        ],
        in_specs=[SMEM_SPEC] + [VMEM_SPEC] * (NEAR + 1),
        out_specs=[VMEM_SPEC] * 2,
        compiler_params=PARAMS,
        cost_estimate=pl.CostEstimate(
            flops=20 * pieces[0].size, bytes_accessed=8 * pieces[0].size, transcendentals=0
        ),
        name="near_dots",
    )(place, *pieces[::-1], gain_parts)


def near_shares(dots):
    low = (factor(dots[0][1], dots[0][0]), factor(dots[0][1], dots[1][1]))
    high = (factor(dots[2][3], dots[2][2]), factor(dots[2][3], dots[3][3]))
    low_sq = (
        low[0] * low[0] * dots[0][0]
        + 2.0 * (low[0] * low[1] * dots[0][1])
        + low[1] * low[1] * dots[1][1]
    )
    high_sq = (
        high[0] * high[0] * dots[2][2]
        + 2.0 * (high[0] * high[1] * dots[2][3])
        + high[1] * high[1] * dots[3][3]
    )
    cross = low[0] * (high[0] * dots[0][2] + high[1] * dots[0][3]) + low[1] * (
        high[0] * dots[1][2] + high[1] * dots[1][3]
    )
    of_low = factor(cross, low_sq)
    of_high = factor(cross, high_sq)
    square = (
        of_low * of_low * low_sq + 2.0 * (of_low * of_high * cross) + of_high * of_high * high_sq
    )
    return (of_low * low[0], of_low * low[1], of_high * high[0], of_high * high[1]), square


def bf16_parts(x):
    parts = []
    for _ in range(3):
        part = x.astype(bf16).astype(f32)
        parts.append(part)
        x = x - part
    return parts


def sent_at(far):
    return far % FAR_Z * (FAR // FAR_Z) + far // FAR_Z


def packed(dots):
    total = dots[0:8]
    for block in range(1, 4):
        total = total + pltpu.roll(dots[8 * block : 8 * block + 8], 32 * block, 1)
    return total


def unpacked(rows):
    lane = lax.broadcasted_iota(jnp.int32, (8, LANES), 1)
    blocks = []
    for block in range(4):
        moved = rows if block == 0 else pltpu.roll(rows, LANES - 32 * block, 1)
        blocks.append(jnp.where(lane < FAR, moved, 0.0))
    return jnp.concatenate(blocks, axis=0)


def near_merge_kernel(place, p3, p2, p1, p0, dots, gains, out):
    here = place[0]
    row = jnp.sum(dots[...], axis=0)
    lane = lax.broadcasted_iota(jnp.int32, (1, LANES), 1)

    def entry(a, b):
        return jnp.sum(jnp.where(lane == NEAR * a + b, row, 0.0), axis=1, keepdims=True)

    shares, square = near_shares([[entry(a, b) if a <= b else None for b in range(NEAR)] for a in range(NEAR)])
    by_apart = []
    for apart in range(NEAR):
        share = shares[apart]
        for other in range(1, NEAR):
            share = jnp.where(here == other, shares[other ^ apart], share)
        by_apart.append(share)
    for far in range(FAR):
        rows = pl.ds(far * PIECE, PIECE)
        total = by_apart[0] * p0[rows, :].astype(f32)
        for share, ref in zip(by_apart[1:], (p1, p2, p3)):
            total = total + share * ref[rows, :].astype(f32)
        out[sent_at(far), pl.ds(0, PIECE), :] = total.astype(bf16)

    gain = [gains[near].astype(f32) for near in range(NEAR)]
    gain_shares, gain_square = near_shares(
        [[all_sum(gain[a] * gain[b]) if a <= b else None for b in range(NEAR)] for a in range(NEAR)]
    )
    merged = gain_shares[0] * gain[0]
    for near in range(1, NEAR):
        merged = merged + gain_shares[near] * gain[near]
    squares = jnp.zeros((1, LANES), f32)
    for at, part in enumerate(bf16_parts(square) + bf16_parts(gain_square)):
        squares = jnp.where(lane == at, part, squares)
    which = lax.broadcasted_iota(jnp.int32, (8, LANES), 0)
    for far in range(FAR):
        last = jnp.where(which == 0, merged[far : far + 1], jnp.where(which == 1, squares, 0.0))
        out[sent_at(far), pl.ds(PIECE, 8), :] = last.astype(bf16)


def near_merge(place, dots, gains, pieces):
    return pl.pallas_call(
        near_merge_kernel,
        out_shape=jax.ShapeDtypeStruct((FAR, PIECE + 8, LANES), bf16),
        in_specs=[SMEM_SPEC] + [VMEM_SPEC] * (2 + NEAR),
        out_specs=VMEM_SPEC,
        compiler_params=PARAMS,
        name="near_merge",
    )(place, *pieces[::-1], dots, gains)


def far_dots_kernel(values, out, by_row, wide):
    for far in range(FAR):
        wide[pl.ds(far * (PIECE + 8), PIECE + 8), :] = values[sent_at(far)].astype(f32)
    columns = []
    for row in range(PIECE + 2):
        block = wide[pl.ds(row, FAR, stride=PIECE + 8), :]
        by_row[pl.ds(row * FAR, FAR), :] = block
        columns.append(block.astype(bf16))

    def dots(matrix):
        padded = jnp.concatenate(
            [matrix, jnp.zeros((LANES - FAR, matrix.shape[1]), bf16)], axis=0
        )
        return lax.dot_general(
            matrix, padded, (((1,), (1,)), ((), ())), preferred_element_type=f32
        )

    key_dots = dots(jnp.concatenate(columns[:PIECE], axis=1))
    gain_dots = dots(columns[PIECE]) * (1.0 / (NEAR * WIDTH))
    row = lax.broadcasted_iota(jnp.int32, key_dots.shape, 0)
    lane = lax.broadcasted_iota(jnp.int32, key_dots.shape, 1)
    both = jnp.where(row < lane, key_dots, jnp.where(row > lane, gain_dots, 0.0))
    out[...] = jnp.broadcast_to(packed(both)[None], out.shape)


def far_dots(values):
    return pl.pallas_call(
        far_dots_kernel,
        out_shape=[
            jax.ShapeDtypeStruct((4 * WIDTH, 8, LANES), f32),
            jax.ShapeDtypeStruct(((PIECE + 2) * FAR, LANES), f32),
        ],
        in_specs=[VMEM_SPEC],
        out_specs=[VMEM_SPEC] * 2,
        scratch_shapes=[pltpu.VMEM((FAR * (PIECE + 8), LANES), f32)],
        compiler_params=PARAMS,
        name="far_dots",
    )(values)


def far_shares(dots, squares):
    row = lax.broadcasted_iota(jnp.int32, dots.shape, 0)
    lane = lax.broadcasted_iota(jnp.int32, dots.shape, 1)
    share = jnp.ones((dots.shape[0], 1), f32)
    square_row = jnp.sum(jnp.where(row == lane, squares, 0.0), axis=0, keepdims=True)
    for level in range(5):
        same = (row >> level) == (lane >> level)
        pair = (row >> (level + 1)) == (lane >> (level + 1))
        own_part = jnp.sum(jnp.where(same, dots, 0.0), axis=0, keepdims=True)
        cross_part = jnp.sum(jnp.where(same, 0.0, jnp.where(pair, dots, 0.0)), axis=0, keepdims=True)
        own_part = 2.0 * own_part + square_row
        own_sq = jnp.sum(jnp.where(same, own_part, 0.0), axis=1, keepdims=True)
        cross = jnp.sum(jnp.where(pair, cross_part, 0.0), axis=1, keepdims=True)
        scale = factor(cross, own_sq)
        share = share * scale
        if level < 4:
            scale_row = jnp.sum(jnp.where(row == lane, scale, 0.0), axis=0, keepdims=True)
            dots = dots * scale * scale_row
            square_row = square_row * scale_row * scale_row
    return share


def far_merge_kernel(place, dots, by_row, key_out, gain_out):
    dots = unpacked(dots[...])
    row = lax.broadcasted_iota(jnp.int32, dots.shape, 0)
    lane = lax.broadcasted_iota(jnp.int32, dots.shape, 1)
    squares = by_row[pl.ds((PIECE + 1) * FAR, FAR), :]
    key_square = jnp.sum(jnp.where(lane < 3, squares, 0.0), axis=1, keepdims=True)
    gain_square = jnp.sum(
        jnp.where(lane < 3, 0.0, jnp.where(lane < 6, squares, 0.0)), axis=1, keepdims=True
    )
    key_share = far_shares(jnp.where(row < lane, dots, 0.0), key_square)
    gain_share = far_shares(jnp.where(row > lane, dots, 0.0), gain_square)
    key_wide = jnp.broadcast_to(key_share, (FAR, LANES))
    rows = []
    for at in range(PIECE):
        rows.append(jnp.sum(key_wide * by_row[pl.ds(at * FAR, FAR), :], axis=0, keepdims=True))
    key_out[...] = jnp.concatenate(rows, axis=0).astype(bf16)
    gain = jnp.sum(gain_share * by_row[pl.ds(PIECE * FAR, FAR), :], axis=0, keepdims=True)
    wide = jnp.broadcast_to(gain, (8, LANES))
    moved = wide
    for near in range(1, NEAR):
        moved = jnp.where(place[0] == near, pltpu.roll(wide, LANES - PIECE * near, 1), moved)
    gain_out[...] = moved[0:1, :PIECE].astype(bf16)


def far_merge(place, dots, by_row):
    return pl.pallas_call(
        far_merge_kernel,
        out_shape=[
            jax.ShapeDtypeStruct((PIECE, LANES), bf16),
            jax.ShapeDtypeStruct((1, PIECE), bf16),
        ],
        in_specs=[SMEM_SPEC] + [VMEM_SPEC] * 2,
        out_specs=[VMEM_SPEC] * 2,
        compiler_params=PARAMS,
        name="far_merge",
    )(place, dots, by_row)


def paired(x, axis, apart):
    return lax.ppermute(x, axis, [(i, i ^ apart) for i in range(lax.axis_size(axis))])


def exchanged(x, axes):
    return lax.all_to_all(x, axes, 0, 0)


def body(hidden_states, key_cotangent, norm_gain, key_weight):
    place = lax.axis_index("zl").astype(jnp.int32).reshape(1)
    *pieces, inv_wide = local_grads(
        place, hidden_states, key_cotangent, norm_gain.reshape(FAR, LANES)
    )
    with jax.named_scope("near_exchange"):
        arrived = {apart: paired(pieces[apart], "zl", apart) for apart in (3, 2, 1)}
    with jax.named_scope("gain_parts"):
        gain = local_gains(hidden_states, key_cotangent, key_weight, inv_wide)
        gain_parts = lax.all_gather(gain, ("x", "core"))
    pieces = [pieces[0]] + [arrived[apart] for apart in range(1, NEAR)]
    dots, gain = near_dots(place, pieces, gain_parts)
    with jax.named_scope("near_dots_sum"):
        dots = exchanged(dots, ("zl", "x", "core"))
    with jax.named_scope("near_gains"):
        gains = lax.all_gather(gain, "zl")
    values = near_merge(place, dots, gains, pieces)
    with jax.named_scope("far_exchange"):
        values = exchanged(values, ("zh", "y"))
    dots, by_row = far_dots(values)
    with jax.named_scope("far_dots_sum"):
        dots = jnp.sum(exchanged(dots, ("y", "x", "core")), axis=0)
        dots = lax.psum(lax.psum(dots, "zl"), "zh")
    merged_key, merged_gain = far_merge(place, dots, by_row)
    return (merged_key, merged_gain.reshape(PIECE))


def solution(mesh):
    split = Mesh(mesh.devices.reshape(4, FAR_Z, NEAR, 4, 2), ("y", "zh", "zl", "x", "core"))
    rows = ("y", "zh", "zl")
    columns = ("x", "core")
    return jax.shard_map(
        body,
        mesh=split,
        in_specs=(P(rows, None), P(rows, columns), P(), P(None, columns)),
        out_specs=(P(rows, columns), P(rows)),
        check_vma=False,
    )
```

```python
import jax
import jax.numpy as jnp
from jax import lax
from jax.experimental import pallas as pl
from jax.experimental.pallas import tpu as pltpu
from jax.sharding import Mesh
from jax.sharding import PartitionSpec as P

eps_norm = 1e-05
eps_merge = 1e-06

f32 = jnp.float32
bf16 = jnp.bfloat16

NEAR = 4
FAR = 32
FAR_Z = 8
WIDTH = 8
GAIN_ROWS = FAR // WIDTH
NEAR_PAIRS = [(a, b) for a in range(NEAR) for b in range(a, NEAR)]
PIECE = 32
LANES = 128
VMEM_SPEC = pl.BlockSpec(memory_space=pltpu.VMEM)
SMEM_SPEC = pl.BlockSpec(memory_space=pltpu.SMEM)
HBM_SPEC = pl.BlockSpec(memory_space=pltpu.HBM)
PARAMS = pltpu.CompilerParams(vmem_limit_bytes=16 << 20)


def in_hbm(x):
    return pltpu.with_memory_space_constraint(x, pltpu.HBM)


def factor(cross, own_sq):
    return 1.0 - cross / (2.0 * (jnp.maximum(own_sq, 0.0) + eps_merge))


def grads_kernel(
    place, hidden_hbm, cot_hbm, gain_hbm, p0, p1, p2, p3, inv_wide, hidden, cot, gain, pieces, sems
):
    tokens, width = hidden.shape
    parts = 8
    height = tokens // parts
    copies = [
        pltpu.make_async_copy(
            hidden_hbm.at[pl.ds(part * height, height)],
            hidden.at[pl.ds(part * height, height)],
            sems.at[part],
        )
        for part in range(parts)
    ]
    for at, (there, here) in enumerate(((cot_hbm, cot), (gain_hbm, gain))):
        copies.append(pltpu.make_async_copy(there, here, sems.at[parts + at]))
    for copy in copies:
        copy.start()
    blocks = width // LANES
    for part in range(parts):
        rows = pl.ds(part * height, height)
        copies[part].wait()
        totals = [jnp.zeros((height, LANES), f32) for _ in range(2)]
        for block in range(blocks):
            x = hidden[rows, pl.ds(block * LANES, LANES)].astype(f32)
            totals[block % 2] = totals[block % 2] + x * x
        mean = jnp.sum(totals[0] + totals[1], axis=1, keepdims=True) * (1.0 / width)
        inv_wide[rows, :] = jnp.broadcast_to(lax.rsqrt(mean + eps_norm), (height, LANES))
    for copy in copies[parts:]:
        copy.wait()
    for chunk in range(blocks // 4):
        inv = inv_wide[...]
        inputs = []
        for block in range(4 * chunk, 4 * chunk + 4):
            x = hidden[:, pl.ds(block * LANES, LANES)].astype(f32) * inv
            inputs.append((x * gain[pl.ds(block, 1), :]).astype(bf16))
        grad = lax.dot_general(
            jnp.concatenate(inputs, axis=1),
            cot[...],
            (((0,), (0,)), ((), ())),
            preferred_element_type=f32,
        ).astype(bf16)
        for sub in range(4):
            for near in range(NEAR):
                at = sub * LANES + near * PIECE
                pieces[near, pl.ds((4 * chunk + sub) * PIECE, PIECE), :] = grad[at : at + PIECE]
    here = place[0] // WIDTH
    for apart, out in enumerate((p0, p1, p2, p3)):
        out[...] = pieces[here ^ apart]


def local_grads(place, hidden, cot, gain):
    piece = jax.ShapeDtypeStruct((FAR * PIECE, LANES), bf16)
    return pl.pallas_call(
        grads_kernel,
        out_shape=[piece] * NEAR + [jax.ShapeDtypeStruct((hidden.shape[0], LANES), f32)],
        in_specs=[SMEM_SPEC] + [HBM_SPEC] * 3,
        out_specs=[VMEM_SPEC] * (NEAR + 1),
        scratch_shapes=[
            pltpu.VMEM(hidden.shape, bf16),
            pltpu.VMEM(cot.shape, bf16),
            pltpu.VMEM(gain.shape, f32),
            pltpu.VMEM((NEAR, FAR * PIECE, LANES), bf16),
            pltpu.SemaphoreType.DMA((10,)),
        ],
        compiler_params=PARAMS,
        name="local_grads",
    )(place, in_hbm(hidden), in_hbm(cot), in_hbm(gain))


def gains_kernel(
    hidden_hbm, cot_hbm, weight_hbm, inv_wide, rows, hidden, cot, weight, sems
):
    blocks = hidden.shape[1] // LANES
    step = 4 * LANES
    copies = [pltpu.make_async_copy(cot_hbm, cot, sems.at[0])]
    for part in range(2):
        half = pl.ds(part * (blocks // 2) * LANES, (blocks // 2) * LANES)
        copies.append(
            pltpu.make_async_copy(weight_hbm.at[half], weight.at[half], sems.at[1 + part])
        )
        copies.append(
            pltpu.make_async_copy(
                hidden_hbm.at[:, half], hidden.at[:, half], sems.at[3 + part]
            )
        )
    for copy in copies:
        copy.start()
    for copy in copies[:3]:
        copy.wait()
    for chunk in range(blocks // 4):
        if chunk == blocks // 8:
            for copy in copies[3:]:
                copy.wait()
        back = lax.dot_general(
            cot[...],
            weight[pl.ds(chunk * step, step), :],
            (((1,), (1,)), ((), ())),
            preferred_element_type=f32,
        )
        inv = inv_wide[...]
        for sub in range(4):
            block = 4 * chunk + sub
            normed = hidden[:, pl.ds(block * LANES, LANES)].astype(f32) * inv
            rows[pl.ds(block, 1), :] = jnp.sum(
                back[:, sub * LANES : (sub + 1) * LANES] * normed, axis=0, keepdims=True
            )


def local_gains(hidden, cot, weight, inv_wide):
    return pl.pallas_call(
        gains_kernel,
        out_shape=jax.ShapeDtypeStruct((FAR, LANES), f32),
        in_specs=[HBM_SPEC] * 3 + [VMEM_SPEC],
        out_specs=VMEM_SPEC,
        scratch_shapes=[
            pltpu.VMEM(hidden.shape, bf16),
            pltpu.VMEM(cot.shape, bf16),
            pltpu.VMEM(weight.shape, bf16),
            pltpu.SemaphoreType.DMA((5,)),
        ],
        compiler_params=PARAMS,
        cost_estimate=pl.CostEstimate(
            flops=2 * hidden.shape[0] * weight.size,
            bytes_accessed=2 * (hidden.size + weight.size),
            transcendentals=0,
        ),
        name="local_gains",
    )(in_hbm(hidden), in_hbm(cot), in_hbm(weight), inv_wide)


def all_sum(x):
    return jnp.sum(jnp.sum(x, axis=0, keepdims=True), axis=1, keepdims=True)


def near_dots_kernel(place, p3, p2, p1, p0, gain_parts, out, shares_of):
    refs = (p0, p1, p2, p3)
    pairs = NEAR_PAIRS
    rows = 64

    def add(step, totals):
        values = [ref[pl.ds(step * rows, rows), :].astype(f32) for ref in refs]
        return tuple(
            total + jnp.sum((values[a] * values[b]).reshape(rows // 8, 8, LANES), axis=0)
            for total, (a, b) in zip(totals, pairs)
        )

    totals = lax.fori_loop(
        0, p0.shape[0] // rows, add, tuple(jnp.zeros((8, LANES), f32) for _ in pairs)
    )
    here = place[0] // WIDTH
    lane = lax.broadcasted_iota(jnp.int32, (1, LANES), 1)
    row = jnp.zeros((1, LANES), f32)
    for total, (a, b) in zip(totals, pairs):
        dot = all_sum(total)
        row = jnp.where(lane == ((NEAR * a + b) ^ (5 * here)), dot, row)
        row = jnp.where(lane == ((NEAR * b + a) ^ (5 * here)), dot, row)
    total = gain_parts[0]
    for part in range(1, WIDTH):
        total = total + gain_parts[part]
    total = total.astype(bf16).astype(f32)
    for part in range(WIDTH):
        shares_of[part] = total[part * GAIN_ROWS : (part + 1) * GAIN_ROWS]
    message = jnp.concatenate(
        [row, shares_of[place[0] % WIDTH], jnp.zeros((7 - GAIN_ROWS, LANES), f32)], axis=0
    )
    out[...] = jnp.broadcast_to(message[None], out.shape)


def near_dots(place, pieces, gain_parts):
    return pl.pallas_call(
        near_dots_kernel,
        out_shape=jax.ShapeDtypeStruct((NEAR * WIDTH, 8, LANES), f32),
        in_specs=[SMEM_SPEC] + [VMEM_SPEC] * (NEAR + 1),
        out_specs=VMEM_SPEC,
        scratch_shapes=[pltpu.VMEM((WIDTH, GAIN_ROWS, LANES), f32)],
        compiler_params=PARAMS,
        cost_estimate=pl.CostEstimate(
            flops=20 * pieces[0].size, bytes_accessed=8 * pieces[0].size, transcendentals=0
        ),
        name="near_dots",
    )(place, *pieces[::-1], gain_parts)


def near_shares(dots):
    low = (factor(dots[0][1], dots[0][0]), factor(dots[0][1], dots[1][1]))
    high = (factor(dots[2][3], dots[2][2]), factor(dots[2][3], dots[3][3]))
    low_sq = (
        low[0] * low[0] * dots[0][0]
        + 2.0 * (low[0] * low[1] * dots[0][1])
        + low[1] * low[1] * dots[1][1]
    )
    high_sq = (
        high[0] * high[0] * dots[2][2]
        + 2.0 * (high[0] * high[1] * dots[2][3])
        + high[1] * high[1] * dots[3][3]
    )
    cross = low[0] * (high[0] * dots[0][2] + high[1] * dots[0][3]) + low[1] * (
        high[0] * dots[1][2] + high[1] * dots[1][3]
    )
    of_low = factor(cross, low_sq)
    of_high = factor(cross, high_sq)
    square = (
        of_low * of_low * low_sq + 2.0 * (of_low * of_high * cross) + of_high * of_high * high_sq
    )
    return (of_low * low[0], of_low * low[1], of_high * high[0], of_high * high[1]), square


def bf16_parts(x):
    parts = []
    for _ in range(3):
        part = x.astype(bf16).astype(f32)
        parts.append(part)
        x = x - part
    return parts


def sent_at(far):
    return far % FAR_Z * (FAR // FAR_Z) + far // FAR_Z


def packed(dots):
    total = dots[0:8]
    for block in range(1, 4):
        total = total + pltpu.roll(dots[8 * block : 8 * block + 8], 32 * block, 1)
    return total


def unpacked(rows):
    lane = lax.broadcasted_iota(jnp.int32, (8, LANES), 1)
    blocks = []
    for block in range(4):
        moved = rows if block == 0 else pltpu.roll(rows, LANES - 32 * block, 1)
        blocks.append(jnp.where(lane < FAR, moved, 0.0))
    return jnp.concatenate(blocks, axis=0)


def near_merge_kernel(place, p3, p2, p1, p0, messages, out, gains):
    here = place[0] // WIDTH
    row = jnp.sum(messages[:, pl.ds(0, 1), :], axis=0)
    lane = lax.broadcasted_iota(jnp.int32, (1, LANES), 1)

    def entry(a, b):
        return jnp.sum(jnp.where(lane == NEAR * a + b, row, 0.0), axis=1, keepdims=True)

    shares, square = near_shares([[entry(a, b) if a <= b else None for b in range(NEAR)] for a in range(NEAR)])
    by_apart = []
    for apart in range(NEAR):
        share = shares[apart]
        for other in range(1, NEAR):
            share = jnp.where(here == other, shares[other ^ apart], share)
        by_apart.append(share)
    for far in range(FAR):
        rows = pl.ds(far * PIECE, PIECE)
        total = by_apart[0] * p0[rows, :].astype(f32)
        for share, ref in zip(by_apart[1:], (p1, p2, p3)):
            total = total + share * ref[rows, :].astype(f32)
        out[sent_at(far), pl.ds(0, PIECE), :] = total.astype(bf16)

    for near in range(NEAR):
        for part in range(WIDTH):
            gains[near, pl.ds(part * GAIN_ROWS, GAIN_ROWS), :] = messages[
                near * WIDTH + part, pl.ds(1, GAIN_ROWS), :
            ]
    gain = [gains[near] for near in range(NEAR)]
    gain_shares, gain_square = near_shares(
        [[all_sum(gain[a] * gain[b]) if a <= b else None for b in range(NEAR)] for a in range(NEAR)]
    )
    merged = gain_shares[0] * gain[0]
    for near in range(1, NEAR):
        merged = merged + gain_shares[near] * gain[near]
    squares = jnp.zeros((1, LANES), f32)
    for at, part in enumerate(bf16_parts(square) + bf16_parts(gain_square)):
        squares = jnp.where(lane == at, part, squares)
    which = lax.broadcasted_iota(jnp.int32, (8, LANES), 0)
    for far in range(FAR):
        last = jnp.where(which == 0, merged[far : far + 1], jnp.where(which == 1, squares, 0.0))
        out[sent_at(far), pl.ds(PIECE, 8), :] = last.astype(bf16)


def near_merge(place, messages, pieces):
    return pl.pallas_call(
        near_merge_kernel,
        out_shape=jax.ShapeDtypeStruct((FAR, PIECE + 8, LANES), bf16),
        in_specs=[SMEM_SPEC] + [VMEM_SPEC] * (1 + NEAR),
        out_specs=VMEM_SPEC,
        scratch_shapes=[pltpu.VMEM((NEAR, FAR, LANES), f32)],
        compiler_params=PARAMS,
        name="near_merge",
    )(place, *pieces[::-1], messages)


def far_dots_kernel(values, out, by_row, wide):
    for far in range(FAR):
        wide[pl.ds(far * (PIECE + 8), PIECE + 8), :] = values[sent_at(far)].astype(f32)
    columns = []
    for row in range(PIECE + 2):
        block = wide[pl.ds(row, FAR, stride=PIECE + 8), :]
        by_row[pl.ds(row * FAR, FAR), :] = block
        columns.append(block.astype(bf16))

    def dots(matrix):
        padded = jnp.concatenate(
            [matrix, jnp.zeros((LANES - FAR, matrix.shape[1]), bf16)], axis=0
        )
        return lax.dot_general(
            matrix, padded, (((1,), (1,)), ((), ())), preferred_element_type=f32
        )

    key_dots = dots(jnp.concatenate(columns[:PIECE], axis=1))
    gain_dots = dots(columns[PIECE]) * (1.0 / (NEAR * WIDTH))
    row = lax.broadcasted_iota(jnp.int32, key_dots.shape, 0)
    lane = lax.broadcasted_iota(jnp.int32, key_dots.shape, 1)
    both = jnp.where(row < lane, key_dots, jnp.where(row > lane, gain_dots, 0.0))
    out[...] = jnp.broadcast_to(packed(both)[None], out.shape)


def far_dots(values):
    return pl.pallas_call(
        far_dots_kernel,
        out_shape=[
            jax.ShapeDtypeStruct((4 * WIDTH, 8, LANES), f32),
            jax.ShapeDtypeStruct(((PIECE + 2) * FAR, LANES), f32),
        ],
        in_specs=[VMEM_SPEC],
        out_specs=[VMEM_SPEC] * 2,
        scratch_shapes=[pltpu.VMEM((FAR * (PIECE + 8), LANES), f32)],
        compiler_params=PARAMS,
        name="far_dots",
    )(values)


def far_shares(dots, squares):
    row = lax.broadcasted_iota(jnp.int32, dots.shape, 0)
    lane = lax.broadcasted_iota(jnp.int32, dots.shape, 1)
    share = jnp.ones((dots.shape[0], 1), f32)
    square_row = jnp.sum(jnp.where(row == lane, squares, 0.0), axis=0, keepdims=True)
    for level in range(5):
        same = (row >> level) == (lane >> level)
        pair = (row >> (level + 1)) == (lane >> (level + 1))
        own_part = jnp.sum(jnp.where(same, dots, 0.0), axis=0, keepdims=True)
        cross_part = jnp.sum(jnp.where(same, 0.0, jnp.where(pair, dots, 0.0)), axis=0, keepdims=True)
        own_part = 2.0 * own_part + square_row
        own_sq = jnp.sum(jnp.where(same, own_part, 0.0), axis=1, keepdims=True)
        cross = jnp.sum(jnp.where(pair, cross_part, 0.0), axis=1, keepdims=True)
        scale = factor(cross, own_sq)
        share = share * scale
        if level < 4:
            scale_row = jnp.sum(jnp.where(row == lane, scale, 0.0), axis=0, keepdims=True)
            dots = dots * scale * scale_row
            square_row = square_row * scale_row * scale_row
    return share


def far_merge_kernel(place, dots, by_row, key_out, gain_out):
    dots = unpacked(dots[...])
    row = lax.broadcasted_iota(jnp.int32, dots.shape, 0)
    lane = lax.broadcasted_iota(jnp.int32, dots.shape, 1)
    squares = by_row[pl.ds((PIECE + 1) * FAR, FAR), :]
    key_square = jnp.sum(jnp.where(lane < 3, squares, 0.0), axis=1, keepdims=True)
    gain_square = jnp.sum(
        jnp.where(lane < 3, 0.0, jnp.where(lane < 6, squares, 0.0)), axis=1, keepdims=True
    )
    key_share = far_shares(jnp.where(row < lane, dots, 0.0), key_square)
    gain_share = far_shares(jnp.where(row > lane, dots, 0.0), gain_square)
    key_wide = jnp.broadcast_to(key_share, (FAR, LANES))
    rows = []
    for at in range(PIECE):
        rows.append(jnp.sum(key_wide * by_row[pl.ds(at * FAR, FAR), :], axis=0, keepdims=True))
    key_out[...] = jnp.concatenate(rows, axis=0).astype(bf16)
    gain = jnp.sum(gain_share * by_row[pl.ds(PIECE * FAR, FAR), :], axis=0, keepdims=True)
    wide = jnp.broadcast_to(gain, (8, LANES))
    moved = wide
    for near in range(1, NEAR):
        moved = jnp.where(place[0] // WIDTH == near, pltpu.roll(wide, LANES - PIECE * near, 1), moved)
    gain_out[...] = moved[0:1, :PIECE].astype(bf16)


def far_merge(place, dots, by_row):
    return pl.pallas_call(
        far_merge_kernel,
        out_shape=[
            jax.ShapeDtypeStruct((PIECE, LANES), bf16),
            jax.ShapeDtypeStruct((1, PIECE), bf16),
        ],
        in_specs=[SMEM_SPEC] + [VMEM_SPEC] * 2,
        out_specs=[VMEM_SPEC] * 2,
        compiler_params=PARAMS,
        name="far_merge",
    )(place, dots, by_row)


def paired(x, axis, apart):
    return lax.ppermute(x, axis, [(i, i ^ apart) for i in range(lax.axis_size(axis))])


def exchanged(x, axes):
    return lax.all_to_all(x, axes, 0, 0)


def body(hidden_states, key_cotangent, norm_gain, key_weight):
    place = lax.axis_index(("zl", "x", "core")).astype(jnp.int32).reshape(1)
    *pieces, inv_wide = local_grads(
        place, hidden_states, key_cotangent, norm_gain.reshape(FAR, LANES)
    )
    with jax.named_scope("near_exchange"):
        arrived = {apart: paired(pieces[apart], "zl", apart) for apart in (3, 2, 1)}
    with jax.named_scope("gain_parts"):
        gain = local_gains(hidden_states, key_cotangent, key_weight, inv_wide)
        gain_parts = lax.all_gather(gain, ("x", "core"))
    pieces = [pieces[0]] + [arrived[apart] for apart in range(1, NEAR)]
    messages = near_dots(place, pieces, gain_parts)
    with jax.named_scope("near_dots_sum"):
        messages = exchanged(messages, ("zl", "x", "core"))
    values = near_merge(place, messages, pieces)
    with jax.named_scope("far_exchange"):
        values = exchanged(values, ("zh", "y"))
    dots, by_row = far_dots(values)
    with jax.named_scope("far_dots_sum"):
        dots = jnp.sum(exchanged(dots, ("y", "x", "core")), axis=0)
        dots = lax.psum(lax.psum(dots, "zl"), "zh")
    merged_key, merged_gain = far_merge(place, dots, by_row)
    return (merged_key, merged_gain.reshape(PIECE))


def solution(mesh):
    split = Mesh(mesh.devices.reshape(4, FAR_Z, NEAR, 4, 2), ("y", "zh", "zl", "x", "core"))
    rows = ("y", "zh", "zl")
    columns = ("x", "core")
    return jax.shard_map(
        body,
        mesh=split,
        in_specs=(P(rows, None), P(rows, columns), P(), P(None, columns)),
        out_specs=(P(rows, columns), P(rows)),
        check_vma=False,
    )
```

```python
import jax
import jax.numpy as jnp
from jax import lax
from jax.experimental import pallas as pl
from jax.experimental.pallas import tpu as pltpu
from jax.sharding import Mesh
from jax.sharding import PartitionSpec as P

eps_norm = 1e-05
eps_merge = 1e-06

f32 = jnp.float32
bf16 = jnp.bfloat16

NEAR = 4
FAR = 32
FAR_Z = 8
WIDTH = 8
GAIN_ROWS = FAR // WIDTH
NEAR_PAIRS = [(a, b) for a in range(NEAR) for b in range(a, NEAR)]
PIECE = 32
LANES = 128
VMEM_SPEC = pl.BlockSpec(memory_space=pltpu.VMEM)
SMEM_SPEC = pl.BlockSpec(memory_space=pltpu.SMEM)
HBM_SPEC = pl.BlockSpec(memory_space=pltpu.HBM)
PARAMS = pltpu.CompilerParams(vmem_limit_bytes=16 << 20)


def in_hbm(x):
    return pltpu.with_memory_space_constraint(x, pltpu.HBM)


def factor(cross, own_sq):
    return 1.0 - cross / (2.0 * (jnp.maximum(own_sq, 0.0) + eps_merge))


def grads_kernel(
    place, hidden_hbm, cot_hbm, gain_hbm, p0, p1, p2, p3, inv_wide, hidden, cot, gain, pieces, sems
):
    tokens, width = hidden.shape
    parts = 8
    height = tokens // parts
    copies = [
        pltpu.make_async_copy(
            hidden_hbm.at[pl.ds(part * height, height)],
            hidden.at[pl.ds(part * height, height)],
            sems.at[part],
        )
        for part in range(parts)
    ]
    for at, (there, here) in enumerate(((cot_hbm, cot), (gain_hbm, gain))):
        copies.append(pltpu.make_async_copy(there, here, sems.at[parts + at]))
    for copy in copies:
        copy.start()
    blocks = width // LANES
    for part in range(parts):
        rows = pl.ds(part * height, height)
        copies[part].wait()
        totals = [jnp.zeros((height, LANES), f32) for _ in range(2)]
        for block in range(blocks):
            x = hidden[rows, pl.ds(block * LANES, LANES)].astype(f32)
            totals[block % 2] = totals[block % 2] + x * x
        mean = jnp.sum(totals[0] + totals[1], axis=1, keepdims=True) * (1.0 / width)
        inv_wide[rows, :] = jnp.broadcast_to(lax.rsqrt(mean + eps_norm), (height, LANES))
    for copy in copies[parts:]:
        copy.wait()
    for chunk in range(blocks // 4):
        inv = inv_wide[...]
        inputs = []
        for block in range(4 * chunk, 4 * chunk + 4):
            x = hidden[:, pl.ds(block * LANES, LANES)].astype(f32) * inv
            inputs.append((x * gain[pl.ds(block, 1), :]).astype(bf16))
        grad = lax.dot_general(
            jnp.concatenate(inputs, axis=1),
            cot[...],
            (((0,), (0,)), ((), ())),
            preferred_element_type=f32,
        ).astype(bf16)
        for sub in range(4):
            for near in range(NEAR):
                at = sub * LANES + near * PIECE
                pieces[near, pl.ds((4 * chunk + sub) * PIECE, PIECE), :] = grad[at : at + PIECE]
    here = place[0] // WIDTH
    for apart, out in enumerate((p0, p1, p2, p3)):
        out[...] = pieces[here ^ apart]


def local_grads(place, hidden, cot, gain):
    piece = jax.ShapeDtypeStruct((FAR * PIECE, LANES), bf16)
    return pl.pallas_call(
        grads_kernel,
        out_shape=[piece] * NEAR + [jax.ShapeDtypeStruct((hidden.shape[0], LANES), f32)],
        in_specs=[SMEM_SPEC] + [HBM_SPEC] * 3,
        out_specs=[VMEM_SPEC] * (NEAR + 1),
        scratch_shapes=[
            pltpu.VMEM(hidden.shape, bf16),
            pltpu.VMEM(cot.shape, bf16),
            pltpu.VMEM(gain.shape, f32),
            pltpu.VMEM((NEAR, FAR * PIECE, LANES), bf16),
            pltpu.SemaphoreType.DMA((10,)),
        ],
        compiler_params=PARAMS,
        name="local_grads",
    )(place, in_hbm(hidden), in_hbm(cot), in_hbm(gain))


def gains_kernel(
    hidden_hbm, cot_hbm, weight_hbm, inv_wide, rows, hidden, cot, weight, sems
):
    blocks = hidden.shape[1] // LANES
    step = 4 * LANES
    copies = [pltpu.make_async_copy(cot_hbm, cot, sems.at[0])]
    for part in range(2):
        half = pl.ds(part * (blocks // 2) * LANES, (blocks // 2) * LANES)
        copies.append(
            pltpu.make_async_copy(weight_hbm.at[half], weight.at[half], sems.at[1 + part])
        )
        copies.append(
            pltpu.make_async_copy(
                hidden_hbm.at[:, half], hidden.at[:, half], sems.at[3 + part]
            )
        )
    for copy in copies:
        copy.start()
    for copy in copies[:3]:
        copy.wait()
    for chunk in range(blocks // 4):
        if chunk == blocks // 8:
            for copy in copies[3:]:
                copy.wait()
        back = lax.dot_general(
            cot[...],
            weight[pl.ds(chunk * step, step), :],
            (((1,), (1,)), ((), ())),
            preferred_element_type=f32,
        )
        inv = inv_wide[...]
        for sub in range(4):
            block = 4 * chunk + sub
            normed = hidden[:, pl.ds(block * LANES, LANES)].astype(f32) * inv
            rows[pl.ds(block, 1), :] = jnp.sum(
                back[:, sub * LANES : (sub + 1) * LANES] * normed, axis=0, keepdims=True
            )


def local_gains(hidden, cot, weight, inv_wide):
    return pl.pallas_call(
        gains_kernel,
        out_shape=jax.ShapeDtypeStruct((FAR, LANES), f32),
        in_specs=[HBM_SPEC] * 3 + [VMEM_SPEC],
        out_specs=VMEM_SPEC,
        scratch_shapes=[
            pltpu.VMEM(hidden.shape, bf16),
            pltpu.VMEM(cot.shape, bf16),
            pltpu.VMEM(weight.shape, bf16),
            pltpu.SemaphoreType.DMA((5,)),
        ],
        compiler_params=PARAMS,
        cost_estimate=pl.CostEstimate(
            flops=2 * hidden.shape[0] * weight.size,
            bytes_accessed=2 * (hidden.size + weight.size),
            transcendentals=0,
        ),
        name="local_gains",
    )(in_hbm(hidden), in_hbm(cot), in_hbm(weight), inv_wide)


def all_sum(x):
    return jnp.sum(jnp.sum(x, axis=0, keepdims=True), axis=1, keepdims=True)


def near_dots_kernel(place, p3, p2, p1, p0, gain_parts, out, shares_of):
    refs = (p0, p1, p2, p3)
    pairs = NEAR_PAIRS
    rows = 64

    def add(step, totals):
        values = [ref[pl.ds(step * rows, rows), :].astype(f32) for ref in refs]
        return tuple(
            total + jnp.sum((values[a] * values[b]).reshape(rows // 8, 8, LANES), axis=0)
            for total, (a, b) in zip(totals, pairs)
        )

    totals = lax.fori_loop(
        0, p0.shape[0] // rows, add, tuple(jnp.zeros((8, LANES), f32) for _ in pairs)
    )
    here = place[0] // WIDTH
    lane = lax.broadcasted_iota(jnp.int32, (1, LANES), 1)
    row = jnp.zeros((1, LANES), f32)
    for total, (a, b) in zip(totals, pairs):
        dot = all_sum(total)
        row = jnp.where(lane == ((NEAR * a + b) ^ (5 * here)), dot, row)
        row = jnp.where(lane == ((NEAR * b + a) ^ (5 * here)), dot, row)
    total = gain_parts[0]
    for part in range(1, WIDTH):
        total = total + gain_parts[part]
    total = total.astype(bf16).astype(f32)
    for part in range(WIDTH):
        shares_of[part] = total[part * GAIN_ROWS : (part + 1) * GAIN_ROWS]
    message = jnp.concatenate(
        [row, shares_of[place[0] % WIDTH], jnp.zeros((7 - GAIN_ROWS, LANES), f32)], axis=0
    )
    out[...] = jnp.broadcast_to(message[None], out.shape)


def near_dots(place, pieces, gain_parts):
    return pl.pallas_call(
        near_dots_kernel,
        out_shape=jax.ShapeDtypeStruct((NEAR * WIDTH, 8, LANES), f32),
        in_specs=[SMEM_SPEC] + [VMEM_SPEC] * (NEAR + 1),
        out_specs=VMEM_SPEC,
        scratch_shapes=[pltpu.VMEM((WIDTH, GAIN_ROWS, LANES), f32)],
        compiler_params=PARAMS,
        cost_estimate=pl.CostEstimate(
            flops=20 * pieces[0].size, bytes_accessed=8 * pieces[0].size, transcendentals=0
        ),
        name="near_dots",
    )(place, *pieces[::-1], gain_parts)


def near_shares(dots):
    low = (factor(dots[0][1], dots[0][0]), factor(dots[0][1], dots[1][1]))
    high = (factor(dots[2][3], dots[2][2]), factor(dots[2][3], dots[3][3]))
    low_sq = (
        low[0] * low[0] * dots[0][0]
        + 2.0 * (low[0] * low[1] * dots[0][1])
        + low[1] * low[1] * dots[1][1]
    )
    high_sq = (
        high[0] * high[0] * dots[2][2]
        + 2.0 * (high[0] * high[1] * dots[2][3])
        + high[1] * high[1] * dots[3][3]
    )
    cross = low[0] * (high[0] * dots[0][2] + high[1] * dots[0][3]) + low[1] * (
        high[0] * dots[1][2] + high[1] * dots[1][3]
    )
    of_low = factor(cross, low_sq)
    of_high = factor(cross, high_sq)
    square = (
        of_low * of_low * low_sq + 2.0 * (of_low * of_high * cross) + of_high * of_high * high_sq
    )
    return (of_low * low[0], of_low * low[1], of_high * high[0], of_high * high[1]), square


def bf16_parts(x):
    parts = []
    for _ in range(3):
        part = x.astype(bf16).astype(f32)
        parts.append(part)
        x = x - part
    return parts


def sent_at(far):
    return far % FAR_Z * (FAR // FAR_Z) + far // FAR_Z


def packed(dots):
    total = dots[0:8]
    for block in range(1, 4):
        total = total + pltpu.roll(dots[8 * block : 8 * block + 8], 32 * block, 1)
    return total


def unpacked(rows):
    lane = lax.broadcasted_iota(jnp.int32, (8, LANES), 1)
    blocks = []
    for block in range(4):
        moved = rows if block == 0 else pltpu.roll(rows, LANES - 32 * block, 1)
        blocks.append(jnp.where(lane < FAR, moved, 0.0))
    return jnp.concatenate(blocks, axis=0)


def near_merge_kernel(place, p3, p2, p1, p0, messages, out, gains):
    here = place[0] // WIDTH
    row = jnp.sum(messages[:, pl.ds(0, 1), :], axis=0)
    lane = lax.broadcasted_iota(jnp.int32, (1, LANES), 1)

    def entry(a, b):
        return jnp.sum(jnp.where(lane == NEAR * a + b, row, 0.0), axis=1, keepdims=True)

    shares, square = near_shares([[entry(a, b) if a <= b else None for b in range(NEAR)] for a in range(NEAR)])
    by_apart = []
    for apart in range(NEAR):
        share = shares[apart]
        for other in range(1, NEAR):
            share = jnp.where(here == other, shares[other ^ apart], share)
        by_apart.append(share)
    for far in range(FAR):
        rows = pl.ds(far * PIECE, PIECE)
        total = by_apart[0] * p0[rows, :].astype(f32)
        for share, ref in zip(by_apart[1:], (p1, p2, p3)):
            total = total + share * ref[rows, :].astype(f32)
        out[sent_at(far), pl.ds(0, PIECE // 2)] = total.astype(bf16).reshape(PIECE // 2, 2, LANES)

    for near in range(NEAR):
        for part in range(WIDTH):
            gains[near, pl.ds(part * GAIN_ROWS, GAIN_ROWS), :] = messages[
                near * WIDTH + part, pl.ds(1, GAIN_ROWS), :
            ]
    gain = [gains[near] for near in range(NEAR)]
    gain_shares, gain_square = near_shares(
        [[all_sum(gain[a] * gain[b]) if a <= b else None for b in range(NEAR)] for a in range(NEAR)]
    )
    merged = gain_shares[0] * gain[0]
    for near in range(1, NEAR):
        merged = merged + gain_shares[near] * gain[near]
    squares = jnp.zeros((1, LANES), f32)
    for at, part in enumerate(bf16_parts(square) + bf16_parts(gain_square)):
        squares = jnp.where(lane == at, part, squares)
    which = lax.broadcasted_iota(jnp.int32, (2, LANES), 0)
    for far in range(FAR):
        last = jnp.where(which == 0, merged[far : far + 1], squares)
        out[sent_at(far), PIECE // 2] = last.astype(bf16)


def near_merge(place, messages, pieces):
    return pl.pallas_call(
        near_merge_kernel,
        out_shape=jax.ShapeDtypeStruct((FAR, PIECE // 2 + 1, 2, LANES), bf16),
        in_specs=[SMEM_SPEC] + [VMEM_SPEC] * (1 + NEAR),
        out_specs=VMEM_SPEC,
        scratch_shapes=[pltpu.VMEM((NEAR, FAR, LANES), f32)],
        compiler_params=PARAMS,
        name="near_merge",
    )(place, *pieces[::-1], messages)


def far_dots_kernel(values, out, last, wide):
    height = PIECE + 8
    for far in range(FAR):
        at = far * height
        wide[pl.ds(at, PIECE), :] = piece_of(values, far)
        wide[pl.ds(at + PIECE, 2), :] = values[sent_at(far), PIECE // 2].astype(f32)
    columns = [
        wide[pl.ds(row, FAR, stride=height), :].astype(bf16) for row in range(PIECE + 1)
    ]
    for row in range(2):
        last[pl.ds(row * FAR, FAR), :] = wide[pl.ds(PIECE + row, FAR, stride=height), :]

    def dots(matrix):
        padded = jnp.concatenate(
            [matrix, jnp.zeros((LANES - FAR, matrix.shape[1]), bf16)], axis=0
        )
        return lax.dot_general(
            matrix, padded, (((1,), (1,)), ((), ())), preferred_element_type=f32
        )

    key_dots = dots(jnp.concatenate(columns[:PIECE], axis=1))
    gain_dots = dots(columns[PIECE]) * (1.0 / (NEAR * WIDTH))
    row = lax.broadcasted_iota(jnp.int32, key_dots.shape, 0)
    lane = lax.broadcasted_iota(jnp.int32, key_dots.shape, 1)
    both = jnp.where(row < lane, key_dots, jnp.where(row > lane, gain_dots, 0.0))
    out[...] = jnp.broadcast_to(packed(both)[None], out.shape)


def piece_of(values, far):
    return values[sent_at(far), pl.ds(0, PIECE // 2)].reshape(PIECE, LANES).astype(f32)


def far_dots(values):
    return pl.pallas_call(
        far_dots_kernel,
        out_shape=[
            jax.ShapeDtypeStruct((WIDTH, 8, LANES), f32),
            jax.ShapeDtypeStruct((2 * FAR, LANES), f32),
        ],
        in_specs=[VMEM_SPEC],
        out_specs=[VMEM_SPEC] * 2,
        scratch_shapes=[pltpu.VMEM((FAR * (PIECE + 8), LANES), f32)],
        compiler_params=PARAMS,
        name="far_dots",
    )(values)


def total_kernel(parts, out):
    total = parts[0]
    for part in range(1, parts.shape[0]):
        total = total + parts[part]
    out[...] = jnp.broadcast_to(total[None], out.shape)


def total_of(parts, copies):
    return pl.pallas_call(
        total_kernel,
        out_shape=jax.ShapeDtypeStruct((copies,) + parts.shape[1:], f32),
        in_specs=[VMEM_SPEC],
        out_specs=VMEM_SPEC,
        compiler_params=PARAMS,
        name="total_of",
    )(parts)


def far_shares(dots, squares):
    row = lax.broadcasted_iota(jnp.int32, dots.shape, 0)
    lane = lax.broadcasted_iota(jnp.int32, dots.shape, 1)
    share = jnp.ones((dots.shape[0], 1), f32)
    square_row = jnp.sum(jnp.where(row == lane, squares, 0.0), axis=0, keepdims=True)
    for level in range(5):
        same = (row >> level) == (lane >> level)
        pair = (row >> (level + 1)) == (lane >> (level + 1))
        own_part = jnp.sum(jnp.where(same, dots, 0.0), axis=0, keepdims=True)
        cross_part = jnp.sum(jnp.where(same, 0.0, jnp.where(pair, dots, 0.0)), axis=0, keepdims=True)
        own_part = 2.0 * own_part + square_row
        own_sq = jnp.sum(jnp.where(same, own_part, 0.0), axis=1, keepdims=True)
        cross = jnp.sum(jnp.where(pair, cross_part, 0.0), axis=1, keepdims=True)
        scale = factor(cross, own_sq)
        share = share * scale
        if level < 4:
            scale_row = jnp.sum(jnp.where(row == lane, scale, 0.0), axis=0, keepdims=True)
            dots = dots * scale * scale_row
            square_row = square_row * scale_row * scale_row
    return share


def far_merge_kernel(place, dots, values, last, key_out, gain_out):
    dots = unpacked(dots[...])
    row = lax.broadcasted_iota(jnp.int32, dots.shape, 0)
    lane = lax.broadcasted_iota(jnp.int32, dots.shape, 1)
    squares = last[pl.ds(FAR, FAR), :]
    key_square = jnp.sum(jnp.where(lane < 3, squares, 0.0), axis=1, keepdims=True)
    gain_square = jnp.sum(
        jnp.where(lane < 3, 0.0, jnp.where(lane < 6, squares, 0.0)), axis=1, keepdims=True
    )
    key_share = far_shares(jnp.where(row < lane, dots, 0.0), key_square)
    gain_share = far_shares(jnp.where(row > lane, dots, 0.0), gain_square)
    key_wide = jnp.broadcast_to(key_share, (FAR, LANES))
    totals = [jnp.zeros((PIECE, LANES), f32) for _ in range(2)]
    for far in range(FAR):
        totals[far % 2] = totals[far % 2] + key_wide[far : far + 1] * piece_of(values, far)
    key_out[...] = (totals[0] + totals[1]).astype(bf16)
    gain = jnp.sum(gain_share * last[pl.ds(0, FAR), :], axis=0, keepdims=True)
    wide = jnp.broadcast_to(gain, (8, LANES))
    moved = wide
    for near in range(1, NEAR):
        moved = jnp.where(place[0] // WIDTH == near, pltpu.roll(wide, LANES - PIECE * near, 1), moved)
    gain_out[...] = moved[0:1, :PIECE].astype(bf16)


def far_merge(place, dots, values, last):
    return pl.pallas_call(
        far_merge_kernel,
        out_shape=[
            jax.ShapeDtypeStruct((PIECE, LANES), bf16),
            jax.ShapeDtypeStruct((1, PIECE), bf16),
        ],
        in_specs=[SMEM_SPEC] + [VMEM_SPEC] * 3,
        out_specs=[VMEM_SPEC] * 2,
        compiler_params=PARAMS,
        name="far_merge",
    )(place, dots, values, last)


def paired(x, axis, apart):
    return lax.ppermute(x, axis, [(i, i ^ apart) for i in range(lax.axis_size(axis))])


def exchanged(x, axes):
    return lax.all_to_all(x, axes, 0, 0)


def body(hidden_states, key_cotangent, norm_gain, key_weight):
    place = lax.axis_index(("zl", "x", "core")).astype(jnp.int32).reshape(1)
    *pieces, inv_wide = local_grads(
        place, hidden_states, key_cotangent, norm_gain.reshape(FAR, LANES)
    )
    with jax.named_scope("near_exchange"):
        arrived = {apart: paired(pieces[apart], "zl", apart) for apart in (3, 2, 1)}
    with jax.named_scope("gain_parts"):
        gain = local_gains(hidden_states, key_cotangent, key_weight, inv_wide)
        gain_parts = lax.all_gather(gain, ("x", "core"))
    pieces = [pieces[0]] + [arrived[apart] for apart in range(1, NEAR)]
    messages = near_dots(place, pieces, gain_parts)
    with jax.named_scope("near_dots_sum"):
        messages = exchanged(messages, ("zl", "x", "core"))
    values = near_merge(place, messages, pieces)
    with jax.named_scope("far_exchange"):
        values = exchanged(values, ("zh", "y"))
    dots, last = far_dots(values)
    with jax.named_scope("far_dots_sum"):
        dots = total_of(exchanged(dots, ("x", "core")), 4 * NEAR)
        dots = total_of(exchanged(dots, ("y", "zl")), 1)
        dots = lax.psum(dots[0], "zh")
    merged_key, merged_gain = far_merge(place, dots, values, last)
    return (merged_key, merged_gain.reshape(PIECE))


def solution(mesh):
    split = Mesh(mesh.devices.reshape(4, FAR_Z, NEAR, 4, 2), ("y", "zh", "zl", "x", "core"))
    rows = ("y", "zh", "zl")
    columns = ("x", "core")
    return jax.shard_map(
        body,
        mesh=split,
        in_specs=(P(rows, None), P(rows, columns), P(), P(None, columns)),
        out_specs=(P(rows, columns), P(rows)),
        check_vma=False,
    )
```

```python
import jax
import jax.numpy as jnp
from jax import lax
from jax.experimental import pallas as pl
from jax.experimental.pallas import tpu as pltpu
from jax.sharding import Mesh
from jax.sharding import PartitionSpec as P

eps_norm = 1e-05
eps_merge = 1e-06

f32 = jnp.float32
bf16 = jnp.bfloat16

NEAR = 4
FAR = 32
FAR_Z = 8
WIDTH = 8
GAIN_ROWS = FAR // WIDTH
NEAR_PAIRS = [(a, b) for a in range(NEAR) for b in range(a, NEAR)]
PIECE = 32
LANES = 128
VMEM_SPEC = pl.BlockSpec(memory_space=pltpu.VMEM)
SMEM_SPEC = pl.BlockSpec(memory_space=pltpu.SMEM)
HBM_SPEC = pl.BlockSpec(memory_space=pltpu.HBM)
PARAMS = pltpu.CompilerParams(vmem_limit_bytes=16 << 20)


def in_hbm(x):
    return pltpu.with_memory_space_constraint(x, pltpu.HBM)


def factor(cross, own_sq):
    return 1.0 - cross / (2.0 * (jnp.maximum(own_sq, 0.0) + eps_merge))


def grads_kernel(
    place, hidden_hbm, cot_hbm, gain_hbm, p0, p1, p2, p3, inv_wide, hidden, cot, gain, pieces, sems
):
    tokens, width = hidden.shape
    parts = 8
    height = tokens // parts
    copies = [
        pltpu.make_async_copy(
            hidden_hbm.at[pl.ds(part * height, height)],
            hidden.at[pl.ds(part * height, height)],
            sems.at[part],
        )
        for part in range(parts)
    ]
    for at, (there, here) in enumerate(((cot_hbm, cot), (gain_hbm, gain))):
        copies.append(pltpu.make_async_copy(there, here, sems.at[parts + at]))
    for copy in copies:
        copy.start()
    blocks = width // LANES
    for part in range(parts):
        rows = pl.ds(part * height, height)
        copies[part].wait()
        totals = [jnp.zeros((height, LANES), f32) for _ in range(2)]
        for block in range(blocks):
            x = hidden[rows, pl.ds(block * LANES, LANES)].astype(f32)
            totals[block % 2] = totals[block % 2] + x * x
        inv_wide[rows, :] = totals[0] + totals[1]
    mean = jnp.sum(inv_wide[...], axis=1, keepdims=True) * (1.0 / width)
    inv_wide[...] = jnp.broadcast_to(lax.rsqrt(mean + eps_norm), inv_wide.shape)
    for copy in copies[parts:]:
        copy.wait()
    for chunk in range(blocks // 4):
        inv = inv_wide[...]
        inputs = []
        for block in range(4 * chunk, 4 * chunk + 4):
            x = hidden[:, pl.ds(block * LANES, LANES)].astype(f32) * inv
            inputs.append((x * gain[pl.ds(block, 1), :]).astype(bf16))
        grad = lax.dot_general(
            jnp.concatenate(inputs, axis=1),
            cot[...],
            (((0,), (0,)), ((), ())),
            preferred_element_type=f32,
        ).astype(bf16)
        for sub in range(4):
            for near in range(NEAR):
                at = sub * LANES + near * PIECE
                pieces[near, pl.ds((4 * chunk + sub) * PIECE, PIECE), :] = grad[at : at + PIECE]
    here = place[0] // WIDTH
    for apart, out in enumerate((p0, p1, p2, p3)):
        out[...] = pieces[here ^ apart]


def local_grads(place, hidden, cot, gain):
    piece = jax.ShapeDtypeStruct((FAR * PIECE, LANES), bf16)
    return pl.pallas_call(
        grads_kernel,
        out_shape=[piece] * NEAR + [jax.ShapeDtypeStruct((hidden.shape[0], LANES), f32)],
        in_specs=[SMEM_SPEC] + [HBM_SPEC] * 3,
        out_specs=[VMEM_SPEC] * (NEAR + 1),
        scratch_shapes=[
            pltpu.VMEM(hidden.shape, bf16),
            pltpu.VMEM(cot.shape, bf16),
            pltpu.VMEM(gain.shape, f32),
            pltpu.VMEM((NEAR, FAR * PIECE, LANES), bf16),
            pltpu.SemaphoreType.DMA((10,)),
        ],
        compiler_params=PARAMS,
        name="local_grads",
    )(place, in_hbm(hidden), in_hbm(cot), in_hbm(gain))


def gains_kernel(
    hidden_hbm, cot_hbm, weight_hbm, inv_wide, rows, hidden, cot, weight, sems
):
    blocks = hidden.shape[1] // LANES
    step = 4 * LANES
    copies = [pltpu.make_async_copy(cot_hbm, cot, sems.at[0])]
    for part in range(2):
        half = pl.ds(part * (blocks // 2) * LANES, (blocks // 2) * LANES)
        copies.append(
            pltpu.make_async_copy(weight_hbm.at[half], weight.at[half], sems.at[1 + part])
        )
        copies.append(
            pltpu.make_async_copy(
                hidden_hbm.at[:, half], hidden.at[:, half], sems.at[3 + part]
            )
        )
    for copy in copies:
        copy.start()
    for copy in copies[:3]:
        copy.wait()
    for chunk in range(blocks // 4):
        if chunk == blocks // 8:
            for copy in copies[3:]:
                copy.wait()
        back = lax.dot_general(
            cot[...],
            weight[pl.ds(chunk * step, step), :],
            (((1,), (1,)), ((), ())),
            preferred_element_type=f32,
        )
        inv = inv_wide[...]
        for sub in range(4):
            block = 4 * chunk + sub
            normed = hidden[:, pl.ds(block * LANES, LANES)].astype(f32) * inv
            rows[pl.ds(block, 1), :] = jnp.sum(
                back[:, sub * LANES : (sub + 1) * LANES] * normed, axis=0, keepdims=True
            )


def local_gains(hidden, cot, weight, inv_wide):
    return pl.pallas_call(
        gains_kernel,
        out_shape=jax.ShapeDtypeStruct((FAR, LANES), f32),
        in_specs=[HBM_SPEC] * 3 + [VMEM_SPEC],
        out_specs=VMEM_SPEC,
        scratch_shapes=[
            pltpu.VMEM(hidden.shape, bf16),
            pltpu.VMEM(cot.shape, bf16),
            pltpu.VMEM(weight.shape, bf16),
            pltpu.SemaphoreType.DMA((5,)),
        ],
        compiler_params=PARAMS,
        cost_estimate=pl.CostEstimate(
            flops=2 * hidden.shape[0] * weight.size,
            bytes_accessed=2 * (hidden.size + weight.size),
            transcendentals=0,
        ),
        name="local_gains",
    )(in_hbm(hidden), in_hbm(cot), in_hbm(weight), inv_wide)


def all_sum(x):
    return jnp.sum(jnp.sum(x, axis=0, keepdims=True), axis=1, keepdims=True)


def near_dots_kernel(place, p3, p2, p1, p0, gain_parts, out, shares_of):
    refs = (p0, p1, p2, p3)
    pairs = NEAR_PAIRS
    rows = 64

    def add(step, totals):
        values = [ref[pl.ds(step * rows, rows), :].astype(f32) for ref in refs]
        return tuple(
            total + jnp.sum((values[a] * values[b]).reshape(rows // 8, 8, LANES), axis=0)
            for total, (a, b) in zip(totals, pairs)
        )

    totals = lax.fori_loop(
        0, p0.shape[0] // rows, add, tuple(jnp.zeros((8, LANES), f32) for _ in pairs)
    )
    here = place[0] // WIDTH
    lane = lax.broadcasted_iota(jnp.int32, (1, LANES), 1)
    row = jnp.zeros((1, LANES), f32)
    for total, (a, b) in zip(totals, pairs):
        dot = all_sum(total)
        row = jnp.where(lane == ((NEAR * a + b) ^ (5 * here)), dot, row)
        row = jnp.where(lane == ((NEAR * b + a) ^ (5 * here)), dot, row)
    total = gain_parts[0]
    for part in range(1, gain_parts.shape[0]):
        total = total + gain_parts[part]
    total = total.astype(bf16).astype(f32)
    for part in range(WIDTH):
        shares_of[part] = total[part * GAIN_ROWS : (part + 1) * GAIN_ROWS]
    message = jnp.concatenate(
        [row, shares_of[place[0] % WIDTH], jnp.zeros((7 - GAIN_ROWS, LANES), f32)], axis=0
    )
    out[...] = jnp.broadcast_to(message[None], out.shape)


def near_dots(place, pieces, gain_parts):
    return pl.pallas_call(
        near_dots_kernel,
        out_shape=jax.ShapeDtypeStruct((NEAR * WIDTH, 8, LANES), f32),
        in_specs=[SMEM_SPEC] + [VMEM_SPEC] * (NEAR + 1),
        out_specs=VMEM_SPEC,
        scratch_shapes=[pltpu.VMEM((WIDTH, GAIN_ROWS, LANES), f32)],
        compiler_params=PARAMS,
        cost_estimate=pl.CostEstimate(
            flops=20 * pieces[0].size, bytes_accessed=8 * pieces[0].size, transcendentals=0
        ),
        name="near_dots",
    )(place, *pieces[::-1], gain_parts)


def near_shares(dots):
    low = (factor(dots[0][1], dots[0][0]), factor(dots[0][1], dots[1][1]))
    high = (factor(dots[2][3], dots[2][2]), factor(dots[2][3], dots[3][3]))
    low_sq = (
        low[0] * low[0] * dots[0][0]
        + 2.0 * (low[0] * low[1] * dots[0][1])
        + low[1] * low[1] * dots[1][1]
    )
    high_sq = (
        high[0] * high[0] * dots[2][2]
        + 2.0 * (high[0] * high[1] * dots[2][3])
        + high[1] * high[1] * dots[3][3]
    )
    cross = low[0] * (high[0] * dots[0][2] + high[1] * dots[0][3]) + low[1] * (
        high[0] * dots[1][2] + high[1] * dots[1][3]
    )
    of_low = factor(cross, low_sq)
    of_high = factor(cross, high_sq)
    square = (
        of_low * of_low * low_sq + 2.0 * (of_low * of_high * cross) + of_high * of_high * high_sq
    )
    return (of_low * low[0], of_low * low[1], of_high * high[0], of_high * high[1]), square


def bf16_parts(x):
    parts = []
    for _ in range(3):
        part = x.astype(bf16).astype(f32)
        parts.append(part)
        x = x - part
    return parts


def sent_at(far):
    return far % FAR_Z * (FAR // FAR_Z) + far // FAR_Z


def packed(dots):
    total = dots[0:8]
    for block in range(1, 4):
        total = total + pltpu.roll(dots[8 * block : 8 * block + 8], 32 * block, 1)
    return total


def unpacked(rows):
    lane = lax.broadcasted_iota(jnp.int32, (8, LANES), 1)
    blocks = []
    for block in range(4):
        moved = rows if block == 0 else pltpu.roll(rows, LANES - 32 * block, 1)
        blocks.append(jnp.where(lane < FAR, moved, 0.0))
    return jnp.concatenate(blocks, axis=0)


def near_merge_kernel(place, p3, p2, p1, p0, messages, out, gains):
    here = place[0] // WIDTH
    row = jnp.sum(messages[:, pl.ds(0, 1), :], axis=0)
    lane = lax.broadcasted_iota(jnp.int32, (1, LANES), 1)

    def entry(a, b):
        return jnp.sum(jnp.where(lane == NEAR * a + b, row, 0.0), axis=1, keepdims=True)

    shares, square = near_shares([[entry(a, b) if a <= b else None for b in range(NEAR)] for a in range(NEAR)])
    by_apart = []
    for apart in range(NEAR):
        share = shares[apart]
        for other in range(1, NEAR):
            share = jnp.where(here == other, shares[other ^ apart], share)
        by_apart.append(share)
    for far in range(FAR):
        rows = pl.ds(far * PIECE, PIECE)
        total = by_apart[0] * p0[rows, :].astype(f32)
        for share, ref in zip(by_apart[1:], (p1, p2, p3)):
            total = total + share * ref[rows, :].astype(f32)
        out[sent_at(far), pl.ds(0, PIECE // 2)] = total.astype(bf16).reshape(PIECE // 2, 2, LANES)

    for near in range(NEAR):
        for part in range(WIDTH):
            gains[near, pl.ds(part * GAIN_ROWS, GAIN_ROWS), :] = messages[
                near * WIDTH + part, pl.ds(1, GAIN_ROWS), :
            ]
    gain = [gains[near] for near in range(NEAR)]
    gain_shares, gain_square = near_shares(
        [[all_sum(gain[a] * gain[b]) if a <= b else None for b in range(NEAR)] for a in range(NEAR)]
    )
    merged = gain_shares[0] * gain[0]
    for near in range(1, NEAR):
        merged = merged + gain_shares[near] * gain[near]
    squares = jnp.zeros((1, LANES), f32)
    for at, part in enumerate(bf16_parts(square) + bf16_parts(gain_square)):
        squares = jnp.where(lane == at, part, squares)
    which = lax.broadcasted_iota(jnp.int32, (2, LANES), 0)
    for far in range(FAR):
        last = jnp.where(which == 0, merged[far : far + 1], squares)
        out[sent_at(far), PIECE // 2] = last.astype(bf16)


def near_merge(place, messages, pieces):
    return pl.pallas_call(
        near_merge_kernel,
        out_shape=jax.ShapeDtypeStruct((FAR, PIECE // 2 + 1, 2, LANES), bf16),
        in_specs=[SMEM_SPEC] + [VMEM_SPEC] * (1 + NEAR),
        out_specs=VMEM_SPEC,
        scratch_shapes=[pltpu.VMEM((NEAR, FAR, LANES), f32)],
        compiler_params=PARAMS,
        name="near_merge",
    )(place, *pieces[::-1], messages)


def far_dots_kernel(values, out, last, wide):
    height = PIECE + 8
    for far in range(FAR):
        at = far * height
        wide[pl.ds(at, PIECE), :] = piece_of(values, far)
        wide[pl.ds(at + PIECE, 2), :] = values[sent_at(far), PIECE // 2].astype(f32)
    columns = [
        wide[pl.ds(row, FAR, stride=height), :].astype(bf16) for row in range(PIECE + 1)
    ]
    for row in range(2):
        last[pl.ds(row * FAR, FAR), :] = wide[pl.ds(PIECE + row, FAR, stride=height), :]

    def dots(matrix):
        padded = jnp.concatenate(
            [matrix, jnp.zeros((LANES - FAR, matrix.shape[1]), bf16)], axis=0
        )
        return lax.dot_general(
            matrix, padded, (((1,), (1,)), ((), ())), preferred_element_type=f32
        )

    key_dots = dots(jnp.concatenate(columns[:PIECE], axis=1))
    gain_dots = dots(columns[PIECE]) * (1.0 / (NEAR * WIDTH))
    row = lax.broadcasted_iota(jnp.int32, key_dots.shape, 0)
    lane = lax.broadcasted_iota(jnp.int32, key_dots.shape, 1)
    both = jnp.where(row < lane, key_dots, jnp.where(row > lane, gain_dots, 0.0))
    out[...] = jnp.broadcast_to(packed(both)[None], out.shape)


def piece_of(values, far):
    return values[sent_at(far), pl.ds(0, PIECE // 2)].reshape(PIECE, LANES).astype(f32)


def far_dots(values):
    return pl.pallas_call(
        far_dots_kernel,
        out_shape=[
            jax.ShapeDtypeStruct((WIDTH, 8, LANES), f32),
            jax.ShapeDtypeStruct((2 * FAR, LANES), f32),
        ],
        in_specs=[VMEM_SPEC],
        out_specs=[VMEM_SPEC] * 2,
        scratch_shapes=[pltpu.VMEM((FAR * (PIECE + 8), LANES), f32)],
        compiler_params=PARAMS,
        name="far_dots",
    )(values)


def total_kernel(parts, out):
    total = parts[0]
    for part in range(1, parts.shape[0]):
        total = total + parts[part]
    out[...] = jnp.broadcast_to(total[None], out.shape)


def total_of(parts, copies):
    return pl.pallas_call(
        total_kernel,
        out_shape=jax.ShapeDtypeStruct((copies,) + parts.shape[1:], f32),
        in_specs=[VMEM_SPEC],
        out_specs=VMEM_SPEC,
        compiler_params=PARAMS,
        name="total_of",
    )(parts)


def far_shares(dots, squares):
    row = lax.broadcasted_iota(jnp.int32, dots.shape, 0)
    lane = lax.broadcasted_iota(jnp.int32, dots.shape, 1)
    share = jnp.ones((dots.shape[0], 1), f32)
    square_row = jnp.sum(jnp.where(row == lane, squares, 0.0), axis=0, keepdims=True)
    for level in range(5):
        same = (row >> level) == (lane >> level)
        pair = (row >> (level + 1)) == (lane >> (level + 1))
        own_part = jnp.sum(jnp.where(same, dots, 0.0), axis=0, keepdims=True)
        cross_part = jnp.sum(jnp.where(same, 0.0, jnp.where(pair, dots, 0.0)), axis=0, keepdims=True)
        own_part = 2.0 * own_part + square_row
        own_sq = jnp.sum(jnp.where(same, own_part, 0.0), axis=1, keepdims=True)
        cross = jnp.sum(jnp.where(pair, cross_part, 0.0), axis=1, keepdims=True)
        scale = factor(cross, own_sq)
        share = share * scale
        if level < 4:
            scale_row = jnp.sum(jnp.where(row == lane, scale, 0.0), axis=0, keepdims=True)
            dots = dots * scale * scale_row
            square_row = square_row * scale_row * scale_row
    return share


def far_merge_kernel(place, dots, values, last, key_out, gain_out):
    dots = unpacked(dots[...])
    row = lax.broadcasted_iota(jnp.int32, dots.shape, 0)
    lane = lax.broadcasted_iota(jnp.int32, dots.shape, 1)
    squares = last[pl.ds(FAR, FAR), :]
    key_square = jnp.sum(jnp.where(lane < 3, squares, 0.0), axis=1, keepdims=True)
    gain_square = jnp.sum(
        jnp.where(lane < 3, 0.0, jnp.where(lane < 6, squares, 0.0)), axis=1, keepdims=True
    )
    key_share = far_shares(jnp.where(row < lane, dots, 0.0), key_square)
    gain_share = far_shares(jnp.where(row > lane, dots, 0.0), gain_square)
    key_wide = jnp.broadcast_to(key_share, (FAR, LANES))
    totals = [jnp.zeros((PIECE, LANES), f32) for _ in range(2)]
    for far in range(FAR):
        totals[far % 2] = totals[far % 2] + key_wide[far : far + 1] * piece_of(values, far)
    key_out[...] = (totals[0] + totals[1]).astype(bf16)
    gain = jnp.sum(gain_share * last[pl.ds(0, FAR), :], axis=0, keepdims=True)
    wide = jnp.broadcast_to(gain, (8, LANES))
    moved = wide
    for near in range(1, NEAR):
        moved = jnp.where(place[0] // WIDTH == near, pltpu.roll(wide, LANES - PIECE * near, 1), moved)
    gain_out[...] = moved[0:1, :PIECE].astype(bf16)


def far_merge(place, dots, values, last):
    return pl.pallas_call(
        far_merge_kernel,
        out_shape=[
            jax.ShapeDtypeStruct((PIECE, LANES), bf16),
            jax.ShapeDtypeStruct((1, PIECE), bf16),
        ],
        in_specs=[SMEM_SPEC] + [VMEM_SPEC] * 3,
        out_specs=[VMEM_SPEC] * 2,
        compiler_params=PARAMS,
        name="far_merge",
    )(place, dots, values, last)


def paired(x, axis, apart):
    return lax.ppermute(x, axis, [(i, i ^ apart) for i in range(lax.axis_size(axis))])


def exchanged(x, axes):
    return lax.all_to_all(x, axes, 0, 0)


def body(hidden_states, key_cotangent, norm_gain, key_weight):
    place = lax.axis_index(("zl", "x", "core")).astype(jnp.int32).reshape(1)
    *pieces, inv_wide = local_grads(
        place, hidden_states, key_cotangent, norm_gain.reshape(FAR, LANES)
    )
    with jax.named_scope("near_exchange"):
        arrived = {apart: paired(pieces[apart], "zl", apart) for apart in (3, 2, 1)}
    with jax.named_scope("gain_parts"):
        gain = local_gains(hidden_states, key_cotangent, key_weight, inv_wide)
        gain_parts = lax.all_gather(lax.all_gather(gain, "core"), "x")
        gain_parts = gain_parts.reshape(WIDTH, FAR, LANES)
    pieces = [pieces[0]] + [arrived[apart] for apart in range(1, NEAR)]
    messages = near_dots(place, pieces, gain_parts)
    with jax.named_scope("near_dots_sum"):
        messages = exchanged(messages, ("zl", "x", "core"))
    values = near_merge(place, messages, pieces)
    with jax.named_scope("far_exchange"):
        values = exchanged(values, ("zh", "y"))
    dots, last = far_dots(values)
    with jax.named_scope("far_dots_sum"):
        dots = total_of(exchanged(dots, ("x", "core")), 4 * NEAR)
        dots = total_of(exchanged(dots, ("y", "zl")), 1)
        dots = lax.psum(dots[0], "zh")
    merged_key, merged_gain = far_merge(place, dots, values, last)
    return (merged_key, merged_gain.reshape(PIECE))


def solution(mesh):
    split = Mesh(mesh.devices.reshape(4, FAR_Z, NEAR, 4, 2), ("y", "zh", "zl", "x", "core"))
    rows = ("y", "zh", "zl")
    columns = ("x", "core")
    return jax.shard_map(
        body,
        mesh=split,
        in_specs=(P(rows, None), P(rows, columns), P(), P(None, columns)),
        out_specs=(P(rows, columns), P(rows)),
        check_vma=False,
    )
```

```python
import jax
import jax.numpy as jnp
from jax import lax
from jax.experimental import pallas as pl
from jax.experimental.pallas import tpu as pltpu
from jax.sharding import Mesh
from jax.sharding import PartitionSpec as P

eps_norm = 1e-05
eps_merge = 1e-06

f32 = jnp.float32
bf16 = jnp.bfloat16

NEAR = 4
FAR = 32
FAR_Z = 8
WIDTH = 8
GAIN_ROWS = FAR // WIDTH
NEAR_PAIRS = [(a, b) for a in range(NEAR) for b in range(a, NEAR)]
PIECE = 32
LANES = 128
VMEM_SPEC = pl.BlockSpec(memory_space=pltpu.VMEM)
SMEM_SPEC = pl.BlockSpec(memory_space=pltpu.SMEM)
HBM_SPEC = pl.BlockSpec(memory_space=pltpu.HBM)
PARAMS = pltpu.CompilerParams(vmem_limit_bytes=16 << 20)


def in_hbm(x):
    return pltpu.with_memory_space_constraint(x, pltpu.HBM)


def factor(cross, own_sq):
    return 1.0 - cross / (2.0 * (jnp.maximum(own_sq, 0.0) + eps_merge))


def within(cross, low_sq, high_sq):
    most = jnp.sqrt(jnp.maximum(low_sq, 0.0)) * jnp.sqrt(jnp.maximum(high_sq, 0.0))
    return jnp.clip(cross, -most, most)


def grads_kernel(
    place, hidden_hbm, cot_hbm, gain_hbm, p0, p1, p2, p3, inv_wide, hidden, cot, gain, pieces, sems
):
    tokens, width = hidden.shape
    parts = 8
    height = tokens // parts
    copies = [
        pltpu.make_async_copy(
            hidden_hbm.at[pl.ds(part * height, height)],
            hidden.at[pl.ds(part * height, height)],
            sems.at[part],
        )
        for part in range(parts)
    ]
    for at, (there, here) in enumerate(((cot_hbm, cot), (gain_hbm, gain))):
        copies.append(pltpu.make_async_copy(there, here, sems.at[parts + at]))
    for copy in copies:
        copy.start()
    blocks = width // LANES
    for part in range(parts):
        rows = pl.ds(part * height, height)
        copies[part].wait()
        totals = [jnp.zeros((height, LANES), f32) for _ in range(2)]
        for block in range(blocks):
            x = hidden[rows, pl.ds(block * LANES, LANES)].astype(f32)
            totals[block % 2] = totals[block % 2] + x * x
        inv_wide[rows, :] = totals[0] + totals[1]
    mean = jnp.sum(inv_wide[...], axis=1, keepdims=True) * (1.0 / width)
    inv_wide[...] = jnp.broadcast_to(lax.rsqrt(mean + eps_norm), inv_wide.shape)
    for copy in copies[parts:]:
        copy.wait()
    for chunk in range(blocks // 4):
        inv = inv_wide[...]
        inputs = []
        for block in range(4 * chunk, 4 * chunk + 4):
            x = hidden[:, pl.ds(block * LANES, LANES)].astype(f32) * inv
            inputs.append((x * gain[pl.ds(block, 1), :]).astype(bf16))
        grad = lax.dot_general(
            jnp.concatenate(inputs, axis=1),
            cot[...],
            (((0,), (0,)), ((), ())),
            preferred_element_type=f32,
        ).astype(bf16)
        for sub in range(4):
            for near in range(NEAR):
                at = sub * LANES + near * PIECE
                pieces[near, pl.ds((4 * chunk + sub) * PIECE, PIECE), :] = grad[at : at + PIECE]
    here = place[0] // WIDTH
    for apart, out in enumerate((p0, p1, p2, p3)):
        out[...] = pieces[here ^ apart]


def local_grads(place, hidden, cot, gain):
    piece = jax.ShapeDtypeStruct((FAR * PIECE, LANES), bf16)
    return pl.pallas_call(
        grads_kernel,
        out_shape=[piece] * NEAR + [jax.ShapeDtypeStruct((hidden.shape[0], LANES), f32)],
        in_specs=[SMEM_SPEC] + [HBM_SPEC] * 3,
        out_specs=[VMEM_SPEC] * (NEAR + 1),
        scratch_shapes=[
            pltpu.VMEM(hidden.shape, bf16),
            pltpu.VMEM(cot.shape, bf16),
            pltpu.VMEM(gain.shape, f32),
            pltpu.VMEM((NEAR, FAR * PIECE, LANES), bf16),
            pltpu.SemaphoreType.DMA((10,)),
        ],
        compiler_params=PARAMS,
        name="local_grads",
    )(place, in_hbm(hidden), in_hbm(cot), in_hbm(gain))


def gains_kernel(
    hidden_hbm, cot_hbm, weight_hbm, inv_wide, rows, hidden, cot, weight, sems
):
    blocks = hidden.shape[1] // LANES
    step = 4 * LANES
    copies = [pltpu.make_async_copy(cot_hbm, cot, sems.at[0])]
    for part in range(2):
        half = pl.ds(part * (blocks // 2) * LANES, (blocks // 2) * LANES)
        copies.append(
            pltpu.make_async_copy(weight_hbm.at[half], weight.at[half], sems.at[1 + part])
        )
        copies.append(
            pltpu.make_async_copy(
                hidden_hbm.at[:, half], hidden.at[:, half], sems.at[3 + part]
            )
        )
    for copy in copies:
        copy.start()
    for copy in copies[:3]:
        copy.wait()
    for chunk in range(blocks // 4):
        if chunk == blocks // 8:
            for copy in copies[3:]:
                copy.wait()
        back = lax.dot_general(
            cot[...],
            weight[pl.ds(chunk * step, step), :],
            (((1,), (1,)), ((), ())),
            preferred_element_type=f32,
        )
        inv = inv_wide[...]
        for sub in range(4):
            block = 4 * chunk + sub
            normed = hidden[:, pl.ds(block * LANES, LANES)].astype(f32) * inv
            rows[pl.ds(block, 1), :] = jnp.sum(
                back[:, sub * LANES : (sub + 1) * LANES] * normed, axis=0, keepdims=True
            )


def local_gains(hidden, cot, weight, inv_wide):
    return pl.pallas_call(
        gains_kernel,
        out_shape=jax.ShapeDtypeStruct((FAR, LANES), f32),
        in_specs=[HBM_SPEC] * 3 + [VMEM_SPEC],
        out_specs=VMEM_SPEC,
        scratch_shapes=[
            pltpu.VMEM(hidden.shape, bf16),
            pltpu.VMEM(cot.shape, bf16),
            pltpu.VMEM(weight.shape, bf16),
            pltpu.SemaphoreType.DMA((5,)),
        ],
        compiler_params=PARAMS,
        cost_estimate=pl.CostEstimate(
            flops=2 * hidden.shape[0] * weight.size,
            bytes_accessed=2 * (hidden.size + weight.size),
            transcendentals=0,
        ),
        name="local_gains",
    )(in_hbm(hidden), in_hbm(cot), in_hbm(weight), inv_wide)


def all_sum(x):
    return jnp.sum(jnp.sum(x, axis=0, keepdims=True), axis=1, keepdims=True)


def near_dots_kernel(place, p3, p2, p1, p0, gain_parts, out, shares_of):
    refs = (p0, p1, p2, p3)
    pairs = NEAR_PAIRS
    rows = 64

    def add(step, totals):
        values = [ref[pl.ds(step * rows, rows), :].astype(f32) for ref in refs]
        return tuple(
            total + jnp.sum((values[a] * values[b]).reshape(rows // 8, 8, LANES), axis=0)
            for total, (a, b) in zip(totals, pairs)
        )

    totals = lax.fori_loop(
        0, p0.shape[0] // rows, add, tuple(jnp.zeros((8, LANES), f32) for _ in pairs)
    )
    here = place[0] // WIDTH
    lane = lax.broadcasted_iota(jnp.int32, (1, LANES), 1)
    row = jnp.zeros((1, LANES), f32)
    for total, (a, b) in zip(totals, pairs):
        dot = all_sum(total)
        row = jnp.where(lane == ((NEAR * a + b) ^ (5 * here)), dot, row)
        row = jnp.where(lane == ((NEAR * b + a) ^ (5 * here)), dot, row)
    total = gain_parts[0]
    for part in range(1, gain_parts.shape[0]):
        total = total + gain_parts[part]
    total = total.astype(bf16).astype(f32)
    for part in range(WIDTH):
        shares_of[part] = total[part * GAIN_ROWS : (part + 1) * GAIN_ROWS]
    message = jnp.concatenate(
        [row, shares_of[place[0] % WIDTH], jnp.zeros((7 - GAIN_ROWS, LANES), f32)], axis=0
    )
    out[...] = jnp.broadcast_to(message[None], out.shape)


def near_dots(place, pieces, gain_parts):
    return pl.pallas_call(
        near_dots_kernel,
        out_shape=jax.ShapeDtypeStruct((NEAR * WIDTH, 8, LANES), f32),
        in_specs=[SMEM_SPEC] + [VMEM_SPEC] * (NEAR + 1),
        out_specs=VMEM_SPEC,
        scratch_shapes=[pltpu.VMEM((WIDTH, GAIN_ROWS, LANES), f32)],
        compiler_params=PARAMS,
        cost_estimate=pl.CostEstimate(
            flops=20 * pieces[0].size, bytes_accessed=8 * pieces[0].size, transcendentals=0
        ),
        name="near_dots",
    )(place, *pieces[::-1], gain_parts)


def near_shares(dots):
    low = (factor(dots[0][1], dots[0][0]), factor(dots[0][1], dots[1][1]))
    high = (factor(dots[2][3], dots[2][2]), factor(dots[2][3], dots[3][3]))
    low_sq = (
        low[0] * low[0] * dots[0][0]
        + 2.0 * (low[0] * low[1] * dots[0][1])
        + low[1] * low[1] * dots[1][1]
    )
    high_sq = (
        high[0] * high[0] * dots[2][2]
        + 2.0 * (high[0] * high[1] * dots[2][3])
        + high[1] * high[1] * dots[3][3]
    )
    cross = low[0] * (high[0] * dots[0][2] + high[1] * dots[0][3]) + low[1] * (
        high[0] * dots[1][2] + high[1] * dots[1][3]
    )
    cross = within(cross, low_sq, high_sq)
    of_low = factor(cross, low_sq)
    of_high = factor(cross, high_sq)
    square = (
        of_low * of_low * low_sq + 2.0 * (of_low * of_high * cross) + of_high * of_high * high_sq
    )
    return (of_low * low[0], of_low * low[1], of_high * high[0], of_high * high[1]), square


def bf16_parts(x):
    parts = []
    for _ in range(3):
        part = x.astype(bf16).astype(f32)
        parts.append(part)
        x = x - part
    return parts


def sent_at(far):
    return far % FAR_Z * (FAR // FAR_Z) + far // FAR_Z


def packed(dots):
    total = dots[0:8]
    for block in range(1, 4):
        total = total + pltpu.roll(dots[8 * block : 8 * block + 8], 32 * block, 1)
    return total


def unpacked(rows):
    lane = lax.broadcasted_iota(jnp.int32, (8, LANES), 1)
    blocks = []
    for block in range(4):
        moved = rows if block == 0 else pltpu.roll(rows, LANES - 32 * block, 1)
        blocks.append(jnp.where(lane < FAR, moved, 0.0))
    return jnp.concatenate(blocks, axis=0)


def near_merge_kernel(place, p3, p2, p1, p0, messages, out, gains):
    here = place[0] // WIDTH
    row = jnp.sum(messages[:, pl.ds(0, 1), :], axis=0)
    lane = lax.broadcasted_iota(jnp.int32, (1, LANES), 1)

    def entry(a, b):
        return jnp.sum(jnp.where(lane == NEAR * a + b, row, 0.0), axis=1, keepdims=True)

    shares, square = near_shares([[entry(a, b) if a <= b else None for b in range(NEAR)] for a in range(NEAR)])
    by_apart = []
    for apart in range(NEAR):
        share = shares[apart]
        for other in range(1, NEAR):
            share = jnp.where(here == other, shares[other ^ apart], share)
        by_apart.append(share)
    for far in range(FAR):
        rows = pl.ds(far * PIECE, PIECE)
        total = by_apart[0] * p0[rows, :].astype(f32)
        for share, ref in zip(by_apart[1:], (p1, p2, p3)):
            total = total + share * ref[rows, :].astype(f32)
        out[sent_at(far), pl.ds(0, PIECE // 2)] = total.astype(bf16).reshape(PIECE // 2, 2, LANES)

    for near in range(NEAR):
        for part in range(WIDTH):
            gains[near, pl.ds(part * GAIN_ROWS, GAIN_ROWS), :] = messages[
                near * WIDTH + part, pl.ds(1, GAIN_ROWS), :
            ]
    gain = [gains[near] for near in range(NEAR)]
    gain_shares, gain_square = near_shares(
        [[all_sum(gain[a] * gain[b]) if a <= b else None for b in range(NEAR)] for a in range(NEAR)]
    )
    merged = gain_shares[0] * gain[0]
    for near in range(1, NEAR):
        merged = merged + gain_shares[near] * gain[near]
    squares = jnp.zeros((1, LANES), f32)
    for at, part in enumerate(bf16_parts(square) + bf16_parts(gain_square)):
        squares = jnp.where(lane == at, part, squares)
    which = lax.broadcasted_iota(jnp.int32, (2, LANES), 0)
    for far in range(FAR):
        last = jnp.where(which == 0, merged[far : far + 1], squares)
        out[sent_at(far), PIECE // 2] = last.astype(bf16)


def near_merge(place, messages, pieces):
    return pl.pallas_call(
        near_merge_kernel,
        out_shape=jax.ShapeDtypeStruct((FAR, PIECE // 2 + 1, 2, LANES), bf16),
        in_specs=[SMEM_SPEC] + [VMEM_SPEC] * (1 + NEAR),
        out_specs=VMEM_SPEC,
        scratch_shapes=[pltpu.VMEM((NEAR, FAR, LANES), f32)],
        compiler_params=PARAMS,
        name="near_merge",
    )(place, *pieces[::-1], messages)


def far_dots_kernel(values, out, last, wide):
    height = PIECE + 8
    for far in range(FAR):
        at = far * height
        wide[pl.ds(at, PIECE), :] = piece_of(values, far)
        wide[pl.ds(at + PIECE, 2), :] = values[sent_at(far), PIECE // 2].astype(f32)
    columns = [
        wide[pl.ds(row, FAR, stride=height), :].astype(bf16) for row in range(PIECE + 1)
    ]
    for row in range(2):
        last[pl.ds(row * FAR, FAR), :] = wide[pl.ds(PIECE + row, FAR, stride=height), :]

    def dots(matrix):
        padded = jnp.concatenate(
            [matrix, jnp.zeros((LANES - FAR, matrix.shape[1]), bf16)], axis=0
        )
        return lax.dot_general(
            matrix, padded, (((1,), (1,)), ((), ())), preferred_element_type=f32
        )

    key_dots = dots(jnp.concatenate(columns[:PIECE], axis=1))
    gain_dots = dots(columns[PIECE]) * (1.0 / (NEAR * WIDTH))
    row = lax.broadcasted_iota(jnp.int32, key_dots.shape, 0)
    lane = lax.broadcasted_iota(jnp.int32, key_dots.shape, 1)
    both = jnp.where(row < lane, key_dots, jnp.where(row > lane, gain_dots, 0.0))
    out[...] = jnp.broadcast_to(packed(both)[None], out.shape)


def piece_of(values, far):
    return values[sent_at(far), pl.ds(0, PIECE // 2)].reshape(PIECE, LANES).astype(f32)


def far_dots(values):
    return pl.pallas_call(
        far_dots_kernel,
        out_shape=[
            jax.ShapeDtypeStruct((WIDTH, 8, LANES), f32),
            jax.ShapeDtypeStruct((2 * FAR, LANES), f32),
        ],
        in_specs=[VMEM_SPEC],
        out_specs=[VMEM_SPEC] * 2,
        scratch_shapes=[pltpu.VMEM((FAR * (PIECE + 8), LANES), f32)],
        compiler_params=PARAMS,
        name="far_dots",
    )(values)


def total_kernel(parts, out):
    total = parts[0]
    for part in range(1, parts.shape[0]):
        total = total + parts[part]
    out[...] = jnp.broadcast_to(total[None], out.shape)


def total_of(parts, copies):
    return pl.pallas_call(
        total_kernel,
        out_shape=jax.ShapeDtypeStruct((copies,) + parts.shape[1:], f32),
        in_specs=[VMEM_SPEC],
        out_specs=VMEM_SPEC,
        compiler_params=PARAMS,
        name="total_of",
    )(parts)


def far_shares(dots, squares):
    row = lax.broadcasted_iota(jnp.int32, dots.shape, 0)
    lane = lax.broadcasted_iota(jnp.int32, dots.shape, 1)
    share = jnp.ones((dots.shape[0], 1), f32)
    square_row = jnp.sum(jnp.where(row == lane, squares, 0.0), axis=0, keepdims=True)
    for level in range(5):
        same = (row >> level) == (lane >> level)
        pair = (row >> (level + 1)) == (lane >> (level + 1))
        own_part = jnp.sum(jnp.where(same, dots, 0.0), axis=0, keepdims=True)
        cross_part = jnp.sum(jnp.where(same, 0.0, jnp.where(pair, dots, 0.0)), axis=0, keepdims=True)
        own_part = 2.0 * own_part + square_row
        own_sq = jnp.sum(jnp.where(same, own_part, 0.0), axis=1, keepdims=True)
        cross = jnp.sum(jnp.where(pair, cross_part, 0.0), axis=1, keepdims=True)
        other_sq = jnp.sum(
            jnp.where(same, 0.0, jnp.where(pair, own_part, 0.0)), axis=1, keepdims=True
        )
        scale = factor(within(cross, own_sq, other_sq), own_sq)
        share = share * scale
        if level < 4:
            scale_row = jnp.sum(jnp.where(row == lane, scale, 0.0), axis=0, keepdims=True)
            dots = dots * scale * scale_row
            square_row = square_row * scale_row * scale_row
    return share


def far_merge_kernel(place, dots, values, last, key_out, gain_out):
    dots = unpacked(dots[...])
    row = lax.broadcasted_iota(jnp.int32, dots.shape, 0)
    lane = lax.broadcasted_iota(jnp.int32, dots.shape, 1)
    squares = last[pl.ds(FAR, FAR), :]
    key_square = jnp.sum(jnp.where(lane < 3, squares, 0.0), axis=1, keepdims=True)
    gain_square = jnp.sum(
        jnp.where(lane < 3, 0.0, jnp.where(lane < 6, squares, 0.0)), axis=1, keepdims=True
    )
    key_share = far_shares(jnp.where(row < lane, dots, 0.0), key_square)
    gain_share = far_shares(jnp.where(row > lane, dots, 0.0), gain_square)
    key_wide = jnp.broadcast_to(key_share, (FAR, LANES))
    totals = [jnp.zeros((PIECE, LANES), f32) for _ in range(2)]
    for far in range(FAR):
        totals[far % 2] = totals[far % 2] + key_wide[far : far + 1] * piece_of(values, far)
    key_out[...] = (totals[0] + totals[1]).astype(bf16)
    gain = jnp.sum(gain_share * last[pl.ds(0, FAR), :], axis=0, keepdims=True)
    wide = jnp.broadcast_to(gain, (8, LANES))
    moved = wide
    for near in range(1, NEAR):
        moved = jnp.where(place[0] // WIDTH == near, pltpu.roll(wide, LANES - PIECE * near, 1), moved)
    gain_out[...] = moved[0:1, :PIECE].astype(bf16)


def far_merge(place, dots, values, last):
    return pl.pallas_call(
        far_merge_kernel,
        out_shape=[
            jax.ShapeDtypeStruct((PIECE, LANES), bf16),
            jax.ShapeDtypeStruct((1, PIECE), bf16),
        ],
        in_specs=[SMEM_SPEC] + [VMEM_SPEC] * 3,
        out_specs=[VMEM_SPEC] * 2,
        compiler_params=PARAMS,
        name="far_merge",
    )(place, dots, values, last)


def paired(x, axis, apart):
    return lax.ppermute(x, axis, [(i, i ^ apart) for i in range(lax.axis_size(axis))])


def exchanged(x, axes):
    return lax.all_to_all(x, axes, 0, 0)


def body(hidden_states, key_cotangent, norm_gain, key_weight):
    place = lax.axis_index(("zl", "x", "core")).astype(jnp.int32).reshape(1)
    *pieces, inv_wide = local_grads(
        place, hidden_states, key_cotangent, norm_gain.reshape(FAR, LANES)
    )
    with jax.named_scope("near_exchange"):
        arrived = {apart: paired(pieces[apart], "zl", apart) for apart in (3, 2, 1)}
    with jax.named_scope("gain_parts"):
        gain = local_gains(hidden_states, key_cotangent, key_weight, inv_wide)
        gain_parts = lax.all_gather(lax.all_gather(gain, "core"), "x")
        gain_parts = gain_parts.reshape(WIDTH, FAR, LANES)
    pieces = [pieces[0]] + [arrived[apart] for apart in range(1, NEAR)]
    messages = near_dots(place, pieces, gain_parts)
    with jax.named_scope("near_dots_sum"):
        messages = exchanged(messages, ("zl", "x", "core"))
    values = near_merge(place, messages, pieces)
    with jax.named_scope("far_exchange"):
        values = exchanged(values, ("zh", "y"))
    dots, last = far_dots(values)
    with jax.named_scope("far_dots_sum"):
        dots = total_of(exchanged(dots, ("x", "core")), 4 * NEAR)
        dots = total_of(exchanged(dots, ("y", "zl")), 1)
        dots = lax.psum(dots[0], "zh")
    merged_key, merged_gain = far_merge(place, dots, values, last)
    return (merged_key, merged_gain.reshape(PIECE))


def solution(mesh):
    split = Mesh(mesh.devices.reshape(4, FAR_Z, NEAR, 4, 2), ("y", "zh", "zl", "x", "core"))
    rows = ("y", "zh", "zl")
    columns = ("x", "core")
    return jax.shard_map(
        body,
        mesh=split,
        in_specs=(P(rows, None), P(rows, columns), P(), P(None, columns)),
        out_specs=(P(rows, columns), P(rows)),
        check_vma=False,
    )
```

```python
import jax
import jax.numpy as jnp
from jax import lax
from jax.experimental import pallas as pl
from jax.experimental.pallas import tpu as pltpu
from jax.sharding import Mesh
from jax.sharding import PartitionSpec as P

eps_norm = 1e-05
eps_merge = 1e-06

f32 = jnp.float32
bf16 = jnp.bfloat16

NEAR = 4
FAR = 32
FAR_Z = 8
WIDTH = 8
GAIN_ROWS = FAR // WIDTH
NEAR_PAIRS = [(a, b) for a in range(NEAR) for b in range(a, NEAR)]
PIECE = 32
LANES = 128
VMEM_SPEC = pl.BlockSpec(memory_space=pltpu.VMEM)
SMEM_SPEC = pl.BlockSpec(memory_space=pltpu.SMEM)
HBM_SPEC = pl.BlockSpec(memory_space=pltpu.HBM)
PARAMS = pltpu.CompilerParams(vmem_limit_bytes=16 << 20)


def in_hbm(x):
    return pltpu.with_memory_space_constraint(x, pltpu.HBM)


def factor(cross, own_sq):
    return 1.0 - cross / (2.0 * (jnp.maximum(own_sq, 0.0) + eps_merge))


def within(cross, low_sq, high_sq):
    most = jnp.sqrt(jnp.maximum(low_sq, 0.0)) * jnp.sqrt(jnp.maximum(high_sq, 0.0))
    return jnp.clip(cross, -most, most)


def grads_kernel(
    place, hidden_hbm, cot_hbm, gain_hbm, p0, p1, p2, p3, inv_wide, hidden, cot, gain, pieces, sems
):
    tokens, width = hidden.shape
    parts = 8
    height = tokens // parts
    copies = [
        pltpu.make_async_copy(
            hidden_hbm.at[pl.ds(part * height, height)],
            hidden.at[pl.ds(part * height, height)],
            sems.at[part],
        )
        for part in range(parts)
    ]
    for at, (there, here) in enumerate(((cot_hbm, cot), (gain_hbm, gain))):
        copies.append(pltpu.make_async_copy(there, here, sems.at[parts + at]))
    for copy in copies:
        copy.start()
    blocks = width // LANES
    for part in range(parts):
        rows = pl.ds(part * height, height)
        copies[part].wait()
        totals = [jnp.zeros((height, LANES), f32) for _ in range(2)]
        for block in range(blocks):
            x = hidden[rows, pl.ds(block * LANES, LANES)].astype(f32)
            totals[block % 2] = totals[block % 2] + x * x
        inv_wide[rows, :] = totals[0] + totals[1]
    mean = jnp.sum(inv_wide[...], axis=1, keepdims=True) * (1.0 / width)
    inv_wide[...] = jnp.broadcast_to(lax.rsqrt(mean + eps_norm), inv_wide.shape)
    for copy in copies[parts:]:
        copy.wait()
    for chunk in range(blocks // 4):
        inv = inv_wide[...]
        inputs = []
        for block in range(4 * chunk, 4 * chunk + 4):
            x = hidden[:, pl.ds(block * LANES, LANES)].astype(f32) * inv
            inputs.append((x * gain[pl.ds(block, 1), :]).astype(bf16))
        grad = lax.dot_general(
            jnp.concatenate(inputs, axis=1),
            cot[...],
            (((0,), (0,)), ((), ())),
            preferred_element_type=f32,
        ).astype(bf16)
        for sub in range(4):
            for near in range(NEAR):
                at = sub * LANES + near * PIECE
                pieces[near, pl.ds((4 * chunk + sub) * PIECE, PIECE), :] = grad[at : at + PIECE]
    here = place[0] // WIDTH
    for apart, out in enumerate((p0, p1, p2, p3)):
        out[...] = pieces[here ^ apart]


def local_grads(place, hidden, cot, gain):
    piece = jax.ShapeDtypeStruct((FAR * PIECE, LANES), bf16)
    return pl.pallas_call(
        grads_kernel,
        out_shape=[piece] * NEAR + [jax.ShapeDtypeStruct((hidden.shape[0], LANES), f32)],
        in_specs=[SMEM_SPEC] + [HBM_SPEC] * 3,
        out_specs=[VMEM_SPEC] * (NEAR + 1),
        scratch_shapes=[
            pltpu.VMEM(hidden.shape, bf16),
            pltpu.VMEM(cot.shape, bf16),
            pltpu.VMEM(gain.shape, f32),
            pltpu.VMEM((NEAR, FAR * PIECE, LANES), bf16),
            pltpu.SemaphoreType.DMA((10,)),
        ],
        compiler_params=PARAMS,
        name="local_grads",
    )(place, in_hbm(hidden), in_hbm(cot), in_hbm(gain))


def gains_kernel(
    hidden_hbm, cot_hbm, weight_hbm, inv_wide, rows, hidden, cot, weight, sems
):
    blocks = hidden.shape[1] // LANES
    step = 4 * LANES
    copies = [pltpu.make_async_copy(cot_hbm, cot, sems.at[0])]
    for part in range(2):
        half = pl.ds(part * (blocks // 2) * LANES, (blocks // 2) * LANES)
        copies.append(
            pltpu.make_async_copy(weight_hbm.at[half], weight.at[half], sems.at[1 + part])
        )
        copies.append(
            pltpu.make_async_copy(
                hidden_hbm.at[:, half], hidden.at[:, half], sems.at[3 + part]
            )
        )
    for copy in copies:
        copy.start()
    for copy in copies[:3]:
        copy.wait()
    for chunk in range(blocks // 4):
        if chunk == blocks // 8:
            for copy in copies[3:]:
                copy.wait()
        back = lax.dot_general(
            cot[...],
            weight[pl.ds(chunk * step, step), :],
            (((1,), (1,)), ((), ())),
            preferred_element_type=f32,
        )
        inv = inv_wide[...]
        for sub in range(4):
            block = 4 * chunk + sub
            normed = hidden[:, pl.ds(block * LANES, LANES)].astype(f32) * inv
            rows[pl.ds(block, 1), :] = jnp.sum(
                back[:, sub * LANES : (sub + 1) * LANES] * normed, axis=0, keepdims=True
            )


def local_gains(hidden, cot, weight, inv_wide):
    return pl.pallas_call(
        gains_kernel,
        out_shape=jax.ShapeDtypeStruct((FAR, LANES), f32),
        in_specs=[HBM_SPEC] * 3 + [VMEM_SPEC],
        out_specs=VMEM_SPEC,
        scratch_shapes=[
            pltpu.VMEM(hidden.shape, bf16),
            pltpu.VMEM(cot.shape, bf16),
            pltpu.VMEM(weight.shape, bf16),
            pltpu.SemaphoreType.DMA((5,)),
        ],
        compiler_params=PARAMS,
        cost_estimate=pl.CostEstimate(
            flops=2 * hidden.shape[0] * weight.size,
            bytes_accessed=2 * (hidden.size + weight.size),
            transcendentals=0,
        ),
        name="local_gains",
    )(in_hbm(hidden), in_hbm(cot), in_hbm(weight), inv_wide)


def all_sum(x):
    return jnp.sum(jnp.sum(x, axis=0, keepdims=True), axis=1, keepdims=True)


def near_dots_kernel(place, p3, p2, p1, p0, gain_parts, out, shares_of):
    refs = (p0, p1, p2, p3)
    pairs = NEAR_PAIRS
    rows = 64

    def add(step, totals):
        values = [ref[pl.ds(step * rows, rows), :].astype(f32) for ref in refs]
        return tuple(
            total + jnp.sum((values[a] * values[b]).reshape(rows // 8, 8, LANES), axis=0)
            for total, (a, b) in zip(totals, pairs)
        )

    totals = lax.fori_loop(
        0, p0.shape[0] // rows, add, tuple(jnp.zeros((8, LANES), f32) for _ in pairs)
    )
    here = place[0] // WIDTH
    lane = lax.broadcasted_iota(jnp.int32, (1, LANES), 1)
    row = jnp.zeros((1, LANES), f32)
    for total, (a, b) in zip(totals, pairs):
        dot = all_sum(total)
        row = jnp.where(lane == ((NEAR * a + b) ^ (5 * here)), dot, row)
        row = jnp.where(lane == ((NEAR * b + a) ^ (5 * here)), dot, row)
    total = gain_parts[0]
    for part in range(1, gain_parts.shape[0]):
        total = total + gain_parts[part]
    total = total.astype(bf16).astype(f32)
    for part in range(WIDTH):
        shares_of[part] = total[part * GAIN_ROWS : (part + 1) * GAIN_ROWS]
    message = jnp.concatenate(
        [row, shares_of[place[0] % WIDTH], jnp.zeros((7 - GAIN_ROWS, LANES), f32)], axis=0
    )
    out[...] = jnp.broadcast_to(message[None], out.shape)


def near_dots(place, pieces, gain_parts):
    return pl.pallas_call(
        near_dots_kernel,
        out_shape=jax.ShapeDtypeStruct((NEAR * WIDTH, 8, LANES), f32),
        in_specs=[SMEM_SPEC] + [VMEM_SPEC] * (NEAR + 1),
        out_specs=VMEM_SPEC,
        scratch_shapes=[pltpu.VMEM((WIDTH, GAIN_ROWS, LANES), f32)],
        compiler_params=PARAMS,
        cost_estimate=pl.CostEstimate(
            flops=20 * pieces[0].size, bytes_accessed=8 * pieces[0].size, transcendentals=0
        ),
        name="near_dots",
    )(place, *pieces[::-1], gain_parts)


def near_shares(dots):
    low = (factor(dots[0][1], dots[0][0]), factor(dots[0][1], dots[1][1]))
    high = (factor(dots[2][3], dots[2][2]), factor(dots[2][3], dots[3][3]))
    low_sq = (
        low[0] * low[0] * dots[0][0]
        + 2.0 * (low[0] * low[1] * dots[0][1])
        + low[1] * low[1] * dots[1][1]
    )
    high_sq = (
        high[0] * high[0] * dots[2][2]
        + 2.0 * (high[0] * high[1] * dots[2][3])
        + high[1] * high[1] * dots[3][3]
    )
    cross = low[0] * (high[0] * dots[0][2] + high[1] * dots[0][3]) + low[1] * (
        high[0] * dots[1][2] + high[1] * dots[1][3]
    )
    cross = within(cross, low_sq, high_sq)
    of_low = factor(cross, low_sq)
    of_high = factor(cross, high_sq)
    square = (
        of_low * of_low * low_sq + 2.0 * (of_low * of_high * cross) + of_high * of_high * high_sq
    )
    return (of_low * low[0], of_low * low[1], of_high * high[0], of_high * high[1]), square


def bf16_parts(x):
    parts = []
    for _ in range(3):
        part = x.astype(bf16).astype(f32)
        parts.append(part)
        x = x - part
    return parts


def sent_at(far):
    return far % FAR_Z * (FAR // FAR_Z) + far // FAR_Z


def packed(dots):
    total = dots[0:8]
    for block in range(1, 4):
        total = total + pltpu.roll(dots[8 * block : 8 * block + 8], 32 * block, 1)
    return total


def unpacked(rows):
    lane = lax.broadcasted_iota(jnp.int32, (8, LANES), 1)
    blocks = []
    for block in range(4):
        moved = rows if block == 0 else pltpu.roll(rows, LANES - 32 * block, 1)
        blocks.append(jnp.where(lane < FAR, moved, 0.0))
    return jnp.concatenate(blocks, axis=0)


def near_merge_kernel(place, p3, p2, p1, p0, messages, out, gains):
    here = place[0] // WIDTH
    row = jnp.sum(messages[:, pl.ds(0, 1), :], axis=0)
    lane = lax.broadcasted_iota(jnp.int32, (1, LANES), 1)

    def entry(a, b):
        return jnp.sum(jnp.where(lane == NEAR * a + b, row, 0.0), axis=1, keepdims=True)

    shares, square = near_shares([[entry(a, b) if a <= b else None for b in range(NEAR)] for a in range(NEAR)])
    by_apart = []
    for apart in range(NEAR):
        share = shares[apart]
        for other in range(1, NEAR):
            share = jnp.where(here == other, shares[other ^ apart], share)
        by_apart.append(share)
    for far in range(FAR):
        rows = pl.ds(far * PIECE, PIECE)
        total = by_apart[0] * p0[rows, :].astype(f32)
        for share, ref in zip(by_apart[1:], (p1, p2, p3)):
            total = total + share * ref[rows, :].astype(f32)
        out[sent_at(far), pl.ds(0, PIECE // 2)] = total.astype(bf16).reshape(PIECE // 2, 2, LANES)

    for near in range(NEAR):
        for part in range(WIDTH):
            gains[near, pl.ds(part * GAIN_ROWS, GAIN_ROWS), :] = messages[
                near * WIDTH + part, pl.ds(1, GAIN_ROWS), :
            ]
    gain = [gains[near] for near in range(NEAR)]
    gain_shares, gain_square = near_shares(
        [[all_sum(gain[a] * gain[b]) if a <= b else None for b in range(NEAR)] for a in range(NEAR)]
    )
    merged = gain_shares[0] * gain[0]
    for near in range(1, NEAR):
        merged = merged + gain_shares[near] * gain[near]
    squares = jnp.zeros((1, LANES), f32)
    for at, part in enumerate(bf16_parts(square) + bf16_parts(gain_square)):
        squares = jnp.where(lane == at, part, squares)
    which = lax.broadcasted_iota(jnp.int32, (2, LANES), 0)
    for far in range(FAR):
        last = jnp.where(which == 0, merged[far : far + 1], squares)
        out[sent_at(far), PIECE // 2] = last.astype(bf16)


def near_merge(place, messages, pieces):
    return pl.pallas_call(
        near_merge_kernel,
        out_shape=jax.ShapeDtypeStruct((FAR, PIECE // 2 + 1, 2, LANES), bf16),
        in_specs=[SMEM_SPEC] + [VMEM_SPEC] * (1 + NEAR),
        out_specs=VMEM_SPEC,
        scratch_shapes=[pltpu.VMEM((NEAR, FAR, LANES), f32)],
        compiler_params=PARAMS,
        name="near_merge",
    )(place, *pieces[::-1], messages)


def far_dots_kernel(values, out, last, wide):
    height = PIECE + 8
    for far in range(FAR):
        at = far * height
        wide[pl.ds(at, PIECE), :] = piece_of(values, far)
        wide[pl.ds(at + PIECE, 2), :] = values[sent_at(far), PIECE // 2].astype(f32)
    columns = [
        wide[pl.ds(row, FAR, stride=height), :].astype(bf16) for row in range(PIECE + 1)
    ]
    for row in range(2):
        last[pl.ds(row * FAR, FAR), :] = wide[pl.ds(PIECE + row, FAR, stride=height), :]

    def dots(matrix):
        padded = jnp.concatenate(
            [matrix, jnp.zeros((LANES - FAR, matrix.shape[1]), bf16)], axis=0
        )
        return lax.dot_general(
            matrix, padded, (((1,), (1,)), ((), ())), preferred_element_type=f32
        )

    key_dots = dots(jnp.concatenate(columns[:PIECE], axis=1))
    gain_dots = dots(columns[PIECE]) * (1.0 / (NEAR * WIDTH))
    row = lax.broadcasted_iota(jnp.int32, key_dots.shape, 0)
    lane = lax.broadcasted_iota(jnp.int32, key_dots.shape, 1)
    both = jnp.where(row < lane, key_dots, jnp.where(row > lane, gain_dots, 0.0))
    out[...] = jnp.broadcast_to(packed(both)[None], out.shape)


def piece_of(values, far):
    return values[sent_at(far), pl.ds(0, PIECE // 2)].reshape(PIECE, LANES).astype(f32)


def far_dots(values):
    return pl.pallas_call(
        far_dots_kernel,
        out_shape=[
            jax.ShapeDtypeStruct((WIDTH, 8, LANES), f32),
            jax.ShapeDtypeStruct((2 * FAR, LANES), f32),
        ],
        in_specs=[VMEM_SPEC],
        out_specs=[VMEM_SPEC] * 2,
        scratch_shapes=[pltpu.VMEM(((FAR + 1) * (PIECE + 8), LANES), f32)],
        compiler_params=PARAMS,
        name="far_dots",
    )(values)


def total_kernel(parts, out):
    total = parts[0]
    for part in range(1, parts.shape[0]):
        total = total + parts[part]
    out[...] = jnp.broadcast_to(total[None], out.shape)


def total_of(parts, copies):
    return pl.pallas_call(
        total_kernel,
        out_shape=jax.ShapeDtypeStruct((copies,) + parts.shape[1:], f32),
        in_specs=[VMEM_SPEC],
        out_specs=VMEM_SPEC,
        compiler_params=PARAMS,
        name="total_of",
    )(parts)


def far_shares(dots, squares):
    row = lax.broadcasted_iota(jnp.int32, dots.shape, 0)
    lane = lax.broadcasted_iota(jnp.int32, dots.shape, 1)
    share = jnp.ones((dots.shape[0], 1), f32)
    square_row = jnp.sum(jnp.where(row == lane, squares, 0.0), axis=0, keepdims=True)
    for level in range(5):
        same = (row >> level) == (lane >> level)
        pair = (row >> (level + 1)) == (lane >> (level + 1))
        own_part = jnp.sum(jnp.where(same, dots, 0.0), axis=0, keepdims=True)
        cross_part = jnp.sum(jnp.where(same, 0.0, jnp.where(pair, dots, 0.0)), axis=0, keepdims=True)
        own_part = 2.0 * own_part + square_row
        own_sq = jnp.sum(jnp.where(same, own_part, 0.0), axis=1, keepdims=True)
        cross = jnp.sum(jnp.where(pair, cross_part, 0.0), axis=1, keepdims=True)
        other_sq = jnp.sum(
            jnp.where(same, 0.0, jnp.where(pair, own_part, 0.0)), axis=1, keepdims=True
        )
        scale = factor(within(cross, own_sq, other_sq), own_sq)
        share = share * scale
        if level < 4:
            scale_row = jnp.sum(jnp.where(row == lane, scale, 0.0), axis=0, keepdims=True)
            dots = dots * scale * scale_row
            square_row = square_row * scale_row * scale_row
    return share


def far_merge_kernel(place, dots, values, last, key_out, gain_out):
    dots = unpacked(dots[...])
    row = lax.broadcasted_iota(jnp.int32, dots.shape, 0)
    lane = lax.broadcasted_iota(jnp.int32, dots.shape, 1)
    squares = last[pl.ds(FAR, FAR), :]
    key_square = jnp.sum(jnp.where(lane < 3, squares, 0.0), axis=1, keepdims=True)
    gain_square = jnp.sum(
        jnp.where(lane < 3, 0.0, jnp.where(lane < 6, squares, 0.0)), axis=1, keepdims=True
    )
    key_share = far_shares(jnp.where(row < lane, dots, 0.0), key_square)
    gain_share = far_shares(jnp.where(row > lane, dots, 0.0), gain_square)
    key_wide = jnp.broadcast_to(key_share, (FAR, LANES))
    totals = [jnp.zeros((PIECE, LANES), f32) for _ in range(2)]
    for far in range(FAR):
        totals[far % 2] = totals[far % 2] + key_wide[far : far + 1] * piece_of(values, far)
    key_out[...] = (totals[0] + totals[1]).astype(bf16)
    gain = jnp.sum(gain_share * last[pl.ds(0, FAR), :], axis=0, keepdims=True)
    wide = jnp.broadcast_to(gain, (8, LANES))
    moved = wide
    for near in range(1, NEAR):
        moved = jnp.where(place[0] // WIDTH == near, pltpu.roll(wide, LANES - PIECE * near, 1), moved)
    gain_out[...] = moved[0:1, :PIECE].astype(bf16)


def far_merge(place, dots, values, last):
    return pl.pallas_call(
        far_merge_kernel,
        out_shape=[
            jax.ShapeDtypeStruct((PIECE, LANES), bf16),
            jax.ShapeDtypeStruct((1, PIECE), bf16),
        ],
        in_specs=[SMEM_SPEC] + [VMEM_SPEC] * 3,
        out_specs=[VMEM_SPEC] * 2,
        compiler_params=PARAMS,
        name="far_merge",
    )(place, dots, values, last)


def paired(x, axis, apart):
    return lax.ppermute(x, axis, [(i, i ^ apart) for i in range(lax.axis_size(axis))])


def exchanged(x, axes):
    return lax.all_to_all(x, axes, 0, 0)


def body(hidden_states, key_cotangent, norm_gain, key_weight):
    place = lax.axis_index(("zl", "x", "core")).astype(jnp.int32).reshape(1)
    *pieces, inv_wide = local_grads(
        place, hidden_states, key_cotangent, norm_gain.reshape(FAR, LANES)
    )
    with jax.named_scope("near_exchange"):
        arrived = {apart: paired(pieces[apart], "zl", apart) for apart in (3, 2, 1)}
    with jax.named_scope("gain_parts"):
        gain = local_gains(hidden_states, key_cotangent, key_weight, inv_wide)
        gain_parts = lax.all_gather(lax.all_gather(gain, "core"), "x")
        gain_parts = gain_parts.reshape(WIDTH, FAR, LANES)
    pieces = [pieces[0]] + [arrived[apart] for apart in range(1, NEAR)]
    messages = near_dots(place, pieces, gain_parts)
    with jax.named_scope("near_dots_sum"):
        messages = exchanged(messages, ("zl", "x", "core"))
    values = near_merge(place, messages, pieces)
    with jax.named_scope("far_exchange"):
        values = exchanged(values, ("zh", "y"))
    dots, last = far_dots(values)
    with jax.named_scope("far_dots_sum"):
        dots = total_of(exchanged(dots, ("x", "core")), 4 * NEAR)
        dots = total_of(exchanged(dots, ("y", "zl")), 1)
        dots = lax.psum(dots[0], "zh")
    merged_key, merged_gain = far_merge(place, dots, values, last)
    return (merged_key, merged_gain.reshape(PIECE))


def solution(mesh):
    split = Mesh(mesh.devices.reshape(4, FAR_Z, NEAR, 4, 2), ("y", "zh", "zl", "x", "core"))
    rows = ("y", "zh", "zl")
    columns = ("x", "core")
    return jax.shard_map(
        body,
        mesh=split,
        in_specs=(P(rows, None), P(rows, columns), P(), P(None, columns)),
        out_specs=(P(rows, columns), P(rows)),
        check_vma=False,
    )
```

```python
import jax
import jax.numpy as jnp
from jax import lax
from jax.experimental import pallas as pl
from jax.experimental.pallas import tpu as pltpu
from jax.sharding import Mesh
from jax.sharding import PartitionSpec as P

eps_norm = 1e-05
eps_merge = 1e-06

f32 = jnp.float32
bf16 = jnp.bfloat16

NEAR = 4
FAR = 32
FAR_Z = 8
WIDTH = 8
GAIN_ROWS = FAR // WIDTH
NEAR_PAIRS = [(a, b) for a in range(NEAR) for b in range(a, NEAR)]
PIECE = 32
LANES = 128
VMEM_SPEC = pl.BlockSpec(memory_space=pltpu.VMEM)
SMEM_SPEC = pl.BlockSpec(memory_space=pltpu.SMEM)
HBM_SPEC = pl.BlockSpec(memory_space=pltpu.HBM)
PARAMS = pltpu.CompilerParams(vmem_limit_bytes=16 << 20)


def in_hbm(x):
    return pltpu.with_memory_space_constraint(x, pltpu.HBM)


def factor(cross, own_sq):
    return 1.0 - cross / (2.0 * (jnp.maximum(own_sq, 0.0) + eps_merge))


def within(cross, low_sq, high_sq):
    most = jnp.sqrt(jnp.maximum(low_sq, 0.0)) * jnp.sqrt(jnp.maximum(high_sq, 0.0))
    return jnp.clip(cross, -most, most)


def grads_kernel(
    place, hidden_hbm, cot_hbm, gain_hbm, p0, p1, p2, p3, inv_wide, hidden, cot, gain, pieces, sems
):
    tokens, width = hidden.shape
    parts = 8
    height = tokens // parts
    copies = [
        pltpu.make_async_copy(
            hidden_hbm.at[pl.ds(part * height, height)],
            hidden.at[pl.ds(part * height, height)],
            sems.at[part],
        )
        for part in range(parts)
    ]
    for at, (there, here) in enumerate(((cot_hbm, cot), (gain_hbm, gain))):
        copies.append(pltpu.make_async_copy(there, here, sems.at[parts + at]))
    for copy in copies:
        copy.start()
    blocks = width // LANES
    for part in range(parts):
        rows = pl.ds(part * height, height)
        copies[part].wait()
        totals = [jnp.zeros((height, LANES), f32) for _ in range(2)]
        for block in range(blocks):
            x = hidden[rows, pl.ds(block * LANES, LANES)].astype(f32)
            totals[block % 2] = totals[block % 2] + x * x
        inv_wide[rows, :] = totals[0] + totals[1]
    mean = jnp.sum(inv_wide[...], axis=1, keepdims=True) * (1.0 / width)
    inv_wide[...] = jnp.broadcast_to(lax.rsqrt(mean + eps_norm), inv_wide.shape)
    for copy in copies[parts:]:
        copy.wait()
    for chunk in range(blocks // 4):
        inv = inv_wide[...]
        inputs = []
        for block in range(4 * chunk, 4 * chunk + 4):
            x = hidden[:, pl.ds(block * LANES, LANES)].astype(f32) * inv
            inputs.append((x * gain[pl.ds(block, 1), :]).astype(bf16))
        grad = lax.dot_general(
            jnp.concatenate(inputs, axis=1),
            cot[...],
            (((0,), (0,)), ((), ())),
            preferred_element_type=f32,
        ).astype(bf16)
        for sub in range(4):
            for near in range(NEAR):
                at = sub * LANES + near * PIECE
                pieces[near, pl.ds((4 * chunk + sub) * PIECE, PIECE), :] = grad[at : at + PIECE]
    here = place[0] // WIDTH
    for apart, out in enumerate((p0, p1, p2, p3)):
        out[...] = pieces[here ^ apart]


def local_grads(place, hidden, cot, gain):
    piece = jax.ShapeDtypeStruct((FAR * PIECE, LANES), bf16)
    return pl.pallas_call(
        grads_kernel,
        out_shape=[piece] * NEAR + [jax.ShapeDtypeStruct((hidden.shape[0], LANES), f32)],
        in_specs=[SMEM_SPEC] + [HBM_SPEC] * 3,
        out_specs=[VMEM_SPEC] * (NEAR + 1),
        scratch_shapes=[
            pltpu.VMEM(hidden.shape, bf16),
            pltpu.VMEM(cot.shape, bf16),
            pltpu.VMEM(gain.shape, f32),
            pltpu.VMEM((NEAR, FAR * PIECE, LANES), bf16),
            pltpu.SemaphoreType.DMA((10,)),
        ],
        compiler_params=PARAMS,
        name="local_grads",
    )(place, in_hbm(hidden), in_hbm(cot), in_hbm(gain))


def gains_kernel(
    hidden_hbm, cot_hbm, weight_hbm, inv_wide, rows, hidden, cot, weight, sems
):
    blocks = hidden.shape[1] // LANES
    step = 4 * LANES
    copies = [pltpu.make_async_copy(cot_hbm, cot, sems.at[0])]
    for part in range(2):
        half = pl.ds(part * (blocks // 2) * LANES, (blocks // 2) * LANES)
        copies.append(
            pltpu.make_async_copy(weight_hbm.at[half], weight.at[half], sems.at[1 + part])
        )
        copies.append(
            pltpu.make_async_copy(
                hidden_hbm.at[:, half], hidden.at[:, half], sems.at[3 + part]
            )
        )
    for copy in copies:
        copy.start()
    for copy in copies[:3]:
        copy.wait()
    for chunk in range(blocks // 4):
        if chunk == blocks // 8:
            for copy in copies[3:]:
                copy.wait()
        back = lax.dot_general(
            cot[...],
            weight[pl.ds(chunk * step, step), :],
            (((1,), (1,)), ((), ())),
            preferred_element_type=f32,
        )
        inv = inv_wide[...]
        for sub in range(4):
            block = 4 * chunk + sub
            normed = hidden[:, pl.ds(block * LANES, LANES)].astype(f32) * inv
            rows[pl.ds(block, 1), :] = jnp.sum(
                back[:, sub * LANES : (sub + 1) * LANES] * normed, axis=0, keepdims=True
            )


def local_gains(hidden, cot, weight, inv_wide):
    return pl.pallas_call(
        gains_kernel,
        out_shape=jax.ShapeDtypeStruct((FAR, LANES), f32),
        in_specs=[HBM_SPEC] * 3 + [VMEM_SPEC],
        out_specs=VMEM_SPEC,
        scratch_shapes=[
            pltpu.VMEM(hidden.shape, bf16),
            pltpu.VMEM(cot.shape, bf16),
            pltpu.VMEM(weight.shape, bf16),
            pltpu.SemaphoreType.DMA((5,)),
        ],
        compiler_params=PARAMS,
        cost_estimate=pl.CostEstimate(
            flops=2 * hidden.shape[0] * weight.size,
            bytes_accessed=2 * (hidden.size + weight.size),
            transcendentals=0,
        ),
        name="local_gains",
    )(in_hbm(hidden), in_hbm(cot), in_hbm(weight), inv_wide)


def all_sum(x):
    return jnp.sum(jnp.sum(x, axis=0, keepdims=True), axis=1, keepdims=True)


def near_dots_kernel(place, p3, p2, p1, p0, gain_parts, out, shares_of):
    refs = (p0, p1, p2, p3)
    pairs = NEAR_PAIRS
    rows = 64

    def add(step, totals):
        values = [ref[pl.ds(step * rows, rows), :].astype(f32) for ref in refs]
        return tuple(
            total + jnp.sum((values[a] * values[b]).reshape(rows // 8, 8, LANES), axis=0)
            for total, (a, b) in zip(totals, pairs)
        )

    totals = lax.fori_loop(
        0, p0.shape[0] // rows, add, tuple(jnp.zeros((8, LANES), f32) for _ in pairs)
    )
    here = place[0] // WIDTH
    lane = lax.broadcasted_iota(jnp.int32, (1, LANES), 1)
    row = jnp.zeros((1, LANES), f32)
    for total, (a, b) in zip(totals, pairs):
        dot = all_sum(total)
        row = jnp.where(lane == ((NEAR * a + b) ^ (5 * here)), dot, row)
        row = jnp.where(lane == ((NEAR * b + a) ^ (5 * here)), dot, row)
    total = gain_parts[0]
    for part in range(1, gain_parts.shape[0]):
        total = total + gain_parts[part]
    total = total.astype(bf16).astype(f32)
    for part in range(WIDTH):
        shares_of[part] = total[part * GAIN_ROWS : (part + 1) * GAIN_ROWS]
    message = jnp.concatenate(
        [row, shares_of[place[0] % WIDTH], jnp.zeros((7 - GAIN_ROWS, LANES), f32)], axis=0
    )
    out[...] = jnp.broadcast_to(message[None], out.shape)


def near_dots(place, pieces, gain_parts):
    return pl.pallas_call(
        near_dots_kernel,
        out_shape=jax.ShapeDtypeStruct((NEAR * WIDTH, 8, LANES), f32),
        in_specs=[SMEM_SPEC] + [VMEM_SPEC] * (NEAR + 1),
        out_specs=VMEM_SPEC,
        scratch_shapes=[pltpu.VMEM((WIDTH, GAIN_ROWS, LANES), f32)],
        compiler_params=PARAMS,
        cost_estimate=pl.CostEstimate(
            flops=20 * pieces[0].size, bytes_accessed=8 * pieces[0].size, transcendentals=0
        ),
        name="near_dots",
    )(place, *pieces[::-1], gain_parts)


def near_shares(dots):
    low = (factor(dots[0][1], dots[0][0]), factor(dots[0][1], dots[1][1]))
    high = (factor(dots[2][3], dots[2][2]), factor(dots[2][3], dots[3][3]))
    low_sq = (
        low[0] * low[0] * dots[0][0]
        + 2.0 * (low[0] * low[1] * dots[0][1])
        + low[1] * low[1] * dots[1][1]
    )
    high_sq = (
        high[0] * high[0] * dots[2][2]
        + 2.0 * (high[0] * high[1] * dots[2][3])
        + high[1] * high[1] * dots[3][3]
    )
    cross = low[0] * (high[0] * dots[0][2] + high[1] * dots[0][3]) + low[1] * (
        high[0] * dots[1][2] + high[1] * dots[1][3]
    )
    cross = within(cross, low_sq, high_sq)
    of_low = factor(cross, low_sq)
    of_high = factor(cross, high_sq)
    square = (
        of_low * of_low * low_sq + 2.0 * (of_low * of_high * cross) + of_high * of_high * high_sq
    )
    return (of_low * low[0], of_low * low[1], of_high * high[0], of_high * high[1]), square


def bf16_parts(x):
    parts = []
    for _ in range(3):
        part = x.astype(bf16).astype(f32)
        parts.append(part)
        x = x - part
    return parts


def sent_at(far):
    return far % FAR_Z * (FAR // FAR_Z) + far // FAR_Z


def packed(dots):
    total = dots[0:8]
    for block in range(1, 4):
        total = total + pltpu.roll(dots[8 * block : 8 * block + 8], 32 * block, 1)
    return total


def unpacked(rows):
    lane = lax.broadcasted_iota(jnp.int32, (8, LANES), 1)
    blocks = []
    for block in range(4):
        moved = rows if block == 0 else pltpu.roll(rows, LANES - 32 * block, 1)
        blocks.append(jnp.where(lane < FAR, moved, 0.0))
    return jnp.concatenate(blocks, axis=0)


def near_merge_kernel(place, p3, p2, p1, p0, messages, out, gains):
    here = place[0] // WIDTH
    row = jnp.sum(messages[:, pl.ds(0, 1), :], axis=0)
    lane = lax.broadcasted_iota(jnp.int32, (1, LANES), 1)

    def entry(a, b):
        return jnp.sum(jnp.where(lane == NEAR * a + b, row, 0.0), axis=1, keepdims=True)

    shares, square = near_shares([[entry(a, b) if a <= b else None for b in range(NEAR)] for a in range(NEAR)])
    by_apart = []
    for apart in range(NEAR):
        share = shares[apart]
        for other in range(1, NEAR):
            share = jnp.where(here == other, shares[other ^ apart], share)
        by_apart.append(share)
    for far in range(FAR):
        rows = pl.ds(far * PIECE, PIECE)
        total = by_apart[0] * p0[rows, :].astype(f32)
        for share, ref in zip(by_apart[1:], (p1, p2, p3)):
            total = total + share * ref[rows, :].astype(f32)
        out[sent_at(far), pl.ds(0, PIECE // 2)] = total.astype(bf16).reshape(PIECE // 2, 2, LANES)

    for near in range(NEAR):
        for part in range(WIDTH):
            gains[near, pl.ds(part * GAIN_ROWS, GAIN_ROWS), :] = messages[
                near * WIDTH + part, pl.ds(1, GAIN_ROWS), :
            ]
    gain = [gains[near] for near in range(NEAR)]
    gain_shares, gain_square = near_shares(
        [[all_sum(gain[a] * gain[b]) if a <= b else None for b in range(NEAR)] for a in range(NEAR)]
    )
    merged = gain_shares[0] * gain[0]
    for near in range(1, NEAR):
        merged = merged + gain_shares[near] * gain[near]
    squares = jnp.zeros((1, LANES), f32)
    for at, part in enumerate(bf16_parts(square) + bf16_parts(gain_square)):
        squares = jnp.where(lane == at, part, squares)
    which = lax.broadcasted_iota(jnp.int32, (2, LANES), 0)
    for far in range(FAR):
        last = jnp.where(which == 0, merged[far : far + 1], squares)
        out[sent_at(far), PIECE // 2] = last.astype(bf16)


def near_merge(place, messages, pieces):
    return pl.pallas_call(
        near_merge_kernel,
        out_shape=jax.ShapeDtypeStruct((FAR, PIECE // 2 + 1, 2, LANES), bf16),
        in_specs=[SMEM_SPEC] + [VMEM_SPEC] * (1 + NEAR),
        out_specs=VMEM_SPEC,
        scratch_shapes=[pltpu.VMEM((NEAR, FAR, LANES), f32)],
        compiler_params=PARAMS,
        name="near_merge",
    )(place, *pieces[::-1], messages)


def far_dots_kernel(values, out, last, wide):
    height = PIECE + 8
    for far in range(FAR):
        at = far * height
        wide[pl.ds(at, PIECE), :] = piece_of(values, far)
        wide[pl.ds(at + PIECE, 2), :] = values[sent_at(far), PIECE // 2].astype(f32)
    columns = [
        wide[pl.ds(row, FAR, stride=height), :].astype(bf16) for row in range(PIECE + 1)
    ]
    for row in range(2):
        last[pl.ds(row * FAR, FAR), :] = wide[pl.ds(PIECE + row, FAR, stride=height), :]

    def dots(matrix):
        padded = jnp.concatenate(
            [matrix, jnp.zeros((LANES - FAR, matrix.shape[1]), bf16)], axis=0
        )
        return lax.dot_general(
            matrix, padded, (((1,), (1,)), ((), ())), preferred_element_type=f32
        )

    key_dots = dots(jnp.concatenate(columns[:PIECE], axis=1))
    gain_dots = dots(columns[PIECE]) * (1.0 / (NEAR * WIDTH))
    row = lax.broadcasted_iota(jnp.int32, key_dots.shape, 0)
    lane = lax.broadcasted_iota(jnp.int32, key_dots.shape, 1)
    both = jnp.where(row < lane, key_dots, jnp.where(row > lane, gain_dots, 0.0))
    out[...] = jnp.broadcast_to(packed(both)[None], out.shape)


def piece_of(values, far):
    return values[sent_at(far), pl.ds(0, PIECE // 2)].reshape(PIECE, LANES).astype(f32)


def far_dots(values):
    return pl.pallas_call(
        far_dots_kernel,
        out_shape=[
            jax.ShapeDtypeStruct((WIDTH, 8, LANES), f32),
            jax.ShapeDtypeStruct((2 * FAR, LANES), f32),
        ],
        in_specs=[VMEM_SPEC],
        out_specs=[VMEM_SPEC] * 2,
        scratch_shapes=[pltpu.VMEM(((FAR + 1) * (PIECE + 8), LANES), f32)],
        compiler_params=PARAMS,
        name="far_dots",
    )(values)


def total_kernel(parts, out):
    total = parts[0]
    for part in range(1, parts.shape[0]):
        total = total + parts[part]
    out[...] = jnp.broadcast_to(total[None], out.shape)


def total_of(parts, copies):
    return pl.pallas_call(
        total_kernel,
        out_shape=jax.ShapeDtypeStruct((copies,) + parts.shape[1:], f32),
        in_specs=[VMEM_SPEC],
        out_specs=VMEM_SPEC,
        compiler_params=PARAMS,
        name="total_of",
    )(parts)


def far_shares(dots, squares):
    row = lax.broadcasted_iota(jnp.int32, dots.shape, 0)
    lane = lax.broadcasted_iota(jnp.int32, dots.shape, 1)
    share = jnp.ones((dots.shape[0], 1), f32)
    square_row = jnp.sum(jnp.where(row == lane, squares, 0.0), axis=0, keepdims=True)
    for level in range(5):
        same = (row >> level) == (lane >> level)
        pair = (row >> (level + 1)) == (lane >> (level + 1))
        own_part = jnp.sum(jnp.where(same, dots, 0.0), axis=0, keepdims=True)
        cross_part = jnp.sum(jnp.where(same, 0.0, jnp.where(pair, dots, 0.0)), axis=0, keepdims=True)
        own_part = 2.0 * own_part + square_row
        own_sq = jnp.sum(jnp.where(same, own_part, 0.0), axis=1, keepdims=True)
        cross = jnp.sum(jnp.where(pair, cross_part, 0.0), axis=1, keepdims=True)
        other_sq = jnp.sum(
            jnp.where(same, 0.0, jnp.where(pair, own_part, 0.0)), axis=1, keepdims=True
        )
        scale = factor(within(cross, own_sq, other_sq), own_sq)
        share = share * scale
        if level < 4:
            scale_row = jnp.sum(jnp.where(row == lane, scale, 0.0), axis=0, keepdims=True)
            dots = dots * scale * scale_row
            square_row = square_row * scale_row * scale_row
    return share


def far_merge_kernel(place, dots, values, last, key_out, gain_out):
    dots = unpacked(dots[...])
    row = lax.broadcasted_iota(jnp.int32, dots.shape, 0)
    lane = lax.broadcasted_iota(jnp.int32, dots.shape, 1)
    squares = last[pl.ds(FAR, FAR), :]
    key_square = jnp.sum(jnp.where(lane < 3, squares, 0.0), axis=1, keepdims=True)
    gain_square = jnp.sum(
        jnp.where(lane < 3, 0.0, jnp.where(lane < 6, squares, 0.0)), axis=1, keepdims=True
    )
    key_share = far_shares(jnp.where(row < lane, dots, 0.0), key_square)
    gain_share = far_shares(jnp.where(row > lane, dots, 0.0), gain_square)
    key_wide = jnp.broadcast_to(key_share, (FAR, LANES))
    totals = [jnp.zeros((PIECE, LANES), f32) for _ in range(2)]
    for far in range(FAR):
        totals[far % 2] = totals[far % 2] + key_wide[far : far + 1] * piece_of(values, far)
    key_out[...] = (totals[0] + totals[1]).astype(bf16)
    gain = jnp.sum(gain_share * last[pl.ds(0, FAR), :], axis=0, keepdims=True)
    wide = jnp.broadcast_to(gain, (8, LANES))
    moved = wide
    for near in range(1, NEAR):
        moved = jnp.where(place[0] // WIDTH == near, pltpu.roll(wide, LANES - PIECE * near, 1), moved)
    gain_out[...] = moved[0:1, :PIECE].astype(bf16)


def far_merge(place, dots, values, last):
    return pl.pallas_call(
        far_merge_kernel,
        out_shape=[
            jax.ShapeDtypeStruct((PIECE, LANES), bf16),
            jax.ShapeDtypeStruct((1, PIECE), bf16),
        ],
        in_specs=[SMEM_SPEC] + [VMEM_SPEC] * 3,
        out_specs=[VMEM_SPEC] * 2,
        compiler_params=PARAMS,
        name="far_merge",
    )(place, dots, values, last)


def paired(x, axis, apart):
    return lax.ppermute(x, axis, [(i, i ^ apart) for i in range(lax.axis_size(axis))])


def exchanged(x, axes):
    return lax.all_to_all(x, axes, 0, 0)


def body(hidden_states, key_cotangent, norm_gain, key_weight):
    place = lax.axis_index(("zl", "x", "core")).astype(jnp.int32).reshape(1)
    *pieces, inv_wide = local_grads(
        place, hidden_states, key_cotangent, norm_gain.reshape(FAR, LANES)
    )
    with jax.named_scope("near_exchange"):
        arrived = {apart: paired(pieces[apart], "zl", apart) for apart in (3, 2, 1)}
    with jax.named_scope("gain_parts"):
        gain = local_gains(hidden_states, key_cotangent, key_weight, inv_wide)
        gain_parts = lax.all_gather(lax.all_gather(gain, "core"), "x")
        gain_parts = gain_parts.reshape(WIDTH, FAR, LANES)
    pieces = [pieces[0]] + [arrived[apart] for apart in range(1, NEAR)]
    messages = near_dots(place, pieces, gain_parts)
    with jax.named_scope("near_dots_sum"):
        messages = exchanged(messages, ("zl", "x", "core"))
    values = near_merge(place, messages, pieces)
    with jax.named_scope("far_exchange"):
        values = exchanged(values, ("zh", "y"))
    dots, last = far_dots(values)
    with jax.named_scope("far_dots_sum"):
        dots = total_of(exchanged(dots, ("y", "core")), 4 * NEAR)
        dots = total_of(exchanged(dots, ("zl", "x")), 1)
        dots = lax.psum(dots[0], "zh")
    merged_key, merged_gain = far_merge(place, dots, values, last)
    return (merged_key, merged_gain.reshape(PIECE))


def solution(mesh):
    split = Mesh(mesh.devices.reshape(4, FAR_Z, NEAR, 4, 2), ("y", "zh", "zl", "x", "core"))
    rows = ("y", "zh", "zl")
    columns = ("x", "core")
    return jax.shard_map(
        body,
        mesh=split,
        in_specs=(P(rows, None), P(rows, columns), P(), P(None, columns)),
        out_specs=(P(rows, columns), P(rows)),
        check_vma=False,
    )
```
